32 devices in a mesh: inv: 2 (over y), tracer: 4 (over z), band: 4 (over x, core).
Axes of the slice: x: 2, y: 2, z: 4, core: 2. Of those that a mesh axis runs over, the one named last changes fastest.
Arguments:
- tracer_state: float32 [32, 32, 48, 512], P(('inv', 'tracer'), 'band'), parts along dimension 0, may hold values from -6 to 6
- control: float32 [32, 32, 512], P(('inv', 'tracer'), 'band'), parts along dimension 0, may hold values from -6 to 6
- prior_tiles: float32 [8, 8, 8], replicated, may hold values from -1 to 1
- tile_index: int32 [4, 4], replicated, may hold values from 0 to 7, as said below
- region_map: int32 [32, 512], P('band'), may hold values from 0 to 21
- region_sigma: float32 [16, 22], P('tracer'), may hold values from 0.3 to 3
- zonal_courant: float32 [64, 48, 512], P(('inv', 'band'), None, 'tracer'), parts along dimension 0, may hold values from -0.3 to 0.3
- meridional_courant: float32 [64, 48, 512], P(('inv', 'band'), None, 'tracer'), parts along dimension 0, may hold values from -0.3 to 0.3
- vertical_diffusion: float32 [64, 48, 512], P(('inv', 'band'), None, 'tracer'), parts along dimension 0, may hold values from 0.02 to 0.2
Outputs:
- final_state: float32 [32, 32, 48, 512], P(('inv', 'tracer'), 'band'), parts along dimension 0
- emission: float32 [32, 32, 512], P(('inv', 'tracer'), 'band'), parts along dimension 0
The draws below stay inside these ranges and needn't reach their ends.
There are 2 independent parts, one for each index of `inv`. The reference program is written for one: setup_inputs(seed, part) draws one part's arguments, and reference() takes and returns one part's arrays. A program takes and returns all parts, laid end to end along the dimension named above; an argument that names none is the same for every part. Nothing has to cross between parts.
Inputs may be any that keep to these rules, and one draw needn't show every extreme that they name: `tile_index`: each entry names one of the 8 tiles; 0 and 7 both occur.
All inputs are finite; a program needn't handle non-finite values.
Results may differ from the reference program's by a relative error of at most 0.000071.
Values sent between devices are 32-bit elements; how exact they have to be, the bound alone decides.
A program may use at most 128 MiB of HBM per device.

```python
import math
import jax
import jax.numpy as jnp
from jax import lax

NTR = 16
LAT_DEV = 8
NLAT = 32
BANDS = 4
LEV = 48
NLON = 512
NREG = 22
NTILE = 8
STEPS = 2


def draw_tile_index(key, part):
    drawn = jax.random.randint(jax.random.fold_in(key, 11), (BANDS, BANDS), 0, NTILE)
    drawn = drawn.at[0, 0].set(NTILE - 1)
    drawn = drawn.at[BANDS - 1, 0].set(0)
    return drawn.astype(jnp.int32)


def with_ends(values, rng, low, high):
    dims = values.shape
    place = [jax.random.randint(jax.random.fold_in(rng, axis), (), 0, dims[axis]) for axis in range(len(dims))]
    values = values.at[tuple(place)].set(low)
    longest = dims.index(max(dims))
    place[longest] = (place[longest] + 1) % dims[longest]
    return values.at[tuple(place)].set(high)


def block_scale(own_key, shape, shards, least, largest):
    def one(dim, blocks):
        draws = jax.random.uniform(jax.random.fold_in(jax.random.fold_in(own_key, 6), dim), (blocks,), jnp.float32, least / len(shards), largest / len(shards))
        return jnp.repeat(jnp.exp(draws), shape[dim] // blocks).reshape((-1,) + (1,) * (len(shape) - dim - 1))

    factor_of = one(*shards[0])
    for cut in shards[1:]:
        factor_of = factor_of * one(*cut)
    return factor_of


def normal_values(rng, dims, scale, most, pieces=(), kind=jnp.bfloat16):
    values = scale * jax.random.normal(rng, dims, jnp.float32)
    if pieces:
        values = values * block_scale(rng, dims, pieces, -0.22, 0.18)
    return jnp.clip(values, -most, most).astype(kind)


def setup_inputs(seed: int = 0, part: int = 0) -> dict:
    arg_keys = jax.random.split(jax.random.key(seed), 10)
    own_keys = jax.random.split(jax.random.fold_in(arg_keys[9], part), 10)
    return {
        "tracer_state": normal_values(own_keys[0], (NTR, NLAT, LEV, NLON), 1.0, 6.0, ((0, 4), (1, 4)), jnp.float32),
        "control": normal_values(own_keys[1], (NTR, NLAT, NLON), 1.0, 6.0, ((0, 4), (1, 4)), jnp.float32),
        "prior_tiles": normal_values(arg_keys[2], (NTILE, LAT_DEV, LAT_DEV), NLAT ** -0.5, 1.0, (), jnp.float32),
        "tile_index": draw_tile_index(jax.random.fold_in(arg_keys[9], 71), part),
        "region_map": with_ends(jax.random.randint(arg_keys[4], (NLAT, NLON), 0, NREG), jax.random.fold_in(arg_keys[4], 1), 0, NREG - 1).astype(jnp.int32),
        "region_sigma": jnp.clip(jnp.exp(math.log(3.0) - 2.3025851 * jax.random.uniform(arg_keys[5], (NTR, NREG), jnp.float32) ** block_scale(arg_keys[5], (NTR, NREG), ((0, 4),), -0.2, 0.2)), 0.3, 3.0),
        "zonal_courant": jnp.clip(jax.random.uniform(own_keys[6], (NLAT, LEV, NLON), jnp.float32, -0.3, 0.3) * block_scale(own_keys[6], (NLAT, LEV, NLON), ((0, 4), (2, 4)), -0.4, 0.0), -0.3, 0.3),
        "meridional_courant": jnp.clip(jax.random.uniform(own_keys[7], (NLAT, LEV, NLON), jnp.float32, -0.3, 0.3) * block_scale(own_keys[7], (NLAT, LEV, NLON), ((0, 4), (2, 4)), -0.4, 0.0), -0.3, 0.3),
        "vertical_diffusion": jnp.clip(jnp.exp(math.log(0.2) - 2.3025851 * jax.random.uniform(own_keys[8], (NLAT, LEV, NLON), jnp.float32) ** block_scale(own_keys[8], (NLAT, LEV, NLON), ((0, 4), (2, 4)), -0.2, 0.2)), 0.02, 0.2),
    }


exact_dot = lax.Precision.HIGHEST


def vertical_mixing(tracer_now, mixing):
    levels = tracer_now.shape[2]
    upper_level = jnp.concatenate([tracer_now[:, :, 1:], jnp.zeros_like(tracer_now[:, :, :1])], axis=2)
    open_top = (lax.broadcasted_iota(jnp.int32, (levels, 1), 0) < levels - 1).astype(jnp.float32)
    flux_up = mixing * (tracer_now - upper_level) * open_top
    flux_down = jnp.concatenate([jnp.zeros_like(flux_up[:, :, :1]), flux_up[:, :, :-1]], axis=2)
    return flux_up - flux_down


def advance(tracer_now, zonal, meridional, mixing, source, north_open):
    east_side = jnp.roll(tracer_now, -1, axis=3)
    flux_east = jnp.maximum(zonal, 0.0) * tracer_now + jnp.minimum(zonal, 0.0) * east_side
    north_side = jnp.concatenate([tracer_now[:, 1:], jnp.zeros_like(tracer_now[:, :1])], axis=1)
    flux_north = (jnp.maximum(meridional, 0.0) * tracer_now + jnp.minimum(meridional, 0.0) * north_side) * north_open
    flux_south = jnp.concatenate([jnp.zeros_like(flux_north[:, :1]), flux_north[:, :-1]], axis=1)
    result = tracer_now - (flux_east - jnp.roll(flux_east, 1, axis=3)) - (flux_north - flux_south) - vertical_mixing(tracer_now, mixing)
    return result.at[:, :, 0, :].add(source)


def reference(tracer_state, control, prior_tiles, tile_index, region_map, region_sigma, zonal_courant, meridional_courant, vertical_diffusion):
    blocks = prior_tiles[tile_index]
    root = jnp.transpose(blocks, (0, 2, 1, 3)).reshape(NLAT, NLAT)
    prior_field = jnp.einsum("ab,kbn->kan", root, control, precision=exact_dot)
    emission = region_sigma[:, region_map] * prior_field
    north_open = (lax.broadcasted_iota(jnp.int32, (NLAT, 1, 1), 0) < NLAT - 1).astype(jnp.float32)
    groups = NTR // 8
    state_groups = tracer_state.reshape(8, groups, NLAT, LEV, NLON)
    source_groups = emission.reshape(8, groups, NLAT, NLON)

    def run_group(pair):
        tracer_now, source = pair
        for substep in range(STEPS):
            tracer_now = advance(tracer_now, zonal_courant, meridional_courant, vertical_diffusion, source, north_open)
        return tracer_now

    final_state = lax.map(run_group, (state_groups, source_groups)).reshape(NTR, NLAT, LEV, NLON)
    return final_state, emission
```

```python
import functools
import jax
import jax.numpy as jnp
from jax import lax
from jax.experimental import pallas as pl
from jax.experimental.pallas import tpu as pltpu
from jax.sharding import PartitionSpec as P

STEPS = 2


exact_dot = lax.Precision.HIGHEST


def padded_2(block, sides, width):
    for axis, dim in sides:
        count = lax.axis_size(axis)
        forward = [(i, i + 1) for i in range(count - 1)]
        backward = [(target, source) for source, target in forward]
        low = lax.ppermute(
            lax.slice_in_dim(block, block.shape[dim] - width, None, axis=dim), axis, forward
        )
        high = lax.ppermute(lax.slice_in_dim(block, 0, width, axis=dim), axis, backward)
        block = jnp.concatenate([low, block, high], axis=dim)
    return block


def passed_along(value, axis, by):
    count = lax.axis_size(axis)
    pairs = [(i, i + by) for i in range(count) if 0 <= i + by < count]
    return lax.ppermute(value, axis, pairs)


def vertical_mixing(tracer_now, mixing):
    levels = tracer_now.shape[2]
    upper_level = jnp.concatenate(
        [tracer_now[:, :, 1:], jnp.zeros_like(tracer_now[:, :, :1])], axis=2
    )
    open_top = (lax.broadcasted_iota(jnp.int32, (levels, 1), 0) < levels - 1).astype(jnp.float32)
    flux_up = mixing * (tracer_now - upper_level) * open_top
    flux_down = jnp.concatenate([jnp.zeros_like(flux_up[:, :, :1]), flux_up[:, :, :-1]], axis=2)
    return flux_up - flux_down


def advance(tracer_now, weather, sideways, north_open, source):
    zonal, zonal_west, meridional, meridional_south, mixing = weather
    west_side, east_side = sideways(tracer_now)
    flux_east = jnp.maximum(zonal, 0.0) * tracer_now + jnp.minimum(zonal, 0.0) * east_side
    flux_west = jnp.maximum(zonal_west, 0.0) * west_side + jnp.minimum(zonal_west, 0.0) * tracer_now
    padded = padded_2(tracer_now, (("band", 1),), 1)
    north_side = padded[:, 2:]
    south_side = padded[:, :-2]
    flux_north = (
        jnp.maximum(meridional, 0.0) * tracer_now + jnp.minimum(meridional, 0.0) * north_side
    ) * north_open
    flux_south = (
        jnp.maximum(meridional_south, 0.0) * south_side
        + jnp.minimum(meridional_south, 0.0) * tracer_now
    )
    result = (
        tracer_now
        - (flux_east - flux_west)
        - (flux_north - flux_south)
        - vertical_mixing(tracer_now, mixing)
    )
    return result.at[:, :, 0, :].add(source)


def on_device(
    tracer_state,
    control,
    prior_tiles,
    tile_index,
    region_map,
    region_sigma,
    zonal_courant,
    meridional_courant,
    vertical_diffusion,
):
    band_count = lax.axis_size("band")
    band_index = lax.axis_index("band")
    tiles_count = prior_tiles.shape[0]
    lat_rows = control.shape[1]
    choose = (
        tile_index[:, :, None] == lax.broadcasted_iota(jnp.int32, (1, 1, tiles_count), 2)
    ).astype(jnp.float32)
    own_row = lax.dynamic_slice_in_dim(choose, band_index, 1, 0)[0]
    blocks = jnp.einsum("bt,tmn->bmn", own_row, prior_tiles, precision=exact_dot)
    row_block = jnp.transpose(blocks, (1, 0, 2)).reshape(lat_rows, band_count * lat_rows)
    prior_field = jnp.einsum(
        "jm,kmn->kjn",
        row_block,
        lax.all_gather(control, "band", axis=1, tiled=True),
        precision=exact_dot,
    )
    regions = region_sigma.shape[1]
    onehot = (region_map[:, :, None] == lax.broadcasted_iota(jnp.int32, (1, 1, regions), 2)).astype(
        jnp.float32
    )
    cell_sigma = jnp.einsum("kr,jnr->kjn", region_sigma, onehot, precision=exact_dot)
    emission = cell_sigma * prior_field
    latitude = band_index * lat_rows + lax.broadcasted_iota(jnp.int32, (lat_rows, 1, 1), 0)
    north_open = (latitude < band_count * lat_rows - 1).astype(jnp.float32)
    south_row = passed_along(meridional_courant[-1:], "band", 1)
    zonal, meridional, mixing, south_edge = (
        lax.all_gather(zonal_courant, "tracer", axis=2, tiled=True),
        lax.all_gather(meridional_courant, "tracer", axis=2, tiled=True),
        lax.all_gather(vertical_diffusion, "tracer", axis=2, tiled=True),
        lax.all_gather(south_row, "tracer", axis=2, tiled=True),
    )
    weather = (
        zonal,
        jnp.roll(zonal, 1, axis=2),
        meridional,
        jnp.concatenate([south_edge, meridional[:-1]], axis=0),
        mixing,
    )

    def sideways(tracer_now):
        return (jnp.roll(tracer_now, 1, axis=3), jnp.roll(tracer_now, -1, axis=3))

    tracer_field = tracer_state
    for substep in range(STEPS):
        tracer_field = advance(tracer_field, weather, sideways, north_open, emission)
    return (tracer_field, emission)


LINE = 4


def fits_fused(mesh):
    return mesh.shape["tracer"] == LINE


def piece(c, rows):
    if isinstance(c, int) and c == 0:
        return pl.ds(0, 4)
    if isinstance(c, int) and c == rows - 1:
        return pl.ds(3 * c + 1, 2)
    return pl.ds(3 * c + 1, 3)


def mirror(z):
    return z + 1 - 2 * lax.rem(z, 2)


def transport_row(weather, emission, source, target, row, target_row, north, south, zonal):
    tracers, _, levels, lons = source.shape
    top = lax.broadcasted_iota(jnp.int32, (levels, lons), 0) == levels - 1

    def item(index):
        return jnp.concatenate([weather[j, index] for j in range(LINE)], axis=1)

    def one(k, carry):
        q, q_north, q_south = source[k, row], source[k, row + 1], source[k, row - 1]
        u, d, m, m_south = item(zonal), item(zonal + 1), item(north), item(south)
        flux_east = u * jnp.where(u > 0.0, q, pltpu.roll(q, lons - 1, 1))
        flux_north = m * jnp.where(m > 0.0, q, q_north)
        flux_south = m_south * jnp.where(m_south > 0.0, q_south, q)
        flux_up = d * (q - jnp.where(top, q, pltpu.roll(q, levels - 1, 0)))
        result = q - (flux_east - pltpu.roll(flux_east, 1, 1)) - (flux_north - flux_south)
        result = result - (flux_up - pltpu.roll(flux_up, 1, 0))
        target[k, target_row] = result
        target[k, target_row, 0:1, :] = result[0:1] + emission[k, pl.ds(row - 1, 1), :]
        return carry

    lax.fori_loop(0, tracers, one, 0)


def window_kernel(
    bands,
    tile_index,
    region_sigma,
    region_map,
    prior_tiles,
    state,
    control,
    zonal_courant,
    meridional_courant,
    vertical_diffusion,
    final,
    emission,
    first,
    second,
    weather,
    increments,
    own_sem,
    state_sem,
    piece_send,
    piece_recv,
    relay_send,
    control_sem,
    control_send,
    control_recv,
    edge_send,
    edge_recv,
):
    z, b = lax.axis_index("tracer"), lax.axis_index("band")
    tracers, rows, levels, lons = state.shape
    regions = region_sigma.shape[1]
    halo_item, closed_item = 3 * rows, 3 * rows + 1
    near, far = mirror(z), jnp.where(z < 2, 2, 1)
    beyond, beyond_next = 3 - z, mirror(3 - z)
    inner = jnp.logical_and(z > 0, z < LINE - 1)
    has_south, has_north = b > 0, b < bands - 1

    def send(src, dst, send_sem, recv_sem, **where):
        return pltpu.make_async_remote_copy(
            src_ref=src, dst_ref=dst, send_sem=send_sem, recv_sem=recv_sem,
            device_id=where, device_id_type=pl.DeviceIdType.MESH,
        )

    def own_item(c, index, array, row):
        return pltpu.make_async_copy(array.at[row], weather.at[z, index], own_sem.at[c])

    def start_own(c):
        row = (c + rows - 1) % rows
        index = 3 * c + 1
        if c == 0:
            own_item(c, 0, meridional_courant, rows - 2).start()
        if c < rows - 1:
            own_item(c, index, meridional_courant, row).start()
            index += 1
        own_item(c, index, zonal_courant, row).start()
        own_item(c, index + 1, vertical_diffusion, row).start()

    for c in range(rows):
        start_own(c)
    load_state = pltpu.make_async_copy(state, first.at[:, pl.ds(1, rows)], state_sem.at[0])
    load_state.start()
    own_rows = pl.ds(pl.multiple_of(b * rows, rows), rows)
    load_control = pltpu.make_async_copy(control, increments.at[:, own_rows], control_sem.at[0])
    load_control.start()

    barrier = pltpu.get_barrier_semaphore()
    for step in range(1, LINE):
        pl.semaphore_signal(
            barrier, inc=1, device_id={"tracer": lax.rem(z + step, LINE)}, device_id_type=pl.DeviceIdType.MESH
        )
    for step in range(1, bands):
        pl.semaphore_signal(
            barrier, inc=1, device_id={"band": lax.rem(b + step, bands)}, device_id_type=pl.DeviceIdType.MESH
        )
    pl.semaphore_wait(barrier, LINE - 1 + bands - 1)

    def piece_copy(c, owner, target, sems, slot):
        part = weather.at[owner, piece(c, rows)]
        return send(part, part, sems.at[c, slot], piece_recv.at[c, owner], tracer=target)

    for c in range(rows):
        part = weather.at[z, piece(c, rows)]
        pltpu.make_async_copy(part, part, own_sem.at[c]).wait()
        piece_copy(c, z, near, piece_send, 0).start()
        piece_copy(c, z, far, piece_send, 1).start()

    def edge_copy(slot):
        src, dst, step = (
            (state.at[:, rows - 1], first.at[:, 0], 1),
            (state.at[:, 0], first.at[:, rows + 1], -1),
            (second.at[:, rows], second.at[:, 0], 1),
            (second.at[:, 1], second.at[:, rows + 1], -1),
            (weather.at[:, 1], weather.at[:, halo_item], 1),
        )[slot]
        target = jnp.clip(b + step, 0, bands - 1)
        return send(src, dst, edge_send.at[slot], edge_recv.at[slot], band=target)

    def control_copy(step):
        return send(
            control, increments.at[:, own_rows], control_send.at[step], control_recv.at[b],
            band=lax.rem(b + step, bands),
        )

    for step in range(1, bands):
        control_copy(step).start()

    @pl.when(has_north)
    def _():
        edge_copy(0).start()

    @pl.when(has_south)
    def _():
        edge_copy(1).start()

    zero_row = jnp.zeros((levels, lons), jnp.float32)
    zero_item = jnp.zeros((levels, lons // LINE), jnp.float32)
    for j in range(LINE):
        weather[j, closed_item] = zero_item

    @pl.when(b == 0)
    def _():
        for j in range(LINE):
            weather[j, halo_item] = zero_item
        for k in range(tracers):
            first[k, 0] = zero_row
            second[k, 0] = zero_row

    @pl.when(b == bands - 1)
    def _():
        for k in range(tracers):
            first[k, rows + 1] = zero_row
            second[k, rows + 1] = zero_row

    load_control.wait()
    for step in range(1, bands):
        source_band = lax.rem(b + step, bands)
        part = increments.at[:, pl.ds(pl.multiple_of(source_band * rows, rows), rows)]
        pltpu.make_async_copy(part, part, control_recv.at[source_band]).wait()
    region = region_map[...]
    for k in range(tracers):
        field = jnp.zeros((rows, lons), jnp.float32)
        for j in range(bands):
            tile = prior_tiles[tile_index[b, j]]
            for row in range(rows):
                field = field + tile[:, row : row + 1] * increments[k, j * rows + row : j * rows + row + 1, :]
        sigma = jnp.zeros((rows, lons), jnp.float32)
        for r in range(regions):
            sigma = jnp.where(region == r, region_sigma[k, r], sigma)
        emission[k] = sigma * field

    load_state.wait()

    @pl.when(has_south)
    def _():
        pltpu.make_async_copy(first.at[:, 0], first.at[:, 0], edge_recv.at[0]).wait()

    @pl.when(has_north)
    def _():
        pltpu.make_async_copy(first.at[:, rows + 1], first.at[:, rows + 1], edge_recv.at[1]).wait()

    def arrive(c):
        for slot, owner in enumerate((beyond, beyond_next)):
            part = weather.at[owner, piece(c, rows)]
            pltpu.make_async_copy(part, part, piece_recv.at[c, owner]).wait()

            @pl.when(inner)
            def _():
                piece_copy(c, owner, near, relay_send, slot).start()

        part = weather.at[near, piece(c, rows)]
        pltpu.make_async_copy(part, part, piece_recv.at[c, near]).wait()

    last_north = jnp.where(has_north, 1, closed_item)
    one_step = functools.partial(transport_row, weather, emission, first, second)
    two_step = functools.partial(transport_row, weather, emission, second, final)

    def second_step(row, north, south, zonal):
        two_step(row + 1, row, north, south, zonal)

    arrive(0)

    @pl.when(has_north)
    def _():
        edge_copy(4).start()

    one_step(rows, rows, last_north, 0, 2)

    @pl.when(has_north)
    def _():
        edge_copy(2).start()

    arrive(1)

    @pl.when(has_south)
    def _():
        pltpu.make_async_copy(weather.at[:, halo_item], weather.at[:, halo_item], edge_recv.at[4]).wait()

    one_step(1, 1, 4, halo_item, 5)

    @pl.when(has_south)
    def _():
        edge_copy(3).start()
        pltpu.make_async_copy(second.at[:, 0], second.at[:, 0], edge_recv.at[2]).wait()

    def middle(c, carry):
        arrive(c)
        one_step(c, c, 3 * c + 1, 3 * c - 2, 3 * c + 2)
        second_step(c - 2, 3 * c - 2, jnp.where(c == 2, halo_item, 3 * c - 5), 3 * c - 1)
        return carry

    lax.fori_loop(2, rows - 1, middle, 0)

    c = rows - 1
    arrive(c)
    one_step(c, c, 0, 3 * c - 2, 3 * c + 1)
    second_step(c - 2, 3 * c - 2, 3 * c - 5, 3 * c - 1)

    @pl.when(has_north)
    def _():
        pltpu.make_async_copy(second.at[:, rows + 1], second.at[:, rows + 1], edge_recv.at[3]).wait()

    second_step(rows - 2, 0, 3 * c - 2, 3 * c + 1)
    second_step(rows - 1, last_north, 0, 2)

    for c in range(rows):
        piece_copy(c, z, near, piece_send, 0).wait_send()
        piece_copy(c, z, far, piece_send, 1).wait_send()

        @pl.when(inner)
        def _():
            piece_copy(c, beyond, near, relay_send, 0).wait_send()
            piece_copy(c, beyond_next, near, relay_send, 1).wait_send()

    for step in range(1, bands):
        control_copy(step).wait_send()

    @pl.when(has_north)
    def _():
        for slot in (0, 2, 4):
            edge_copy(slot).wait_send()

    @pl.when(has_south)
    def _():
        for slot in (1, 3):
            edge_copy(slot).wait_send()


def on_device_fused(
    tracer_state,
    control,
    prior_tiles,
    tile_index,
    region_map,
    region_sigma,
    zonal_courant,
    meridional_courant,
    vertical_diffusion,
):
    tracers, rows, levels, lons = tracer_state.shape
    bands = lax.axis_size("band")
    dma = pltpu.SemaphoreType.DMA
    smem = pl.BlockSpec(memory_space=pltpu.SMEM)
    vmem = pl.BlockSpec(memory_space=pltpu.VMEM)
    anywhere = pl.BlockSpec(memory_space=pl.ANY)
    return pl.pallas_call(
        functools.partial(window_kernel, bands),
        out_shape=(
            jax.ShapeDtypeStruct(tracer_state.shape, jnp.float32),
            jax.ShapeDtypeStruct(control.shape, jnp.float32),
        ),
        in_specs=[smem, smem, vmem, vmem] + [anywhere] * 5,
        out_specs=(vmem, vmem),
        scratch_shapes=[
            pltpu.VMEM((tracers, rows + 2, levels, lons), jnp.float32),
            pltpu.VMEM((tracers, rows + 2, levels, lons), jnp.float32),
            pltpu.VMEM((LINE, 3 * rows + 2, levels, lons // LINE), jnp.float32),
            pltpu.VMEM((tracers, bands * rows, lons), jnp.float32),
            dma((rows,)),
            dma((1,)),
            dma((rows, 2)),
            dma((rows, LINE)),
            dma((rows, 2)),
            dma((1,)),
            dma((bands,)),
            dma((bands,)),
            dma((5,)),
            dma((5,)),
        ],
        compiler_params=pltpu.CompilerParams(
            collective_id=0, has_side_effects=True, vmem_limit_bytes=40 * 1024 * 1024
        ),
    )(
        tile_index,
        region_sigma,
        region_map,
        prior_tiles,
        tracer_state,
        control,
        zonal_courant,
        meridional_courant,
        vertical_diffusion,
    )


def solution(mesh):
    in_specs = (
        P(("inv", "tracer"), "band", None, None),
        P(("inv", "tracer"), "band", None),
        P(),
        P(),
        P("band", None),
        P("tracer", None),
        P(("inv", "band"), None, "tracer"),
        P(("inv", "band"), None, "tracer"),
        P(("inv", "band"), None, "tracer"),
    )
    out_specs = (P(("inv", "tracer"), "band", None, None), P(("inv", "tracer"), "band", None))
    body = on_device_fused if fits_fused(mesh) else on_device
    return jax.shard_map(
        body, mesh=mesh, in_specs=in_specs, out_specs=out_specs, check_vma=False
    )
```

```python
import functools
import jax
import jax.numpy as jnp
from jax import lax
from jax.experimental import pallas as pl
from jax.experimental.pallas import tpu as pltpu
from jax.sharding import PartitionSpec as P

STEPS = 2


exact_dot = lax.Precision.HIGHEST


def padded_2(block, sides, width):
    for axis, dim in sides:
        count = lax.axis_size(axis)
        forward = [(i, i + 1) for i in range(count - 1)]
        backward = [(target, source) for source, target in forward]
        low = lax.ppermute(
            lax.slice_in_dim(block, block.shape[dim] - width, None, axis=dim), axis, forward
        )
        high = lax.ppermute(lax.slice_in_dim(block, 0, width, axis=dim), axis, backward)
        block = jnp.concatenate([low, block, high], axis=dim)
    return block


def passed_along(value, axis, by):
    count = lax.axis_size(axis)
    pairs = [(i, i + by) for i in range(count) if 0 <= i + by < count]
    return lax.ppermute(value, axis, pairs)


def vertical_mixing(tracer_now, mixing):
    levels = tracer_now.shape[2]
    upper_level = jnp.concatenate(
        [tracer_now[:, :, 1:], jnp.zeros_like(tracer_now[:, :, :1])], axis=2
    )
    open_top = (lax.broadcasted_iota(jnp.int32, (levels, 1), 0) < levels - 1).astype(jnp.float32)
    flux_up = mixing * (tracer_now - upper_level) * open_top
    flux_down = jnp.concatenate([jnp.zeros_like(flux_up[:, :, :1]), flux_up[:, :, :-1]], axis=2)
    return flux_up - flux_down


def advance(tracer_now, weather, sideways, north_open, source):
    zonal, zonal_west, meridional, meridional_south, mixing = weather
    west_side, east_side = sideways(tracer_now)
    flux_east = jnp.maximum(zonal, 0.0) * tracer_now + jnp.minimum(zonal, 0.0) * east_side
    flux_west = jnp.maximum(zonal_west, 0.0) * west_side + jnp.minimum(zonal_west, 0.0) * tracer_now
    padded = padded_2(tracer_now, (("band", 1),), 1)
    north_side = padded[:, 2:]
    south_side = padded[:, :-2]
    flux_north = (
        jnp.maximum(meridional, 0.0) * tracer_now + jnp.minimum(meridional, 0.0) * north_side
    ) * north_open
    flux_south = (
        jnp.maximum(meridional_south, 0.0) * south_side
        + jnp.minimum(meridional_south, 0.0) * tracer_now
    )
    result = (
        tracer_now
        - (flux_east - flux_west)
        - (flux_north - flux_south)
        - vertical_mixing(tracer_now, mixing)
    )
    return result.at[:, :, 0, :].add(source)


def on_device(
    tracer_state,
    control,
    prior_tiles,
    tile_index,
    region_map,
    region_sigma,
    zonal_courant,
    meridional_courant,
    vertical_diffusion,
):
    band_count = lax.axis_size("band")
    band_index = lax.axis_index("band")
    tiles_count = prior_tiles.shape[0]
    lat_rows = control.shape[1]
    choose = (
        tile_index[:, :, None] == lax.broadcasted_iota(jnp.int32, (1, 1, tiles_count), 2)
    ).astype(jnp.float32)
    own_row = lax.dynamic_slice_in_dim(choose, band_index, 1, 0)[0]
    blocks = jnp.einsum("bt,tmn->bmn", own_row, prior_tiles, precision=exact_dot)
    row_block = jnp.transpose(blocks, (1, 0, 2)).reshape(lat_rows, band_count * lat_rows)
    prior_field = jnp.einsum(
        "jm,kmn->kjn",
        row_block,
        lax.all_gather(control, "band", axis=1, tiled=True),
        precision=exact_dot,
    )
    regions = region_sigma.shape[1]
    onehot = (region_map[:, :, None] == lax.broadcasted_iota(jnp.int32, (1, 1, regions), 2)).astype(
        jnp.float32
    )
    cell_sigma = jnp.einsum("kr,jnr->kjn", region_sigma, onehot, precision=exact_dot)
    emission = cell_sigma * prior_field
    latitude = band_index * lat_rows + lax.broadcasted_iota(jnp.int32, (lat_rows, 1, 1), 0)
    north_open = (latitude < band_count * lat_rows - 1).astype(jnp.float32)
    south_row = passed_along(meridional_courant[-1:], "band", 1)
    zonal, meridional, mixing, south_edge = (
        lax.all_gather(zonal_courant, "tracer", axis=2, tiled=True),
        lax.all_gather(meridional_courant, "tracer", axis=2, tiled=True),
        lax.all_gather(vertical_diffusion, "tracer", axis=2, tiled=True),
        lax.all_gather(south_row, "tracer", axis=2, tiled=True),
    )
    weather = (
        zonal,
        jnp.roll(zonal, 1, axis=2),
        meridional,
        jnp.concatenate([south_edge, meridional[:-1]], axis=0),
        mixing,
    )

    def sideways(tracer_now):
        return (jnp.roll(tracer_now, 1, axis=3), jnp.roll(tracer_now, -1, axis=3))

    tracer_field = tracer_state
    for substep in range(STEPS):
        tracer_field = advance(tracer_field, weather, sideways, north_open, emission)
    return (tracer_field, emission)


LINE = 4


def fits_fused(mesh):
    return mesh.shape["tracer"] == LINE


def piece(c, rows):
    if isinstance(c, int) and c == 0:
        return pl.ds(0, 4)
    if isinstance(c, int) and c == rows - 1:
        return pl.ds(3 * c + 1, 2)
    return pl.ds(3 * c + 1, 3)


def mirror(z):
    return z + 1 - 2 * lax.rem(z, 2)


def transport_row(weather, emission, source, target, row, target_row, north, south, zonal):
    tracers, _, levels, lons = source.shape
    top = lax.broadcasted_iota(jnp.int32, (levels, lons), 0) == levels - 1

    def item(index):
        return jnp.concatenate([weather[j, index] for j in range(LINE)], axis=1)

    def one(k, carry):
        q, q_north, q_south = source[k, row], source[k, row + 1], source[k, row - 1]
        u, d, m, m_south = item(zonal), item(zonal + 1), item(north), item(south)
        flux_east = u * jnp.where(u > 0.0, q, pltpu.roll(q, lons - 1, 1))
        flux_north = m * jnp.where(m > 0.0, q, q_north)
        flux_south = m_south * jnp.where(m_south > 0.0, q_south, q)
        flux_up = d * (q - jnp.where(top, q, pltpu.roll(q, levels - 1, 0)))
        result = q - (flux_east - pltpu.roll(flux_east, 1, 1)) - (flux_north - flux_south)
        result = result - (flux_up - pltpu.roll(flux_up, 1, 0))
        target[k, target_row] = result
        target[k, target_row, 0:1, :] = result[0:1] + emission[k, pl.ds(row - 1, 1), :]
        return carry

    lax.fori_loop(0, tracers, one, 0)


def window_kernel(
    bands,
    tile_index_hbm,
    region_sigma_hbm,
    region_map_hbm,
    prior_tiles_hbm,
    state,
    control,
    zonal_courant,
    meridional_courant,
    vertical_diffusion,
    final,
    emission,
    first,
    second,
    weather,
    increments,
    tile_index,
    region_sigma,
    region_map,
    prior_tiles,
    table_sem,
    own_sem,
    state_sem,
    piece_send,
    piece_recv,
    relay_send,
    control_sem,
    control_send,
    control_recv,
    edge_send,
    edge_recv,
):
    z, b = lax.axis_index("tracer"), lax.axis_index("band")
    tracers, rows, levels, lons = state.shape
    regions = region_sigma.shape[1]
    halo_item, closed_item = 3 * rows, 3 * rows + 1
    near, far, opposite = mirror(z), jnp.where(z < 2, 2, 1), LINE - 1 - z
    inner = jnp.logical_and(z > 0, z < LINE - 1)
    has_south, has_north = b > 0, b < bands - 1

    def send(src, dst, send_sem, recv_sem, **where):
        return pltpu.make_async_remote_copy(
            src_ref=src, dst_ref=dst, send_sem=send_sem, recv_sem=recv_sem,
            device_id=where, device_id_type=pl.DeviceIdType.MESH,
        )

    def own_item(c, index, array, row):
        return pltpu.make_async_copy(array.at[row], weather.at[z, index], own_sem.at[c])

    def start_own(c):
        row = (c + rows - 1) % rows
        index = 3 * c + 1
        if c == 0:
            own_item(c, 0, meridional_courant, rows - 2).start()
        if c < rows - 1:
            own_item(c, index, meridional_courant, row).start()
            index += 1
        own_item(c, index, zonal_courant, row).start()
        own_item(c, index + 1, vertical_diffusion, row).start()

    for c in range(rows):
        start_own(c)
    load_state = pltpu.make_async_copy(state, first.at[:, pl.ds(1, rows)], state_sem.at[0])
    load_state.start()
    own_rows = pl.ds(pl.multiple_of(b * rows, rows), rows)
    load_control = pltpu.make_async_copy(control, increments.at[:, own_rows], control_sem.at[0])
    load_control.start()
    tables = (
        (tile_index_hbm, tile_index), (region_sigma_hbm, region_sigma),
        (region_map_hbm, region_map), (prior_tiles_hbm, prior_tiles),
    )
    load_tables = [pltpu.make_async_copy(src, dst, table_sem.at[i]) for i, (src, dst) in enumerate(tables)]
    for load in load_tables:
        load.start()

    barrier = pltpu.get_barrier_semaphore()
    for step in range(1, LINE):
        pl.semaphore_signal(
            barrier, inc=1, device_id={"tracer": lax.rem(z + step, LINE)}, device_id_type=pl.DeviceIdType.MESH
        )
    for step in range(1, bands):
        pl.semaphore_signal(
            barrier, inc=1, device_id={"band": lax.rem(b + step, bands)}, device_id_type=pl.DeviceIdType.MESH
        )
    pl.semaphore_wait(barrier, LINE - 1 + bands - 1)

    def piece_copy(c, owner, target, sems, slot):
        part = weather.at[owner, piece(c, rows)]
        return send(part, part, sems.at[c, slot], piece_recv.at[c, owner], tracer=target)

    for c in range(rows):
        part = weather.at[z, piece(c, rows)]
        pltpu.make_async_copy(part, part, own_sem.at[c]).wait()
        piece_copy(c, z, near, piece_send, 0).start()
        piece_copy(c, z, far, piece_send, 1).start()

        @pl.when(jnp.logical_not(inner))
        def _():
            piece_copy(c, z, opposite, relay_send, 0).start()

    def edge_copy(slot):
        src, dst, step = (
            (state.at[:, rows - 1], first.at[:, 0], 1),
            (state.at[:, 0], first.at[:, rows + 1], -1),
            (second.at[:, rows], second.at[:, 0], 1),
            (second.at[:, 1], second.at[:, rows + 1], -1),
            (weather.at[:, 1], weather.at[:, halo_item], 1),
        )[slot]
        target = jnp.clip(b + step, 0, bands - 1)
        return send(src, dst, edge_send.at[slot], edge_recv.at[slot], band=target)

    def control_copy(step):
        return send(
            control, increments.at[:, own_rows], control_send.at[step], control_recv.at[b],
            band=lax.rem(b + step, bands),
        )

    for step in range(1, bands):
        control_copy(step).start()

    @pl.when(has_north)
    def _():
        edge_copy(0).start()

    @pl.when(has_south)
    def _():
        edge_copy(1).start()

    zero_row = jnp.zeros((levels, lons), jnp.float32)
    zero_item = jnp.zeros((levels, lons // LINE), jnp.float32)
    for j in range(LINE):
        weather[j, closed_item] = zero_item

    @pl.when(b == 0)
    def _():
        for j in range(LINE):
            weather[j, halo_item] = zero_item
        for k in range(tracers):
            first[k, 0] = zero_row
            second[k, 0] = zero_row

    @pl.when(b == bands - 1)
    def _():
        for k in range(tracers):
            first[k, rows + 1] = zero_row
            second[k, rows + 1] = zero_row

    load_control.wait()
    for load in load_tables:
        load.wait()
    for step in range(1, bands):
        source_band = lax.rem(b + step, bands)
        part = increments.at[:, pl.ds(pl.multiple_of(source_band * rows, rows), rows)]
        pltpu.make_async_copy(part, part, control_recv.at[source_band]).wait()
    region = region_map[...]
    choice = tile_index[pl.ds(b, 1), :]
    tiles = []
    for j in range(bands):
        tile = jnp.zeros((rows, rows), jnp.float32)
        for t in range(prior_tiles.shape[0]):
            tile = jnp.where(choice[:, j : j + 1] == t, prior_tiles[t], tile)
        tiles.append(tile)
    for k in range(tracers):
        field = jnp.zeros((rows, lons), jnp.float32)
        for j in range(bands):
            for row in range(rows):
                field = field + tiles[j][:, row : row + 1] * increments[k, j * rows + row : j * rows + row + 1, :]
        sigma = jnp.zeros((rows, lons), jnp.float32)
        for r in range(regions):
            sigma = jnp.where(region == r, region_sigma[k : k + 1, r : r + 1], sigma)
        emission[k] = sigma * field

    load_state.wait()

    @pl.when(has_south)
    def _():
        pltpu.make_async_copy(first.at[:, 0], first.at[:, 0], edge_recv.at[0]).wait()

    @pl.when(has_north)
    def _():
        pltpu.make_async_copy(first.at[:, rows + 1], first.at[:, rows + 1], edge_recv.at[1]).wait()

    def arrive(c):
        def wait_for(owner):
            part = weather.at[owner, piece(c, rows)]
            pltpu.make_async_copy(part, part, piece_recv.at[c, owner]).wait()

        wait_for(opposite)

        @pl.when(inner)
        def _():
            piece_copy(c, opposite, near, relay_send, 0).start()

        wait_for(near)
        wait_for(mirror(opposite))

    last_north = jnp.where(has_north, 1, closed_item)
    one_step = functools.partial(transport_row, weather, emission, first, second)
    two_step = functools.partial(transport_row, weather, emission, second, final)

    def second_step(row, north, south, zonal):
        two_step(row + 1, row, north, south, zonal)

    arrive(0)

    @pl.when(has_north)
    def _():
        edge_copy(4).start()

    one_step(rows, rows, last_north, 0, 2)

    @pl.when(has_north)
    def _():
        edge_copy(2).start()

    arrive(1)

    @pl.when(has_south)
    def _():
        pltpu.make_async_copy(weather.at[:, halo_item], weather.at[:, halo_item], edge_recv.at[4]).wait()

    one_step(1, 1, 4, halo_item, 5)

    @pl.when(has_south)
    def _():
        edge_copy(3).start()
        pltpu.make_async_copy(second.at[:, 0], second.at[:, 0], edge_recv.at[2]).wait()

    def middle(c, carry):
        arrive(c)
        one_step(c, c, 3 * c + 1, 3 * c - 2, 3 * c + 2)
        second_step(c - 2, 3 * c - 2, jnp.where(c == 2, halo_item, 3 * c - 5), 3 * c - 1)
        return carry

    lax.fori_loop(2, rows - 1, middle, 0)

    c = rows - 1
    arrive(c)
    one_step(c, c, 0, 3 * c - 2, 3 * c + 1)
    second_step(c - 2, 3 * c - 2, 3 * c - 5, 3 * c - 1)

    @pl.when(has_north)
    def _():
        pltpu.make_async_copy(second.at[:, rows + 1], second.at[:, rows + 1], edge_recv.at[3]).wait()

    second_step(rows - 2, 0, 3 * c - 2, 3 * c + 1)
    second_step(rows - 1, last_north, 0, 2)

    for c in range(rows):
        piece_copy(c, z, near, piece_send, 0).wait_send()
        piece_copy(c, z, far, piece_send, 1).wait_send()
        piece_copy(c, z, opposite, relay_send, 0).wait_send()

    for step in range(1, bands):
        control_copy(step).wait_send()

    @pl.when(has_north)
    def _():
        for slot in (0, 2, 4):
            edge_copy(slot).wait_send()

    @pl.when(has_south)
    def _():
        for slot in (1, 3):
            edge_copy(slot).wait_send()


def on_device_fused(
    tracer_state,
    control,
    prior_tiles,
    tile_index,
    region_map,
    region_sigma,
    zonal_courant,
    meridional_courant,
    vertical_diffusion,
):
    tracers, rows, levels, lons = tracer_state.shape
    bands = lax.axis_size("band")
    dma = pltpu.SemaphoreType.DMA
    vmem = pl.BlockSpec(memory_space=pltpu.VMEM)
    hbm = pl.BlockSpec(memory_space=pltpu.HBM)
    operands = [
        pltpu.with_memory_space_constraint(operand, pltpu.HBM)
        for operand in (
            tile_index,
            region_sigma,
            region_map,
            prior_tiles,
            tracer_state,
            control,
            zonal_courant,
            meridional_courant,
            vertical_diffusion,
        )
    ]
    return pl.pallas_call(
        functools.partial(window_kernel, bands),
        out_shape=(
            jax.ShapeDtypeStruct(tracer_state.shape, jnp.float32),
            jax.ShapeDtypeStruct(control.shape, jnp.float32),
        ),
        in_specs=[hbm] * len(operands),
        out_specs=(vmem, vmem),
        scratch_shapes=[
            pltpu.VMEM((tracers, rows + 2, levels, lons), jnp.float32),
            pltpu.VMEM((tracers, rows + 2, levels, lons), jnp.float32),
            pltpu.VMEM((LINE, 3 * rows + 2, levels, lons // LINE), jnp.float32),
            pltpu.VMEM((tracers, bands * rows, lons), jnp.float32),
            pltpu.VMEM(tile_index.shape, jnp.int32),
            pltpu.VMEM(region_sigma.shape, jnp.float32),
            pltpu.VMEM(region_map.shape, jnp.int32),
            pltpu.VMEM(prior_tiles.shape, jnp.float32),
            dma((4,)),
            dma((rows,)),
            dma((1,)),
            dma((rows, 2)),
            dma((rows, LINE)),
            dma((rows, 1)),
            dma((1,)),
            dma((bands,)),
            dma((bands,)),
            dma((5,)),
            dma((5,)),
        ],
        compiler_params=pltpu.CompilerParams(
            collective_id=0, has_side_effects=True, vmem_limit_bytes=40 * 1024 * 1024
        ),
    )(*operands)


def solution(mesh):
    in_specs = (
        P(("inv", "tracer"), "band", None, None),
        P(("inv", "tracer"), "band", None),
        P(),
        P(),
        P("band", None),
        P("tracer", None),
        P(("inv", "band"), None, "tracer"),
        P(("inv", "band"), None, "tracer"),
        P(("inv", "band"), None, "tracer"),
    )
    out_specs = (P(("inv", "tracer"), "band", None, None), P(("inv", "tracer"), "band", None))
    body = on_device_fused if fits_fused(mesh) else on_device
    return jax.shard_map(
        body, mesh=mesh, in_specs=in_specs, out_specs=out_specs, check_vma=False
    )
```

```python
import functools
import jax
import jax.numpy as jnp
from jax import lax
from jax.experimental import pallas as pl
from jax.experimental.pallas import tpu as pltpu
from jax.sharding import PartitionSpec as P

STEPS = 2


exact_dot = lax.Precision.HIGHEST


def padded_2(block, sides, width):
    for axis, dim in sides:
        count = lax.axis_size(axis)
        forward = [(i, i + 1) for i in range(count - 1)]
        backward = [(target, source) for source, target in forward]
        low = lax.ppermute(
            lax.slice_in_dim(block, block.shape[dim] - width, None, axis=dim), axis, forward
        )
        high = lax.ppermute(lax.slice_in_dim(block, 0, width, axis=dim), axis, backward)
        block = jnp.concatenate([low, block, high], axis=dim)
    return block


def passed_along(value, axis, by):
    count = lax.axis_size(axis)
    pairs = [(i, i + by) for i in range(count) if 0 <= i + by < count]
    return lax.ppermute(value, axis, pairs)


def vertical_mixing(tracer_now, mixing):
    levels = tracer_now.shape[2]
    upper_level = jnp.concatenate(
        [tracer_now[:, :, 1:], jnp.zeros_like(tracer_now[:, :, :1])], axis=2
    )
    open_top = (lax.broadcasted_iota(jnp.int32, (levels, 1), 0) < levels - 1).astype(jnp.float32)
    flux_up = mixing * (tracer_now - upper_level) * open_top
    flux_down = jnp.concatenate([jnp.zeros_like(flux_up[:, :, :1]), flux_up[:, :, :-1]], axis=2)
    return flux_up - flux_down


def advance(tracer_now, weather, sideways, north_open, source):
    zonal, zonal_west, meridional, meridional_south, mixing = weather
    west_side, east_side = sideways(tracer_now)
    flux_east = jnp.maximum(zonal, 0.0) * tracer_now + jnp.minimum(zonal, 0.0) * east_side
    flux_west = jnp.maximum(zonal_west, 0.0) * west_side + jnp.minimum(zonal_west, 0.0) * tracer_now
    padded = padded_2(tracer_now, (("band", 1),), 1)
    north_side = padded[:, 2:]
    south_side = padded[:, :-2]
    flux_north = (
        jnp.maximum(meridional, 0.0) * tracer_now + jnp.minimum(meridional, 0.0) * north_side
    ) * north_open
    flux_south = (
        jnp.maximum(meridional_south, 0.0) * south_side
        + jnp.minimum(meridional_south, 0.0) * tracer_now
    )
    result = (
        tracer_now
        - (flux_east - flux_west)
        - (flux_north - flux_south)
        - vertical_mixing(tracer_now, mixing)
    )
    return result.at[:, :, 0, :].add(source)


def on_device(
    tracer_state,
    control,
    prior_tiles,
    tile_index,
    region_map,
    region_sigma,
    zonal_courant,
    meridional_courant,
    vertical_diffusion,
):
    band_count = lax.axis_size("band")
    band_index = lax.axis_index("band")
    tiles_count = prior_tiles.shape[0]
    lat_rows = control.shape[1]
    choose = (
        tile_index[:, :, None] == lax.broadcasted_iota(jnp.int32, (1, 1, tiles_count), 2)
    ).astype(jnp.float32)
    own_row = lax.dynamic_slice_in_dim(choose, band_index, 1, 0)[0]
    blocks = jnp.einsum("bt,tmn->bmn", own_row, prior_tiles, precision=exact_dot)
    row_block = jnp.transpose(blocks, (1, 0, 2)).reshape(lat_rows, band_count * lat_rows)
    prior_field = jnp.einsum(
        "jm,kmn->kjn",
        row_block,
        lax.all_gather(control, "band", axis=1, tiled=True),
        precision=exact_dot,
    )
    regions = region_sigma.shape[1]
    onehot = (region_map[:, :, None] == lax.broadcasted_iota(jnp.int32, (1, 1, regions), 2)).astype(
        jnp.float32
    )
    cell_sigma = jnp.einsum("kr,jnr->kjn", region_sigma, onehot, precision=exact_dot)
    emission = cell_sigma * prior_field
    latitude = band_index * lat_rows + lax.broadcasted_iota(jnp.int32, (lat_rows, 1, 1), 0)
    north_open = (latitude < band_count * lat_rows - 1).astype(jnp.float32)
    south_row = passed_along(meridional_courant[-1:], "band", 1)
    zonal, meridional, mixing, south_edge = (
        lax.all_gather(zonal_courant, "tracer", axis=2, tiled=True),
        lax.all_gather(meridional_courant, "tracer", axis=2, tiled=True),
        lax.all_gather(vertical_diffusion, "tracer", axis=2, tiled=True),
        lax.all_gather(south_row, "tracer", axis=2, tiled=True),
    )
    weather = (
        zonal,
        jnp.roll(zonal, 1, axis=2),
        meridional,
        jnp.concatenate([south_edge, meridional[:-1]], axis=0),
        mixing,
    )

    def sideways(tracer_now):
        return (jnp.roll(tracer_now, 1, axis=3), jnp.roll(tracer_now, -1, axis=3))

    tracer_field = tracer_state
    for substep in range(STEPS):
        tracer_field = advance(tracer_field, weather, sideways, north_open, emission)
    return (tracer_field, emission)


LINE = 4
STRIP = 8


def fits_fused(mesh):
    return mesh.shape["tracer"] == LINE and mesh.shape["band"] > 1


def piece(c, rows):
    if isinstance(c, int) and c == 0:
        return pl.ds(0, 4)
    if isinstance(c, int) and c == rows - 1:
        return pl.ds(3 * c + 1, 2)
    return pl.ds(3 * c + 1, 3)


def mirror(z):
    return z + 1 - 2 * lax.rem(z, 2)


def transport_row(weather, emission, source, target, row, target_row, north, south, zonal):
    tracers, _, levels, lons = source.shape
    sublane = lax.broadcasted_iota(jnp.int32, (STRIP, lons), 0)
    first_sublane, last_sublane = sublane == 0, sublane == STRIP - 1
    strips = levels // STRIP

    def one(k, carry):
        def field(at, strip):
            return source[k, at, strip * STRIP : (strip + 1) * STRIP, :]

        q = field(row, 0)
        q_raised = pltpu.roll(q, STRIP - 1, 0)
        below = jnp.zeros((STRIP, lons), jnp.float32)
        for strip in range(strips):
            levels_here = slice(strip * STRIP, (strip + 1) * STRIP)

            def item(index):
                return jnp.concatenate([weather[j, index, levels_here, :] for j in range(LINE)], axis=1)

            u = item(zonal)
            flux = u * jnp.where(u > 0.0, q, pltpu.roll(q, lons - 1, 1))
            result = q - flux + pltpu.roll(flux, 1, 1)
            m = item(north)
            result = result - m * jnp.where(m > 0.0, q, field(row + 1, strip))
            m = item(south)
            result = result + m * jnp.where(m > 0.0, field(row - 1, strip), q)
            if strip < strips - 1:
                q_next = field(row, strip + 1)
                q_next_raised = pltpu.roll(q_next, STRIP - 1, 0)
                q_up = jnp.where(last_sublane, q_next_raised, q_raised)
            else:
                q_next = q_next_raised = None
                q_up = jnp.where(last_sublane, q, q_raised)
            flux = item(zonal + 1) * (q - q_up)
            lowered = pltpu.roll(flux, 1, 0)
            result = result - flux + jnp.where(first_sublane, below, lowered)
            if strip == 0:
                result = result + jnp.where(first_sublane, emission[k, pl.ds(row - 1, 1), :], 0.0)
            target[k, target_row, levels_here, :] = result
            q, q_raised, below = q_next, q_next_raised, lowered
        return carry

    lax.fori_loop(0, tracers, one, 0)


def window_kernel(
    bands,
    tile_index_hbm,
    region_sigma_hbm,
    region_map_hbm,
    prior_tiles_hbm,
    state,
    control,
    zonal_courant,
    meridional_courant,
    vertical_diffusion,
    final,
    emission,
    first,
    second,
    weather,
    increments,
    tile_index,
    region_sigma,
    region_map,
    prior_tiles,
    table_sem,
    own_sem,
    state_sem,
    piece_send,
    piece_recv,
    relay_send,
    control_sem,
    control_send,
    control_recv,
    edge_send,
    edge_recv,
):
    z, b = lax.axis_index("tracer"), lax.axis_index("band")
    tracers, rows, levels, lons = state.shape
    regions = region_sigma.shape[1]
    halo_item, closed_item = 3 * rows, 3 * rows + 1
    near, far = mirror(z), jnp.where(z < 2, 2, 1)
    beyond, beyond_next = 3 - z, mirror(3 - z)
    inner = jnp.logical_and(z > 0, z < LINE - 1)
    has_south, has_north = b > 0, b < bands - 1

    def send(src, dst, send_sem, recv_sem, **where):
        return pltpu.make_async_remote_copy(
            src_ref=src, dst_ref=dst, send_sem=send_sem, recv_sem=recv_sem,
            device_id=where, device_id_type=pl.DeviceIdType.MESH,
        )

    barrier = pltpu.get_barrier_semaphore()
    for step in range(1, LINE):
        pl.semaphore_signal(
            barrier, inc=1, device_id={"tracer": lax.rem(z + step, LINE)}, device_id_type=pl.DeviceIdType.MESH
        )
    for step in range(1, bands):
        pl.semaphore_signal(
            barrier, inc=1, device_id={"band": lax.rem(b + step, bands)}, device_id_type=pl.DeviceIdType.MESH
        )

    def own_item(c, index, array, row):
        return pltpu.make_async_copy(array.at[row], weather.at[z, index], own_sem.at[c])

    def start_own(c):
        row = (c + rows - 1) % rows
        index = 3 * c + 1
        if c == 0:
            own_item(c, 0, meridional_courant, rows - 2).start()
        if c < rows - 1:
            own_item(c, index, meridional_courant, row).start()
            index += 1
        own_item(c, index, zonal_courant, row).start()
        own_item(c, index + 1, vertical_diffusion, row).start()

    for c in range(rows):
        start_own(c)
    load_state = pltpu.make_async_copy(state, first.at[:, pl.ds(1, rows)], state_sem.at[0])
    load_state.start()
    own_rows = pl.ds(pl.multiple_of(b * rows, rows), rows)
    load_control = pltpu.make_async_copy(control, increments.at[:, own_rows], control_sem.at[0])
    load_control.start()
    tables = (
        (tile_index_hbm, tile_index), (region_sigma_hbm, region_sigma),
        (region_map_hbm, region_map), (prior_tiles_hbm, prior_tiles),
    )
    load_tables = [pltpu.make_async_copy(src, dst, table_sem.at[i]) for i, (src, dst) in enumerate(tables)]
    for load in load_tables:
        load.start()

    pl.semaphore_wait(barrier, LINE - 1 + bands - 1)

    def piece_copy(c, owner, target, sems, slot):
        part = weather.at[owner, piece(c, rows)]
        return send(part, part, sems.at[c, slot], piece_recv.at[c, owner], tracer=target)

    for c in range(rows):
        part = weather.at[z, piece(c, rows)]
        pltpu.make_async_copy(part, part, own_sem.at[c]).wait()
        piece_copy(c, z, near, piece_send, 0).start()
        piece_copy(c, z, far, piece_send, 1).start()

    def edge_copy(slot):
        src, dst, step = (
            (state.at[:, rows - 1], first.at[:, 0], 1),
            (state.at[:, 0], first.at[:, rows + 1], -1),
            (second.at[:, rows], second.at[:, 0], 1),
            (second.at[:, 1], second.at[:, rows + 1], -1),
            (weather.at[:, 1], weather.at[:, halo_item], 1),
        )[slot]
        target = jnp.clip(b + step, 0, bands - 1)
        return send(src, dst, edge_send.at[slot], edge_recv.at[slot], band=target)

    def control_copy(step):
        return send(
            control, increments.at[:, own_rows], control_send.at[step], control_recv.at[b],
            band=lax.rem(b + step, bands),
        )

    for step in range(1, bands):
        control_copy(step).start()

    @pl.when(has_north)
    def _():
        edge_copy(0).start()

    @pl.when(has_south)
    def _():
        edge_copy(1).start()

    zero_row = jnp.zeros((levels, lons), jnp.float32)
    zero_item = jnp.zeros((levels, lons // LINE), jnp.float32)
    for j in range(LINE):
        weather[j, closed_item] = zero_item

    @pl.when(b == 0)
    def _():
        for j in range(LINE):
            weather[j, halo_item] = zero_item
        for k in range(tracers):
            first[k, 0] = zero_row
            second[k, 0] = zero_row

    @pl.when(b == bands - 1)
    def _():
        for k in range(tracers):
            first[k, rows + 1] = zero_row
            second[k, rows + 1] = zero_row

    load_control.wait()
    for load in load_tables:
        load.wait()
    for step in range(1, bands):
        source_band = lax.rem(b + step, bands)
        part = increments.at[:, pl.ds(pl.multiple_of(source_band * rows, rows), rows)]
        pltpu.make_async_copy(part, part, control_recv.at[source_band]).wait()
    region = region_map[...]
    choice = tile_index[pl.ds(b, 1), :]
    tiles = []
    for j in range(bands):
        tile = jnp.zeros((rows, rows), jnp.float32)
        for t in range(prior_tiles.shape[0]):
            tile = jnp.where(choice[:, j : j + 1] == t, prior_tiles[t], tile)
        tiles.append(tile)
    for k in range(tracers):
        field = jnp.zeros((rows, lons), jnp.float32)
        for j in range(bands):
            for row in range(rows):
                field = field + tiles[j][:, row : row + 1] * increments[k, j * rows + row : j * rows + row + 1, :]
        sigma = jnp.zeros((rows, lons), jnp.float32)
        for r in range(regions):
            sigma = jnp.where(region == r, region_sigma[k : k + 1, r : r + 1], sigma)
        emission[k] = sigma * field

    load_state.wait()

    @pl.when(has_south)
    def _():
        pltpu.make_async_copy(first.at[:, 0], first.at[:, 0], edge_recv.at[0]).wait()

    @pl.when(has_north)
    def _():
        pltpu.make_async_copy(first.at[:, rows + 1], first.at[:, rows + 1], edge_recv.at[1]).wait()

    def arrive(c):
        def wait_for(owner):
            part = weather.at[owner, piece(c, rows)]
            pltpu.make_async_copy(part, part, piece_recv.at[c, owner]).wait()

        for slot, owner in enumerate((beyond, beyond_next)):
            wait_for(owner)

            @pl.when(inner)
            def _():
                piece_copy(c, owner, near, relay_send, slot).start()

        wait_for(near)

    last_north = jnp.where(has_north, 1, closed_item)
    one_step = functools.partial(transport_row, weather, emission, first, second)
    two_step = functools.partial(transport_row, weather, emission, second, final)

    def second_step(row, north, south, zonal):
        two_step(row + 1, row, north, south, zonal)

    arrive(0)

    @pl.when(has_north)
    def _():
        edge_copy(4).start()

    one_step(rows, rows, last_north, 0, 2)

    @pl.when(has_north)
    def _():
        edge_copy(2).start()

    arrive(1)

    @pl.when(has_south)
    def _():
        pltpu.make_async_copy(weather.at[:, halo_item], weather.at[:, halo_item], edge_recv.at[4]).wait()

    one_step(1, 1, 4, halo_item, 5)

    @pl.when(has_south)
    def _():
        edge_copy(3).start()
        pltpu.make_async_copy(second.at[:, 0], second.at[:, 0], edge_recv.at[2]).wait()

    def middle(c, carry):
        arrive(c)
        one_step(c, c, 3 * c + 1, 3 * c - 2, 3 * c + 2)
        second_step(c - 2, 3 * c - 2, jnp.where(c == 2, halo_item, 3 * c - 5), 3 * c - 1)
        return carry

    lax.fori_loop(2, rows - 1, middle, 0)

    c = rows - 1
    arrive(c)
    one_step(c, c, 0, 3 * c - 2, 3 * c + 1)
    second_step(c - 2, 3 * c - 2, 3 * c - 5, 3 * c - 1)

    @pl.when(has_north)
    def _():
        pltpu.make_async_copy(second.at[:, rows + 1], second.at[:, rows + 1], edge_recv.at[3]).wait()

    second_step(rows - 2, 0, 3 * c - 2, 3 * c + 1)
    second_step(rows - 1, last_north, 0, 2)

    for c in range(rows):
        piece_copy(c, z, near, piece_send, 0).wait_send()
        piece_copy(c, z, far, piece_send, 1).wait_send()

        @pl.when(inner)
        def _():
            piece_copy(c, beyond, near, relay_send, 0).wait_send()
            piece_copy(c, beyond_next, near, relay_send, 1).wait_send()

    for step in range(1, bands):
        control_copy(step).wait_send()

    @pl.when(has_north)
    def _():
        for slot in (0, 2, 4):
            edge_copy(slot).wait_send()

    @pl.when(has_south)
    def _():
        for slot in (1, 3):
            edge_copy(slot).wait_send()


def on_device_fused(
    tracer_state,
    control,
    prior_tiles,
    tile_index,
    region_map,
    region_sigma,
    zonal_courant,
    meridional_courant,
    vertical_diffusion,
):
    tracers, rows, levels, lons = tracer_state.shape
    bands = lax.axis_size("band")
    dma = pltpu.SemaphoreType.DMA
    vmem = pl.BlockSpec(memory_space=pltpu.VMEM)
    hbm = pl.BlockSpec(memory_space=pltpu.HBM)
    operands = [
        pltpu.with_memory_space_constraint(operand, pltpu.HBM)
        for operand in (
            tile_index,
            region_sigma,
            region_map,
            prior_tiles,
            tracer_state,
            control,
            zonal_courant,
            meridional_courant,
            vertical_diffusion,
        )
    ]
    return pl.pallas_call(
        functools.partial(window_kernel, bands),
        out_shape=(
            jax.ShapeDtypeStruct(tracer_state.shape, jnp.float32),
            jax.ShapeDtypeStruct(control.shape, jnp.float32),
        ),
        in_specs=[hbm] * len(operands),
        out_specs=(vmem, vmem),
        scratch_shapes=[
            pltpu.VMEM((tracers, rows + 2, levels, lons), jnp.float32),
            pltpu.VMEM((tracers, rows + 2, levels, lons), jnp.float32),
            pltpu.VMEM((LINE, 3 * rows + 2, levels, lons // LINE), jnp.float32),
            pltpu.VMEM((tracers, bands * rows, lons), jnp.float32),
            pltpu.VMEM(tile_index.shape, jnp.int32),
            pltpu.VMEM(region_sigma.shape, jnp.float32),
            pltpu.VMEM(region_map.shape, jnp.int32),
            pltpu.VMEM(prior_tiles.shape, jnp.float32),
            dma((4,)),
            dma((rows,)),
            dma((1,)),
            dma((rows, 2)),
            dma((rows, LINE)),
            dma((rows, 2)),
            dma((1,)),
            dma((bands,)),
            dma((bands,)),
            dma((5,)),
            dma((5,)),
        ],
        compiler_params=pltpu.CompilerParams(
            collective_id=0, has_side_effects=True, vmem_limit_bytes=40 * 1024 * 1024
        ),
    )(*operands)


def solution(mesh):
    in_specs = (
        P(("inv", "tracer"), "band", None, None),
        P(("inv", "tracer"), "band", None),
        P(),
        P(),
        P("band", None),
        P("tracer", None),
        P(("inv", "band"), None, "tracer"),
        P(("inv", "band"), None, "tracer"),
        P(("inv", "band"), None, "tracer"),
    )
    out_specs = (P(("inv", "tracer"), "band", None, None), P(("inv", "tracer"), "band", None))
    body = on_device_fused if fits_fused(mesh) else on_device
    return jax.shard_map(
        body, mesh=mesh, in_specs=in_specs, out_specs=out_specs, check_vma=False
    )
```

```python
import functools
import jax
import jax.numpy as jnp
from jax import lax
from jax.experimental import pallas as pl
from jax.experimental.pallas import tpu as pltpu
from jax.sharding import PartitionSpec as P

STEPS = 2


exact_dot = lax.Precision.HIGHEST


def padded_2(block, sides, width):
    for axis, dim in sides:
        count = lax.axis_size(axis)
        forward = [(i, i + 1) for i in range(count - 1)]
        backward = [(target, source) for source, target in forward]
        low = lax.ppermute(
            lax.slice_in_dim(block, block.shape[dim] - width, None, axis=dim), axis, forward
        )
        high = lax.ppermute(lax.slice_in_dim(block, 0, width, axis=dim), axis, backward)
        block = jnp.concatenate([low, block, high], axis=dim)
    return block


def passed_along(value, axis, by):
    count = lax.axis_size(axis)
    pairs = [(i, i + by) for i in range(count) if 0 <= i + by < count]
    return lax.ppermute(value, axis, pairs)


def vertical_mixing(tracer_now, mixing):
    levels = tracer_now.shape[2]
    upper_level = jnp.concatenate(
        [tracer_now[:, :, 1:], jnp.zeros_like(tracer_now[:, :, :1])], axis=2
    )
    open_top = (lax.broadcasted_iota(jnp.int32, (levels, 1), 0) < levels - 1).astype(jnp.float32)
    flux_up = mixing * (tracer_now - upper_level) * open_top
    flux_down = jnp.concatenate([jnp.zeros_like(flux_up[:, :, :1]), flux_up[:, :, :-1]], axis=2)
    return flux_up - flux_down


def advance(tracer_now, weather, sideways, north_open, source):
    zonal, zonal_west, meridional, meridional_south, mixing = weather
    west_side, east_side = sideways(tracer_now)
    flux_east = jnp.maximum(zonal, 0.0) * tracer_now + jnp.minimum(zonal, 0.0) * east_side
    flux_west = jnp.maximum(zonal_west, 0.0) * west_side + jnp.minimum(zonal_west, 0.0) * tracer_now
    padded = padded_2(tracer_now, (("band", 1),), 1)
    north_side = padded[:, 2:]
    south_side = padded[:, :-2]
    flux_north = (
        jnp.maximum(meridional, 0.0) * tracer_now + jnp.minimum(meridional, 0.0) * north_side
    ) * north_open
    flux_south = (
        jnp.maximum(meridional_south, 0.0) * south_side
        + jnp.minimum(meridional_south, 0.0) * tracer_now
    )
    result = (
        tracer_now
        - (flux_east - flux_west)
        - (flux_north - flux_south)
        - vertical_mixing(tracer_now, mixing)
    )
    return result.at[:, :, 0, :].add(source)


def on_device(
    tracer_state,
    control,
    prior_tiles,
    tile_index,
    region_map,
    region_sigma,
    zonal_courant,
    meridional_courant,
    vertical_diffusion,
):
    band_count = lax.axis_size("band")
    band_index = lax.axis_index("band")
    tiles_count = prior_tiles.shape[0]
    lat_rows = control.shape[1]
    choose = (
        tile_index[:, :, None] == lax.broadcasted_iota(jnp.int32, (1, 1, tiles_count), 2)
    ).astype(jnp.float32)
    own_row = lax.dynamic_slice_in_dim(choose, band_index, 1, 0)[0]
    blocks = jnp.einsum("bt,tmn->bmn", own_row, prior_tiles, precision=exact_dot)
    row_block = jnp.transpose(blocks, (1, 0, 2)).reshape(lat_rows, band_count * lat_rows)
    prior_field = jnp.einsum(
        "jm,kmn->kjn",
        row_block,
        lax.all_gather(control, "band", axis=1, tiled=True),
        precision=exact_dot,
    )
    regions = region_sigma.shape[1]
    onehot = (region_map[:, :, None] == lax.broadcasted_iota(jnp.int32, (1, 1, regions), 2)).astype(
        jnp.float32
    )
    cell_sigma = jnp.einsum("kr,jnr->kjn", region_sigma, onehot, precision=exact_dot)
    emission = cell_sigma * prior_field
    latitude = band_index * lat_rows + lax.broadcasted_iota(jnp.int32, (lat_rows, 1, 1), 0)
    north_open = (latitude < band_count * lat_rows - 1).astype(jnp.float32)
    south_row = passed_along(meridional_courant[-1:], "band", 1)
    zonal, meridional, mixing, south_edge = (
        lax.all_gather(zonal_courant, "tracer", axis=2, tiled=True),
        lax.all_gather(meridional_courant, "tracer", axis=2, tiled=True),
        lax.all_gather(vertical_diffusion, "tracer", axis=2, tiled=True),
        lax.all_gather(south_row, "tracer", axis=2, tiled=True),
    )
    weather = (
        zonal,
        jnp.roll(zonal, 1, axis=2),
        meridional,
        jnp.concatenate([south_edge, meridional[:-1]], axis=0),
        mixing,
    )

    def sideways(tracer_now):
        return (jnp.roll(tracer_now, 1, axis=3), jnp.roll(tracer_now, -1, axis=3))

    tracer_field = tracer_state
    for substep in range(STEPS):
        tracer_field = advance(tracer_field, weather, sideways, north_open, emission)
    return (tracer_field, emission)


LINE = 4
STRIP = 8


def fits_fused(mesh):
    return mesh.shape["tracer"] == LINE and mesh.shape["band"] > 1


def last_parts(levels):
    return 3 if levels % (3 * STRIP) == 0 else 1


def piece(c, rows, levels):
    if isinstance(c, int) and c == 0:
        return pl.ds(0, 4), pl.ds(0, levels)
    if isinstance(c, int) and c >= rows - 1:
        depth = levels // last_parts(levels)
        return pl.ds(3 * rows - 2, 2), pl.ds((c - rows + 1) * depth, depth)
    return pl.ds(3 * c + 1, 3), pl.ds(0, levels)


def mirror(z):
    return z + 1 - 2 * lax.rem(z, 2)


def transport_row(weather, emission, source, target, row, target_row, north, south, zonal, strips=None):
    tracers, _, levels, lons = source.shape
    sublane = lax.broadcasted_iota(jnp.int32, (STRIP, lons), 0)
    first_sublane, last_sublane = sublane == 0, sublane == STRIP - 1
    count = levels // STRIP
    begin, end = strips or (0, count)

    def one(k, carry):
        def field(at, strip):
            return source[k, at, strip * STRIP : (strip + 1) * STRIP, :]

        def item(index, strip):
            levels_here = slice(strip * STRIP, (strip + 1) * STRIP)
            return jnp.concatenate([weather[j, index, levels_here, :] for j in range(LINE)], axis=1)

        q = field(row, begin)
        q_raised = pltpu.roll(q, STRIP - 1, 0)
        below = jnp.zeros((STRIP, lons), jnp.float32)
        if begin > 0:
            q_below = field(row, begin - 1)
            q_up = jnp.where(last_sublane, q_raised, pltpu.roll(q_below, STRIP - 1, 0))
            below = pltpu.roll(item(zonal + 1, begin - 1) * (q_below - q_up), 1, 0)
        for strip in range(begin, end):
            u = item(zonal, strip)
            flux = u * jnp.where(u > 0.0, q, pltpu.roll(q, lons - 1, 1))
            result = q - flux + pltpu.roll(flux, 1, 1)
            m = item(north, strip)
            result = result - m * jnp.where(m > 0.0, q, field(row + 1, strip))
            m = item(south, strip)
            result = result + m * jnp.where(m > 0.0, field(row - 1, strip), q)
            if strip < count - 1:
                q_next = field(row, strip + 1)
                q_next_raised = pltpu.roll(q_next, STRIP - 1, 0)
                q_up = jnp.where(last_sublane, q_next_raised, q_raised)
            else:
                q_next = q_next_raised = None
                q_up = jnp.where(last_sublane, q, q_raised)
            flux = item(zonal + 1, strip) * (q - q_up)
            lowered = pltpu.roll(flux, 1, 0)
            result = result - flux + jnp.where(first_sublane, below, lowered)
            if strip == 0:
                result = result + jnp.where(first_sublane, emission[k, pl.ds(row - 1, 1), :], 0.0)
            target[k, target_row, strip * STRIP : (strip + 1) * STRIP, :] = result
            q, q_raised, below = q_next, q_next_raised, lowered
        return carry

    lax.fori_loop(0, tracers, one, 0)


def window_kernel(
    bands,
    tile_index_hbm,
    region_sigma_hbm,
    region_map_hbm,
    prior_tiles_hbm,
    state,
    control,
    zonal_courant,
    meridional_courant,
    vertical_diffusion,
    final,
    emission,
    first,
    second,
    weather,
    increments,
    tile_index,
    region_sigma,
    region_map,
    prior_tiles,
    table_sem,
    own_sem,
    state_sem,
    piece_send,
    piece_recv,
    relay_send,
    control_sem,
    control_send,
    control_recv,
    edge_send,
    edge_recv,
):
    z, b = lax.axis_index("tracer"), lax.axis_index("band")
    tracers, rows, levels, lons = state.shape
    regions = region_sigma.shape[1]
    parts, strips = last_parts(levels), levels // STRIP
    pieces = rows - 1 + parts
    halo_item, closed_item = 3 * rows, 3 * rows + 1
    near, far = mirror(z), jnp.where(z < 2, 2, 1)
    beyond, beyond_next = 3 - z, mirror(3 - z)
    inner = jnp.logical_and(z > 0, z < LINE - 1)
    has_south, has_north = b > 0, b < bands - 1

    def send(src, dst, send_sem, recv_sem, **where):
        return pltpu.make_async_remote_copy(
            src_ref=src, dst_ref=dst, send_sem=send_sem, recv_sem=recv_sem,
            device_id=where, device_id_type=pl.DeviceIdType.MESH,
        )

    barrier = pltpu.get_barrier_semaphore()
    def enter(**where):
        pl.semaphore_signal(barrier, inc=1, device_id=where, device_id_type=pl.DeviceIdType.MESH)

    enter(tracer=near)

    @pl.when(inner)
    def _():
        enter(tracer=beyond)
        enter(tracer=beyond_next)

    for step in range(1, bands):
        enter(band=lax.rem(b + step, bands))

    def own_item(c, index, array, row):
        return pltpu.make_async_copy(array.at[row], weather.at[z, index], own_sem.at[c])

    def start_own(c):
        row = (c + rows - 1) % rows
        index = 3 * c + 1
        if c == 0:
            own_item(c, 0, meridional_courant, rows - 2).start()
        if c < rows - 1:
            own_item(c, index, meridional_courant, row).start()
            index += 1
        own_item(c, index, zonal_courant, row).start()
        own_item(c, index + 1, vertical_diffusion, row).start()

    for c in range(rows):
        start_own(c)
    load_state = pltpu.make_async_copy(state, first.at[:, pl.ds(1, rows)], state_sem.at[0])
    load_state.start()
    own_rows = pl.ds(pl.multiple_of(b * rows, rows), rows)
    load_control = pltpu.make_async_copy(control, increments.at[:, own_rows], control_sem.at[0])
    load_control.start()
    tables = (
        (tile_index_hbm, tile_index), (region_sigma_hbm, region_sigma),
        (region_map_hbm, region_map), (prior_tiles_hbm, prior_tiles),
    )
    load_tables = [pltpu.make_async_copy(src, dst, table_sem.at[i]) for i, (src, dst) in enumerate(tables)]
    for load in load_tables:
        load.start()

    pl.semaphore_wait(barrier, 2 + bands - 1)

    def piece_copy(c, owner, target, sems, slot):
        part = weather.at[owner, *piece(c, rows, levels)]
        return send(part, part, sems.at[c, slot], piece_recv.at[c, owner], tracer=target)

    for c in range(pieces):
        if c < rows:
            part = weather.at[z, piece(c, rows, levels)[0]]
            pltpu.make_async_copy(part, part, own_sem.at[c]).wait()
        piece_copy(c, z, near, piece_send, 0).start()
        piece_copy(c, z, far, piece_send, 1).start()

    def edge_copy(slot):
        src, dst, step = (
            (state.at[:, rows - 1], first.at[:, 0], 1),
            (state.at[:, 0], first.at[:, rows + 1], -1),
            (second.at[:, rows], second.at[:, 0], 1),
            (second.at[:, 1], second.at[:, rows + 1], -1),
            (weather.at[:, 1], weather.at[:, halo_item], 1),
        )[slot]
        target = jnp.clip(b + step, 0, bands - 1)
        return send(src, dst, edge_send.at[slot], edge_recv.at[slot], band=target)

    def control_copy(step):
        return send(
            control, increments.at[:, own_rows], control_send.at[step], control_recv.at[b],
            band=lax.rem(b + step, bands),
        )

    for step in range(1, bands):
        control_copy(step).start()

    @pl.when(has_north)
    def _():
        edge_copy(0).start()

    @pl.when(has_south)
    def _():
        edge_copy(1).start()

    zero_row = jnp.zeros((levels, lons), jnp.float32)
    zero_item = jnp.zeros((levels, lons // LINE), jnp.float32)
    for j in range(LINE):
        weather[j, closed_item] = zero_item

    @pl.when(b == 0)
    def _():
        for j in range(LINE):
            weather[j, halo_item] = zero_item
        for k in range(tracers):
            first[k, 0] = zero_row
            second[k, 0] = zero_row

    @pl.when(b == bands - 1)
    def _():
        for k in range(tracers):
            first[k, rows + 1] = zero_row
            second[k, rows + 1] = zero_row

    load_control.wait()
    for load in load_tables:
        load.wait()
    for step in range(1, bands):
        source_band = lax.rem(b + step, bands)
        part = increments.at[:, pl.ds(pl.multiple_of(source_band * rows, rows), rows)]
        pltpu.make_async_copy(part, part, control_recv.at[source_band]).wait()
    region = region_map[...]
    choice = tile_index[pl.ds(b, 1), :]
    tiles = []
    for j in range(bands):
        tile = jnp.zeros((rows, rows), jnp.float32)
        for t in range(prior_tiles.shape[0]):
            tile = jnp.where(choice[:, j : j + 1] == t, prior_tiles[t], tile)
        tiles.append(tile)
    for k in range(tracers):
        field = jnp.zeros((rows, lons), jnp.float32)
        for j in range(bands):
            for row in range(rows):
                field = field + tiles[j][:, row : row + 1] * increments[k, j * rows + row : j * rows + row + 1, :]
        sigma = jnp.zeros((rows, lons), jnp.float32)
        for r in range(regions):
            sigma = jnp.where(region == r, region_sigma[k : k + 1, r : r + 1], sigma)
        emission[k] = sigma * field

    load_state.wait()

    @pl.when(has_south)
    def _():
        pltpu.make_async_copy(first.at[:, 0], first.at[:, 0], edge_recv.at[0]).wait()

    @pl.when(has_north)
    def _():
        pltpu.make_async_copy(first.at[:, rows + 1], first.at[:, rows + 1], edge_recv.at[1]).wait()

    def arrive(c):
        def wait_for(owner):
            part = weather.at[owner, *piece(c, rows, levels)]
            pltpu.make_async_copy(part, part, piece_recv.at[c, owner]).wait()

        for slot, owner in enumerate((beyond, beyond_next)):
            wait_for(owner)

            @pl.when(inner)
            def _():
                piece_copy(c, owner, near, relay_send, slot).start()

        wait_for(near)

    last_north = jnp.where(has_north, 1, closed_item)
    one_step = functools.partial(transport_row, weather, emission, first, second)
    two_step = functools.partial(transport_row, weather, emission, second, final)

    def second_step(row, north, south, zonal, part=None):
        two_step(row + 1, row, north, south, zonal, part)

    arrive(0)

    @pl.when(has_north)
    def _():
        edge_copy(4).start()

    one_step(rows, rows, last_north, 0, 2)

    @pl.when(has_north)
    def _():
        edge_copy(2).start()

    arrive(1)

    @pl.when(has_south)
    def _():
        pltpu.make_async_copy(weather.at[:, halo_item], weather.at[:, halo_item], edge_recv.at[4]).wait()

    one_step(1, 1, 4, halo_item, 5)

    @pl.when(has_south)
    def _():
        edge_copy(3).start()
        pltpu.make_async_copy(second.at[:, 0], second.at[:, 0], edge_recv.at[2]).wait()

    def middle(c, carry):
        arrive(c)
        one_step(c, c, 3 * c + 1, 3 * c - 2, 3 * c + 2)
        second_step(c - 2, 3 * c - 2, jnp.where(c == 2, halo_item, 3 * c - 5), 3 * c - 1)
        return carry

    lax.fori_loop(2, rows - 1, middle, 0)

    @pl.when(has_north)
    def _():
        pltpu.make_async_copy(second.at[:, rows + 1], second.at[:, rows + 1], edge_recv.at[3]).wait()

    c, done = rows - 1, 0
    for part in range(parts):
        arrive(c + part)
        here = (part * strips // parts, (part + 1) * strips // parts)
        one_step(c, c, 0, 3 * c - 2, 3 * c + 1, here)
        second_step(c - 2, 3 * c - 2, 3 * c - 5, 3 * c - 1, here)
        second_step(c, last_north, 0, 2, here)
        ready = here[1] if part == parts - 1 else here[1] - 1
        second_step(c - 1, 0, 3 * c - 2, 3 * c + 1, (done, ready))
        done = ready

    for c in range(pieces):
        piece_copy(c, z, near, piece_send, 0).wait_send()
        piece_copy(c, z, far, piece_send, 1).wait_send()

        @pl.when(inner)
        def _():
            piece_copy(c, beyond, near, relay_send, 0).wait_send()
            piece_copy(c, beyond_next, near, relay_send, 1).wait_send()

    for step in range(1, bands):
        control_copy(step).wait_send()

    @pl.when(has_north)
    def _():
        for slot in (0, 2, 4):
            edge_copy(slot).wait_send()

    @pl.when(has_south)
    def _():
        for slot in (1, 3):
            edge_copy(slot).wait_send()


def on_device_fused(
    tracer_state,
    control,
    prior_tiles,
    tile_index,
    region_map,
    region_sigma,
    zonal_courant,
    meridional_courant,
    vertical_diffusion,
):
    tracers, rows, levels, lons = tracer_state.shape
    bands = lax.axis_size("band")
    pieces = rows - 1 + last_parts(levels)
    dma = pltpu.SemaphoreType.DMA
    vmem = pl.BlockSpec(memory_space=pltpu.VMEM)
    hbm = pl.BlockSpec(memory_space=pltpu.HBM)
    operands = [
        pltpu.with_memory_space_constraint(operand, pltpu.HBM)
        for operand in (
            tile_index,
            region_sigma,
            region_map,
            prior_tiles,
            tracer_state,
            control,
            zonal_courant,
            meridional_courant,
            vertical_diffusion,
        )
    ]
    return pl.pallas_call(
        functools.partial(window_kernel, bands),
        out_shape=(
            jax.ShapeDtypeStruct(tracer_state.shape, jnp.float32),
            jax.ShapeDtypeStruct(control.shape, jnp.float32),
        ),
        in_specs=[hbm] * len(operands),
        out_specs=(vmem, vmem),
        scratch_shapes=[
            pltpu.VMEM((tracers, rows + 2, levels, lons), jnp.float32),
            pltpu.VMEM((tracers, rows + 2, levels, lons), jnp.float32),
            pltpu.VMEM((LINE, 3 * rows + 2, levels, lons // LINE), jnp.float32),
            pltpu.VMEM((tracers, bands * rows, lons), jnp.float32),
            pltpu.VMEM(tile_index.shape, jnp.int32),
            pltpu.VMEM(region_sigma.shape, jnp.float32),
            pltpu.VMEM(region_map.shape, jnp.int32),
            pltpu.VMEM(prior_tiles.shape, jnp.float32),
            dma((4,)),
            dma((rows,)),
            dma((1,)),
            dma((pieces, 2)),
            dma((pieces, LINE)),
            dma((pieces, 2)),
            dma((1,)),
            dma((bands,)),
            dma((bands,)),
            dma((5,)),
            dma((5,)),
        ],
        compiler_params=pltpu.CompilerParams(
            collective_id=0, has_side_effects=True, vmem_limit_bytes=40 * 1024 * 1024
        ),
    )(*operands)


def solution(mesh):
    in_specs = (
        P(("inv", "tracer"), "band", None, None),
        P(("inv", "tracer"), "band", None),
        P(),
        P(),
        P("band", None),
        P("tracer", None),
        P(("inv", "band"), None, "tracer"),
        P(("inv", "band"), None, "tracer"),
        P(("inv", "band"), None, "tracer"),
    )
    out_specs = (P(("inv", "tracer"), "band", None, None), P(("inv", "tracer"), "band", None))
    body = on_device_fused if fits_fused(mesh) else on_device
    return jax.shard_map(
        body, mesh=mesh, in_specs=in_specs, out_specs=out_specs, check_vma=False
    )
```

```python
import functools
import jax
import jax.numpy as jnp
from jax import lax
from jax.experimental import pallas as pl
from jax.experimental.pallas import tpu as pltpu
from jax.sharding import PartitionSpec as P

STEPS = 2


exact_dot = lax.Precision.HIGHEST


def padded_2(block, sides, width):
    for axis, dim in sides:
        count = lax.axis_size(axis)
        forward = [(i, i + 1) for i in range(count - 1)]
        backward = [(target, source) for source, target in forward]
        low = lax.ppermute(
            lax.slice_in_dim(block, block.shape[dim] - width, None, axis=dim), axis, forward
        )
        high = lax.ppermute(lax.slice_in_dim(block, 0, width, axis=dim), axis, backward)
        block = jnp.concatenate([low, block, high], axis=dim)
    return block


def passed_along(value, axis, by):
    count = lax.axis_size(axis)
    pairs = [(i, i + by) for i in range(count) if 0 <= i + by < count]
    return lax.ppermute(value, axis, pairs)


def vertical_mixing(tracer_now, mixing):
    levels = tracer_now.shape[2]
    upper_level = jnp.concatenate(
        [tracer_now[:, :, 1:], jnp.zeros_like(tracer_now[:, :, :1])], axis=2
    )
    open_top = (lax.broadcasted_iota(jnp.int32, (levels, 1), 0) < levels - 1).astype(jnp.float32)
    flux_up = mixing * (tracer_now - upper_level) * open_top
    flux_down = jnp.concatenate([jnp.zeros_like(flux_up[:, :, :1]), flux_up[:, :, :-1]], axis=2)
    return flux_up - flux_down


def advance(tracer_now, weather, sideways, north_open, source):
    zonal, zonal_west, meridional, meridional_south, mixing = weather
    west_side, east_side = sideways(tracer_now)
    flux_east = jnp.maximum(zonal, 0.0) * tracer_now + jnp.minimum(zonal, 0.0) * east_side
    flux_west = jnp.maximum(zonal_west, 0.0) * west_side + jnp.minimum(zonal_west, 0.0) * tracer_now
    padded = padded_2(tracer_now, (("band", 1),), 1)
    north_side = padded[:, 2:]
    south_side = padded[:, :-2]
    flux_north = (
        jnp.maximum(meridional, 0.0) * tracer_now + jnp.minimum(meridional, 0.0) * north_side
    ) * north_open
    flux_south = (
        jnp.maximum(meridional_south, 0.0) * south_side
        + jnp.minimum(meridional_south, 0.0) * tracer_now
    )
    result = (
        tracer_now
        - (flux_east - flux_west)
        - (flux_north - flux_south)
        - vertical_mixing(tracer_now, mixing)
    )
    return result.at[:, :, 0, :].add(source)


def on_device(
    tracer_state,
    control,
    prior_tiles,
    tile_index,
    region_map,
    region_sigma,
    zonal_courant,
    meridional_courant,
    vertical_diffusion,
):
    band_count = lax.axis_size("band")
    band_index = lax.axis_index("band")
    tiles_count = prior_tiles.shape[0]
    lat_rows = control.shape[1]
    choose = (
        tile_index[:, :, None] == lax.broadcasted_iota(jnp.int32, (1, 1, tiles_count), 2)
    ).astype(jnp.float32)
    own_row = lax.dynamic_slice_in_dim(choose, band_index, 1, 0)[0]
    blocks = jnp.einsum("bt,tmn->bmn", own_row, prior_tiles, precision=exact_dot)
    row_block = jnp.transpose(blocks, (1, 0, 2)).reshape(lat_rows, band_count * lat_rows)
    prior_field = jnp.einsum(
        "jm,kmn->kjn",
        row_block,
        lax.all_gather(control, "band", axis=1, tiled=True),
        precision=exact_dot,
    )
    regions = region_sigma.shape[1]
    onehot = (region_map[:, :, None] == lax.broadcasted_iota(jnp.int32, (1, 1, regions), 2)).astype(
        jnp.float32
    )
    cell_sigma = jnp.einsum("kr,jnr->kjn", region_sigma, onehot, precision=exact_dot)
    emission = cell_sigma * prior_field
    latitude = band_index * lat_rows + lax.broadcasted_iota(jnp.int32, (lat_rows, 1, 1), 0)
    north_open = (latitude < band_count * lat_rows - 1).astype(jnp.float32)
    south_row = passed_along(meridional_courant[-1:], "band", 1)
    zonal, meridional, mixing, south_edge = (
        lax.all_gather(zonal_courant, "tracer", axis=2, tiled=True),
        lax.all_gather(meridional_courant, "tracer", axis=2, tiled=True),
        lax.all_gather(vertical_diffusion, "tracer", axis=2, tiled=True),
        lax.all_gather(south_row, "tracer", axis=2, tiled=True),
    )
    weather = (
        zonal,
        jnp.roll(zonal, 1, axis=2),
        meridional,
        jnp.concatenate([south_edge, meridional[:-1]], axis=0),
        mixing,
    )

    def sideways(tracer_now):
        return (jnp.roll(tracer_now, 1, axis=3), jnp.roll(tracer_now, -1, axis=3))

    tracer_field = tracer_state
    for substep in range(STEPS):
        tracer_field = advance(tracer_field, weather, sideways, north_open, emission)
    return (tracer_field, emission)


LINE = 4
STRIP = 8
HOLD = 4


def fits_fused(mesh):
    return mesh.shape["tracer"] == LINE and mesh.shape["band"] > 1


def last_parts(levels):
    return 3 if levels % (3 * STRIP) == 0 else 1


def piece(c, rows, levels):
    if isinstance(c, int) and c == 0:
        return pl.ds(0, 4), pl.ds(0, levels)
    if isinstance(c, int) and c >= rows - 1:
        depth = levels // last_parts(levels)
        return pl.ds(3 * rows - 2, 2), pl.ds((c - rows + 1) * depth, depth)
    return pl.ds(3 * c + 1, 3), pl.ds(0, levels)


def mirror(z):
    return z + 1 - 2 * lax.rem(z, 2)


def transport_row(weather, emission, source, target, row, target_row, north, south, zonal, strips=None):
    tracers, _, levels, lons = source.shape
    sublane = lax.broadcasted_iota(jnp.int32, (STRIP, lons), 0)
    first_sublane, last_sublane = sublane == 0, sublane == STRIP - 1
    count = levels // STRIP
    begin, end = strips or (0, count)

    held_back = []

    def store():
        k, strip, result = held_back.pop(0)
        target[k, target_row, strip * STRIP : (strip + 1) * STRIP, :] = result

    def one(k):
        def field(at, strip):
            return source[k, at, strip * STRIP : (strip + 1) * STRIP, :]

        def item(index, strip):
            levels_here = slice(strip * STRIP, (strip + 1) * STRIP)
            return jnp.concatenate([weather[j, index, levels_here, :] for j in range(LINE)], axis=1)

        q = field(row, begin)
        q_raised = pltpu.roll(q, STRIP - 1, 0)
        below = jnp.zeros((STRIP, lons), jnp.float32)
        if begin > 0:
            q_below = field(row, begin - 1)
            q_up = jnp.where(last_sublane, q_raised, pltpu.roll(q_below, STRIP - 1, 0))
            below = pltpu.roll(item(zonal + 1, begin - 1) * (q_below - q_up), 1, 0)
        for strip in range(begin, end):
            u = item(zonal, strip)
            flux = u * jnp.where(u > 0.0, q, pltpu.roll(q, lons - 1, 1))
            result = q - flux + pltpu.roll(flux, 1, 1)
            m = item(north, strip)
            result = result - m * jnp.where(m > 0.0, q, field(row + 1, strip))
            m = item(south, strip)
            result = result + m * jnp.where(m > 0.0, field(row - 1, strip), q)
            if strip < count - 1:
                q_next = field(row, strip + 1)
                q_next_raised = pltpu.roll(q_next, STRIP - 1, 0)
                q_up = jnp.where(last_sublane, q_next_raised, q_raised)
            else:
                q_next = q_next_raised = None
                q_up = jnp.where(last_sublane, q, q_raised)
            flux = item(zonal + 1, strip) * (q - q_up)
            lowered = pltpu.roll(flux, 1, 0)
            result = result - flux + jnp.where(first_sublane, below, lowered)
            if strip == 0:
                result = result + jnp.where(first_sublane, emission[k, pl.ds(row - 1, 1), :], 0.0)
            held_back.append((k, strip, result))
            if len(held_back) > HOLD:
                store()
            q, q_raised, below = q_next, q_next_raised, lowered

    for k in range(tracers):
        one(k)
    while held_back:
        store()


def window_kernel(
    bands,
    tile_index_hbm,
    region_sigma_hbm,
    region_map_hbm,
    prior_tiles_hbm,
    state,
    control,
    zonal_courant,
    meridional_courant,
    vertical_diffusion,
    final,
    emission,
    first,
    second,
    weather,
    increments,
    tile_index,
    region_sigma,
    region_map,
    prior_tiles,
    table_sem,
    own_sem,
    state_sem,
    piece_send,
    piece_recv,
    relay_send,
    control_sem,
    control_send,
    control_recv,
    edge_send,
    edge_recv,
):
    z, b = lax.axis_index("tracer"), lax.axis_index("band")
    tracers, rows, levels, lons = state.shape
    regions = region_sigma.shape[1]
    parts, strips = last_parts(levels), levels // STRIP
    pieces = rows - 1 + parts
    halo_item, closed_item = 3 * rows, 3 * rows + 1
    near, far = mirror(z), jnp.where(z < 2, 2, 1)
    beyond, beyond_next = 3 - z, mirror(3 - z)
    inner = jnp.logical_and(z > 0, z < LINE - 1)
    has_south, has_north = b > 0, b < bands - 1

    def send(src, dst, send_sem, recv_sem, **where):
        return pltpu.make_async_remote_copy(
            src_ref=src, dst_ref=dst, send_sem=send_sem, recv_sem=recv_sem,
            device_id=where, device_id_type=pl.DeviceIdType.MESH,
        )

    barrier = pltpu.get_barrier_semaphore()
    def enter(**where):
        pl.semaphore_signal(barrier, inc=1, device_id=where, device_id_type=pl.DeviceIdType.MESH)

    enter(tracer=near)

    @pl.when(inner)
    def _():
        enter(tracer=beyond)
        enter(tracer=beyond_next)

    for step in range(1, bands):
        enter(band=lax.rem(b + step, bands))

    def own_item(c, index, array, row):
        return pltpu.make_async_copy(array.at[row], weather.at[z, index], own_sem.at[c])

    def start_own(c):
        row = (c + rows - 1) % rows
        index = 3 * c + 1
        if c == 0:
            own_item(c, 0, meridional_courant, rows - 2).start()
        if c < rows - 1:
            own_item(c, index, meridional_courant, row).start()
            index += 1
        own_item(c, index, zonal_courant, row).start()
        own_item(c, index + 1, vertical_diffusion, row).start()

    for c in range(rows):
        start_own(c)
    load_state = pltpu.make_async_copy(state, first.at[:, pl.ds(1, rows)], state_sem.at[0])
    load_state.start()
    own_rows = pl.ds(pl.multiple_of(b * rows, rows), rows)
    load_control = pltpu.make_async_copy(control, increments.at[:, own_rows], control_sem.at[0])
    load_control.start()
    tables = (
        (tile_index_hbm, tile_index), (region_sigma_hbm, region_sigma),
        (region_map_hbm, region_map), (prior_tiles_hbm, prior_tiles),
    )
    load_tables = [pltpu.make_async_copy(src, dst, table_sem.at[i]) for i, (src, dst) in enumerate(tables)]
    for load in load_tables:
        load.start()

    pl.semaphore_wait(barrier, 2 + bands - 1)

    def piece_copy(c, owner, target, sems, slot):
        part = weather.at[owner, *piece(c, rows, levels)]
        return send(part, part, sems.at[c, slot], piece_recv.at[c, owner], tracer=target)

    for c in range(pieces):
        if c < rows:
            part = weather.at[z, piece(c, rows, levels)[0]]
            pltpu.make_async_copy(part, part, own_sem.at[c]).wait()
        piece_copy(c, z, near, piece_send, 0).start()
        piece_copy(c, z, far, piece_send, 1).start()

    def edge_copy(slot):
        src, dst, step = (
            (state.at[:, rows - 1], first.at[:, 0], 1),
            (state.at[:, 0], first.at[:, rows + 1], -1),
            (second.at[:, rows], second.at[:, 0], 1),
            (second.at[:, 1], second.at[:, rows + 1], -1),
            (weather.at[:, 1], weather.at[:, halo_item], 1),
        )[slot]
        target = jnp.clip(b + step, 0, bands - 1)
        return send(src, dst, edge_send.at[slot], edge_recv.at[slot], band=target)

    def control_copy(step):
        return send(
            control, increments.at[:, own_rows], control_send.at[step], control_recv.at[b],
            band=lax.rem(b + step, bands),
        )

    for step in range(1, bands):
        control_copy(step).start()

    @pl.when(has_north)
    def _():
        edge_copy(0).start()

    @pl.when(has_south)
    def _():
        edge_copy(1).start()

    zero_row = jnp.zeros((levels, lons), jnp.float32)
    zero_item = jnp.zeros((levels, lons // LINE), jnp.float32)
    for j in range(LINE):
        weather[j, closed_item] = zero_item

    @pl.when(b == 0)
    def _():
        for j in range(LINE):
            weather[j, halo_item] = zero_item
        for k in range(tracers):
            first[k, 0] = zero_row
            second[k, 0] = zero_row

    @pl.when(b == bands - 1)
    def _():
        for k in range(tracers):
            first[k, rows + 1] = zero_row
            second[k, rows + 1] = zero_row

    load_control.wait()
    for load in load_tables:
        load.wait()
    for step in range(1, bands):
        source_band = lax.rem(b + step, bands)
        part = increments.at[:, pl.ds(pl.multiple_of(source_band * rows, rows), rows)]
        pltpu.make_async_copy(part, part, control_recv.at[source_band]).wait()
    region = region_map[...]
    choice = tile_index[pl.ds(b, 1), :]
    tiles = []
    for j in range(bands):
        tile = jnp.zeros((rows, rows), jnp.float32)
        for t in range(prior_tiles.shape[0]):
            tile = jnp.where(choice[:, j : j + 1] == t, prior_tiles[t], tile)
        tiles.append(tile)
    for k in range(tracers):
        field = jnp.zeros((rows, lons), jnp.float32)
        for j in range(bands):
            for row in range(rows):
                field = field + tiles[j][:, row : row + 1] * increments[k, j * rows + row : j * rows + row + 1, :]
        sigma = jnp.zeros((rows, lons), jnp.float32)
        for r in range(regions):
            sigma = jnp.where(region == r, region_sigma[k : k + 1, r : r + 1], sigma)
        emission[k] = sigma * field

    load_state.wait()

    @pl.when(has_south)
    def _():
        pltpu.make_async_copy(first.at[:, 0], first.at[:, 0], edge_recv.at[0]).wait()

    @pl.when(has_north)
    def _():
        pltpu.make_async_copy(first.at[:, rows + 1], first.at[:, rows + 1], edge_recv.at[1]).wait()

    def arrive(c):
        def wait_for(owner):
            part = weather.at[owner, *piece(c, rows, levels)]
            pltpu.make_async_copy(part, part, piece_recv.at[c, owner]).wait()

        for slot, owner in enumerate((beyond, beyond_next)):
            wait_for(owner)

            @pl.when(inner)
            def _():
                piece_copy(c, owner, near, relay_send, slot).start()

        wait_for(near)

    last_north = jnp.where(has_north, 1, closed_item)
    one_step = functools.partial(transport_row, weather, emission, first, second)
    two_step = functools.partial(transport_row, weather, emission, second, final)

    def second_step(row, north, south, zonal, part=None):
        two_step(row + 1, row, north, south, zonal, part)

    arrive(0)

    @pl.when(has_north)
    def _():
        edge_copy(4).start()

    one_step(rows, rows, last_north, 0, 2)

    @pl.when(has_north)
    def _():
        edge_copy(2).start()

    arrive(1)

    @pl.when(has_south)
    def _():
        pltpu.make_async_copy(weather.at[:, halo_item], weather.at[:, halo_item], edge_recv.at[4]).wait()

    one_step(1, 1, 4, halo_item, 5)

    @pl.when(has_south)
    def _():
        edge_copy(3).start()
        pltpu.make_async_copy(second.at[:, 0], second.at[:, 0], edge_recv.at[2]).wait()

    def middle(c, carry):
        arrive(c)
        one_step(c, c, 3 * c + 1, 3 * c - 2, 3 * c + 2)
        second_step(c - 2, 3 * c - 2, jnp.where(c == 2, halo_item, 3 * c - 5), 3 * c - 1)
        return carry

    lax.fori_loop(2, rows - 1, middle, 0)

    @pl.when(has_north)
    def _():
        pltpu.make_async_copy(second.at[:, rows + 1], second.at[:, rows + 1], edge_recv.at[3]).wait()

    c, done = rows - 1, 0
    for part in range(parts):
        arrive(c + part)
        here = (part * strips // parts, (part + 1) * strips // parts)
        one_step(c, c, 0, 3 * c - 2, 3 * c + 1, here)
        second_step(c - 2, 3 * c - 2, 3 * c - 5, 3 * c - 1, here)
        second_step(c, last_north, 0, 2, here)
        ready = here[1] if part == parts - 1 else here[1] - 1
        second_step(c - 1, 0, 3 * c - 2, 3 * c + 1, (done, ready))
        done = ready

    for c in range(pieces):
        piece_copy(c, z, near, piece_send, 0).wait_send()
        piece_copy(c, z, far, piece_send, 1).wait_send()

        @pl.when(inner)
        def _():
            piece_copy(c, beyond, near, relay_send, 0).wait_send()
            piece_copy(c, beyond_next, near, relay_send, 1).wait_send()

    for step in range(1, bands):
        control_copy(step).wait_send()

    @pl.when(has_north)
    def _():
        for slot in (0, 2, 4):
            edge_copy(slot).wait_send()

    @pl.when(has_south)
    def _():
        for slot in (1, 3):
            edge_copy(slot).wait_send()


def on_device_fused(
    tracer_state,
    control,
    prior_tiles,
    tile_index,
    region_map,
    region_sigma,
    zonal_courant,
    meridional_courant,
    vertical_diffusion,
):
    tracers, rows, levels, lons = tracer_state.shape
    bands = lax.axis_size("band")
    pieces = rows - 1 + last_parts(levels)
    dma = pltpu.SemaphoreType.DMA
    vmem = pl.BlockSpec(memory_space=pltpu.VMEM)
    hbm = pl.BlockSpec(memory_space=pltpu.HBM)
    operands = [
        pltpu.with_memory_space_constraint(operand, pltpu.HBM)
        for operand in (
            tile_index,
            region_sigma,
            region_map,
            prior_tiles,
            tracer_state,
            control,
            zonal_courant,
            meridional_courant,
            vertical_diffusion,
        )
    ]
    return pl.pallas_call(
        functools.partial(window_kernel, bands),
        out_shape=(
            jax.ShapeDtypeStruct(tracer_state.shape, jnp.float32),
            jax.ShapeDtypeStruct(control.shape, jnp.float32),
        ),
        in_specs=[hbm] * len(operands),
        out_specs=(vmem, vmem),
        scratch_shapes=[
            pltpu.VMEM((tracers, rows + 2, levels, lons), jnp.float32),
            pltpu.VMEM((tracers, rows + 2, levels, lons), jnp.float32),
            pltpu.VMEM((LINE, 3 * rows + 2, levels, lons // LINE), jnp.float32),
            pltpu.VMEM((tracers, bands * rows, lons), jnp.float32),
            pltpu.VMEM(tile_index.shape, jnp.int32),
            pltpu.VMEM(region_sigma.shape, jnp.float32),
            pltpu.VMEM(region_map.shape, jnp.int32),
            pltpu.VMEM(prior_tiles.shape, jnp.float32),
            dma((4,)),
            dma((rows,)),
            dma((1,)),
            dma((pieces, 2)),
            dma((pieces, LINE)),
            dma((pieces, 2)),
            dma((1,)),
            dma((bands,)),
            dma((bands,)),
            dma((5,)),
            dma((5,)),
        ],
        compiler_params=pltpu.CompilerParams(
            collective_id=0, has_side_effects=True, vmem_limit_bytes=40 * 1024 * 1024
        ),
    )(*operands)


def solution(mesh):
    in_specs = (
        P(("inv", "tracer"), "band", None, None),
        P(("inv", "tracer"), "band", None),
        P(),
        P(),
        P("band", None),
        P("tracer", None),
        P(("inv", "band"), None, "tracer"),
        P(("inv", "band"), None, "tracer"),
        P(("inv", "band"), None, "tracer"),
    )
    out_specs = (P(("inv", "tracer"), "band", None, None), P(("inv", "tracer"), "band", None))
    body = on_device_fused if fits_fused(mesh) else on_device
    return jax.shard_map(
        body, mesh=mesh, in_specs=in_specs, out_specs=out_specs, check_vma=False
    )
```

```python
import functools
import jax
import jax.numpy as jnp
from jax import lax
from jax.experimental import pallas as pl
from jax.experimental.pallas import tpu as pltpu
from jax.sharding import PartitionSpec as P

STEPS = 2


exact_dot = lax.Precision.HIGHEST


def padded_2(block, sides, width):
    for axis, dim in sides:
        count = lax.axis_size(axis)
        forward = [(i, i + 1) for i in range(count - 1)]
        backward = [(target, source) for source, target in forward]
        low = lax.ppermute(
            lax.slice_in_dim(block, block.shape[dim] - width, None, axis=dim), axis, forward
        )
        high = lax.ppermute(lax.slice_in_dim(block, 0, width, axis=dim), axis, backward)
        block = jnp.concatenate([low, block, high], axis=dim)
    return block


def passed_along(value, axis, by):
    count = lax.axis_size(axis)
    pairs = [(i, i + by) for i in range(count) if 0 <= i + by < count]
    return lax.ppermute(value, axis, pairs)


def vertical_mixing(tracer_now, mixing):
    levels = tracer_now.shape[2]
    upper_level = jnp.concatenate(
        [tracer_now[:, :, 1:], jnp.zeros_like(tracer_now[:, :, :1])], axis=2
    )
    open_top = (lax.broadcasted_iota(jnp.int32, (levels, 1), 0) < levels - 1).astype(jnp.float32)
    flux_up = mixing * (tracer_now - upper_level) * open_top
    flux_down = jnp.concatenate([jnp.zeros_like(flux_up[:, :, :1]), flux_up[:, :, :-1]], axis=2)
    return flux_up - flux_down


def advance(tracer_now, weather, sideways, north_open, source):
    zonal, zonal_west, meridional, meridional_south, mixing = weather
    west_side, east_side = sideways(tracer_now)
    flux_east = jnp.maximum(zonal, 0.0) * tracer_now + jnp.minimum(zonal, 0.0) * east_side
    flux_west = jnp.maximum(zonal_west, 0.0) * west_side + jnp.minimum(zonal_west, 0.0) * tracer_now
    padded = padded_2(tracer_now, (("band", 1),), 1)
    north_side = padded[:, 2:]
    south_side = padded[:, :-2]
    flux_north = (
        jnp.maximum(meridional, 0.0) * tracer_now + jnp.minimum(meridional, 0.0) * north_side
    ) * north_open
    flux_south = (
        jnp.maximum(meridional_south, 0.0) * south_side
        + jnp.minimum(meridional_south, 0.0) * tracer_now
    )
    result = (
        tracer_now
        - (flux_east - flux_west)
        - (flux_north - flux_south)
        - vertical_mixing(tracer_now, mixing)
    )
    return result.at[:, :, 0, :].add(source)


def on_device(
    tracer_state,
    control,
    prior_tiles,
    tile_index,
    region_map,
    region_sigma,
    zonal_courant,
    meridional_courant,
    vertical_diffusion,
):
    band_count = lax.axis_size("band")
    band_index = lax.axis_index("band")
    tiles_count = prior_tiles.shape[0]
    lat_rows = control.shape[1]
    choose = (
        tile_index[:, :, None] == lax.broadcasted_iota(jnp.int32, (1, 1, tiles_count), 2)
    ).astype(jnp.float32)
    own_row = lax.dynamic_slice_in_dim(choose, band_index, 1, 0)[0]
    blocks = jnp.einsum("bt,tmn->bmn", own_row, prior_tiles, precision=exact_dot)
    row_block = jnp.transpose(blocks, (1, 0, 2)).reshape(lat_rows, band_count * lat_rows)
    prior_field = jnp.einsum(
        "jm,kmn->kjn",
        row_block,
        lax.all_gather(control, "band", axis=1, tiled=True),
        precision=exact_dot,
    )
    regions = region_sigma.shape[1]
    onehot = (region_map[:, :, None] == lax.broadcasted_iota(jnp.int32, (1, 1, regions), 2)).astype(
        jnp.float32
    )
    cell_sigma = jnp.einsum("kr,jnr->kjn", region_sigma, onehot, precision=exact_dot)
    emission = cell_sigma * prior_field
    latitude = band_index * lat_rows + lax.broadcasted_iota(jnp.int32, (lat_rows, 1, 1), 0)
    north_open = (latitude < band_count * lat_rows - 1).astype(jnp.float32)
    south_row = passed_along(meridional_courant[-1:], "band", 1)
    zonal, meridional, mixing, south_edge = (
        lax.all_gather(zonal_courant, "tracer", axis=2, tiled=True),
        lax.all_gather(meridional_courant, "tracer", axis=2, tiled=True),
        lax.all_gather(vertical_diffusion, "tracer", axis=2, tiled=True),
        lax.all_gather(south_row, "tracer", axis=2, tiled=True),
    )
    weather = (
        zonal,
        jnp.roll(zonal, 1, axis=2),
        meridional,
        jnp.concatenate([south_edge, meridional[:-1]], axis=0),
        mixing,
    )

    def sideways(tracer_now):
        return (jnp.roll(tracer_now, 1, axis=3), jnp.roll(tracer_now, -1, axis=3))

    tracer_field = tracer_state
    for substep in range(STEPS):
        tracer_field = advance(tracer_field, weather, sideways, north_open, emission)
    return (tracer_field, emission)


LINE = 4
STRIP = 8
HOLD = 4
AHEAD = 2
LAST_PARTS = 1


def fits_fused(mesh):
    return mesh.shape["tracer"] == LINE and mesh.shape["band"] > 1


def last_parts(levels):
    return LAST_PARTS if levels % (LAST_PARTS * STRIP) == 0 else 1


def piece(c, rows, levels):
    if isinstance(c, int) and c == 0:
        return pl.ds(0, 4), pl.ds(0, levels)
    if isinstance(c, int) and c >= rows - 1:
        depth = levels // last_parts(levels)
        return pl.ds(3 * rows - 2, 2), pl.ds((c - rows + 1) * depth, depth)
    return pl.ds(3 * c + 1, 3), pl.ds(0, levels)


def mirror(z):
    return z + 1 - 2 * lax.rem(z, 2)


def transport_row(weather, emission, source, target, row, target_row, north, south, zonal, strips=None):
    tracers, _, levels, lons = source.shape
    sublane = lax.broadcasted_iota(jnp.int32, (STRIP, lons), 0)
    first_sublane, last_sublane = sublane == 0, sublane == STRIP - 1
    count = levels // STRIP
    begin, end = strips or (0, count)

    held_back = []

    def store():
        k, strip, result = held_back.pop(0)
        target[k, target_row, strip * STRIP : (strip + 1) * STRIP, :] = result

    def one(k):
        def field(at, strip):
            return source[k, at, strip * STRIP : (strip + 1) * STRIP, :]

        def item(index, strip):
            levels_here = slice(strip * STRIP, (strip + 1) * STRIP)
            return jnp.concatenate([weather[j, index, levels_here, :] for j in range(LINE)], axis=1)

        q = field(row, begin)
        q_raised = pltpu.roll(q, STRIP - 1, 0)
        below = jnp.zeros((STRIP, lons), jnp.float32)
        if begin > 0:
            q_below = field(row, begin - 1)
            q_up = jnp.where(last_sublane, q_raised, pltpu.roll(q_below, STRIP - 1, 0))
            below = pltpu.roll(item(zonal + 1, begin - 1) * (q_below - q_up), 1, 0)
        for strip in range(begin, end):
            u = item(zonal, strip)
            flux = u * jnp.where(u > 0.0, q, pltpu.roll(q, lons - 1, 1))
            result = q - flux + pltpu.roll(flux, 1, 1)
            m = item(north, strip)
            result = result - m * jnp.where(m > 0.0, q, field(row + 1, strip))
            m = item(south, strip)
            result = result + m * jnp.where(m > 0.0, field(row - 1, strip), q)
            if strip < count - 1:
                q_next = field(row, strip + 1)
                q_next_raised = pltpu.roll(q_next, STRIP - 1, 0)
                q_up = jnp.where(last_sublane, q_next_raised, q_raised)
            else:
                q_next = q_next_raised = None
                q_up = jnp.where(last_sublane, q, q_raised)
            flux = item(zonal + 1, strip) * (q - q_up)
            lowered = pltpu.roll(flux, 1, 0)
            result = result - flux + jnp.where(first_sublane, below, lowered)
            if strip == 0:
                result = result + jnp.where(first_sublane, emission[k, pl.ds(row - 1, 1), :], 0.0)
            held_back.append((k, strip, result))
            if len(held_back) > HOLD:
                store()
            q, q_raised, below = q_next, q_next_raised, lowered

    for k in range(tracers):
        one(k)
    while held_back:
        store()


def window_kernel(
    bands,
    tile_index_hbm,
    region_sigma_hbm,
    region_map_hbm,
    prior_tiles_hbm,
    state,
    control,
    zonal_courant,
    meridional_courant,
    vertical_diffusion,
    final,
    emission,
    first,
    second,
    weather,
    increments,
    tile_index,
    region_sigma,
    region_map,
    prior_tiles,
    table_sem,
    own_sem,
    state_sem,
    piece_send,
    piece_recv,
    relay_send,
    control_sem,
    control_send,
    control_recv,
    edge_send,
    edge_recv,
):
    z, b = lax.axis_index("tracer"), lax.axis_index("band")
    tracers, rows, levels, lons = state.shape
    regions = region_sigma.shape[1]
    parts, strips = last_parts(levels), levels // STRIP
    pieces = rows - 1 + parts
    halo_item, closed_item = 3 * rows, 3 * rows + 1
    near, far = mirror(z), jnp.where(z < 2, 2, 1)
    beyond, beyond_next = 3 - z, mirror(3 - z)
    inner = jnp.logical_and(z > 0, z < LINE - 1)
    has_south, has_north = b > 0, b < bands - 1

    def send(src, dst, send_sem, recv_sem, **where):
        return pltpu.make_async_remote_copy(
            src_ref=src, dst_ref=dst, send_sem=send_sem, recv_sem=recv_sem,
            device_id=where, device_id_type=pl.DeviceIdType.MESH,
        )

    barrier = pltpu.get_barrier_semaphore()
    def enter(**where):
        pl.semaphore_signal(barrier, inc=1, device_id=where, device_id_type=pl.DeviceIdType.MESH)

    enter(tracer=near)

    @pl.when(inner)
    def _():
        enter(tracer=beyond)
        enter(tracer=beyond_next)

    for step in range(1, bands):
        enter(band=lax.rem(b + step, bands))

    def own_item(c, index, array, row):
        return pltpu.make_async_copy(array.at[row], weather.at[z, index], own_sem.at[c])

    def start_own(c):
        row = (c + rows - 1) % rows
        index = 3 * c + 1
        if c == 0:
            own_item(c, 0, meridional_courant, rows - 2).start()
        if c < rows - 1:
            own_item(c, index, meridional_courant, row).start()
            index += 1
        own_item(c, index, zonal_courant, row).start()
        own_item(c, index + 1, vertical_diffusion, row).start()

    for c in range(rows):
        start_own(c)
    load_state = pltpu.make_async_copy(state, first.at[:, pl.ds(1, rows)], state_sem.at[0])
    load_state.start()
    own_rows = pl.ds(pl.multiple_of(b * rows, rows), rows)
    load_control = pltpu.make_async_copy(control, increments.at[:, own_rows], control_sem.at[0])
    load_control.start()
    tables = (
        (tile_index_hbm, tile_index), (region_sigma_hbm, region_sigma),
        (region_map_hbm, region_map), (prior_tiles_hbm, prior_tiles),
    )
    load_tables = [pltpu.make_async_copy(src, dst, table_sem.at[i]) for i, (src, dst) in enumerate(tables)]
    for load in load_tables:
        load.start()

    pl.semaphore_wait(barrier, 2 + bands - 1)

    def piece_copy(c, owner, target, sems, slot):
        part = weather.at[owner, *piece(c, rows, levels)]
        return send(part, part, sems.at[c, slot], piece_recv.at[c, owner], tracer=target)

    def feed(c):
        piece_copy(c, z, near, piece_send, 0).start()
        piece_copy(c, z, far, piece_send, 1).start()

    for c in range(rows):
        part = weather.at[z, piece(c, rows, levels)[0]]
        pltpu.make_async_copy(part, part, own_sem.at[c]).wait()
        if c < AHEAD:
            feed(c)

    def edge_copy(slot):
        src, dst, step = (
            (state.at[:, rows - 1], first.at[:, 0], 1),
            (state.at[:, 0], first.at[:, rows + 1], -1),
            (second.at[:, rows], second.at[:, 0], 1),
            (second.at[:, 1], second.at[:, rows + 1], -1),
            (weather.at[:, 1], weather.at[:, halo_item], 1),
        )[slot]
        target = jnp.clip(b + step, 0, bands - 1)
        return send(src, dst, edge_send.at[slot], edge_recv.at[slot], band=target)

    def control_copy(step):
        return send(
            control, increments.at[:, own_rows], control_send.at[step], control_recv.at[b],
            band=lax.rem(b + step, bands),
        )

    for step in range(1, bands):
        control_copy(step).start()

    @pl.when(has_north)
    def _():
        edge_copy(0).start()

    @pl.when(has_south)
    def _():
        edge_copy(1).start()

    zero_row = jnp.zeros((levels, lons), jnp.float32)
    zero_item = jnp.zeros((levels, lons // LINE), jnp.float32)
    for j in range(LINE):
        weather[j, closed_item] = zero_item

    @pl.when(b == 0)
    def _():
        for j in range(LINE):
            weather[j, halo_item] = zero_item
        for k in range(tracers):
            first[k, 0] = zero_row
            second[k, 0] = zero_row

    @pl.when(b == bands - 1)
    def _():
        for k in range(tracers):
            first[k, rows + 1] = zero_row
            second[k, rows + 1] = zero_row

    load_control.wait()
    for load in load_tables:
        load.wait()
    for step in range(1, bands):
        source_band = lax.rem(b + step, bands)
        part = increments.at[:, pl.ds(pl.multiple_of(source_band * rows, rows), rows)]
        pltpu.make_async_copy(part, part, control_recv.at[source_band]).wait()
    region = region_map[...]
    choice = tile_index[pl.ds(b, 1), :]
    tiles = []
    for j in range(bands):
        tile = jnp.zeros((rows, rows), jnp.float32)
        for t in range(prior_tiles.shape[0]):
            tile = jnp.where(choice[:, j : j + 1] == t, prior_tiles[t], tile)
        tiles.append(tile)
    for k in range(tracers):
        field = jnp.zeros((rows, lons), jnp.float32)
        for j in range(bands):
            for row in range(rows):
                field = field + tiles[j][:, row : row + 1] * increments[k, j * rows + row : j * rows + row + 1, :]
        sigma = jnp.zeros((rows, lons), jnp.float32)
        for r in range(regions):
            sigma = jnp.where(region == r, region_sigma[k : k + 1, r : r + 1], sigma)
        emission[k] = sigma * field

    load_state.wait()

    @pl.when(has_south)
    def _():
        pltpu.make_async_copy(first.at[:, 0], first.at[:, 0], edge_recv.at[0]).wait()

    @pl.when(has_north)
    def _():
        pltpu.make_async_copy(first.at[:, rows + 1], first.at[:, rows + 1], edge_recv.at[1]).wait()

    def arrive(c):
        if isinstance(c, int):
            if c + AHEAD < pieces:
                feed(c + AHEAD)
        else:

            @pl.when(c + AHEAD < rows - 1)
            def _():
                feed(c + AHEAD)

            for later in range(rows - 1, pieces):

                @pl.when(c + AHEAD == later)
                def _():
                    feed(later)

        def wait_for(owner):
            part = weather.at[owner, *piece(c, rows, levels)]
            pltpu.make_async_copy(part, part, piece_recv.at[c, owner]).wait()

        for slot, owner in enumerate((beyond, beyond_next)):
            wait_for(owner)

            @pl.when(inner)
            def _():
                piece_copy(c, owner, near, relay_send, slot).start()

        wait_for(near)

    last_north = jnp.where(has_north, 1, closed_item)
    one_step = functools.partial(transport_row, weather, emission, first, second)
    two_step = functools.partial(transport_row, weather, emission, second, final)

    def second_step(row, north, south, zonal, part=None):
        two_step(row + 1, row, north, south, zonal, part)

    arrive(0)

    @pl.when(has_north)
    def _():
        edge_copy(4).start()

    one_step(rows, rows, last_north, 0, 2)

    @pl.when(has_north)
    def _():
        edge_copy(2).start()

    arrive(1)

    @pl.when(has_south)
    def _():
        pltpu.make_async_copy(weather.at[:, halo_item], weather.at[:, halo_item], edge_recv.at[4]).wait()

    one_step(1, 1, 4, halo_item, 5)

    @pl.when(has_south)
    def _():
        edge_copy(3).start()
        pltpu.make_async_copy(second.at[:, 0], second.at[:, 0], edge_recv.at[2]).wait()

    def middle(c, carry):
        arrive(c)
        one_step(c, c, 3 * c + 1, 3 * c - 2, 3 * c + 2)
        second_step(c - 2, 3 * c - 2, jnp.where(c == 2, halo_item, 3 * c - 5), 3 * c - 1)
        return carry

    lax.fori_loop(2, rows - 1, middle, 0)

    @pl.when(has_north)
    def _():
        pltpu.make_async_copy(second.at[:, rows + 1], second.at[:, rows + 1], edge_recv.at[3]).wait()

    c, done = rows - 1, 0
    for part in range(parts):
        arrive(c + part)
        here = (part * strips // parts, (part + 1) * strips // parts)
        one_step(c, c, 0, 3 * c - 2, 3 * c + 1, here)
        second_step(c - 2, 3 * c - 2, 3 * c - 5, 3 * c - 1, here)
        second_step(c, last_north, 0, 2, here)
        ready = here[1] if part == parts - 1 else here[1] - 1
        second_step(c - 1, 0, 3 * c - 2, 3 * c + 1, (done, ready))
        done = ready

    for c in range(pieces):
        piece_copy(c, z, near, piece_send, 0).wait_send()
        piece_copy(c, z, far, piece_send, 1).wait_send()

        @pl.when(inner)
        def _():
            piece_copy(c, beyond, near, relay_send, 0).wait_send()
            piece_copy(c, beyond_next, near, relay_send, 1).wait_send()

    for step in range(1, bands):
        control_copy(step).wait_send()

    @pl.when(has_north)
    def _():
        for slot in (0, 2, 4):
            edge_copy(slot).wait_send()

    @pl.when(has_south)
    def _():
        for slot in (1, 3):
            edge_copy(slot).wait_send()


def on_device_fused(
    tracer_state,
    control,
    prior_tiles,
    tile_index,
    region_map,
    region_sigma,
    zonal_courant,
    meridional_courant,
    vertical_diffusion,
):
    tracers, rows, levels, lons = tracer_state.shape
    bands = lax.axis_size("band")
    pieces = rows - 1 + last_parts(levels)
    dma = pltpu.SemaphoreType.DMA
    vmem = pl.BlockSpec(memory_space=pltpu.VMEM)
    hbm = pl.BlockSpec(memory_space=pltpu.HBM)
    operands = [
        pltpu.with_memory_space_constraint(operand, pltpu.HBM)
        for operand in (
            tile_index,
            region_sigma,
            region_map,
            prior_tiles,
            tracer_state,
            control,
            zonal_courant,
            meridional_courant,
            vertical_diffusion,
        )
    ]
    return pl.pallas_call(
        functools.partial(window_kernel, bands),
        out_shape=(
            jax.ShapeDtypeStruct(tracer_state.shape, jnp.float32),
            jax.ShapeDtypeStruct(control.shape, jnp.float32),
        ),
        in_specs=[hbm] * len(operands),
        out_specs=(vmem, vmem),
        scratch_shapes=[
            pltpu.VMEM((tracers, rows + 2, levels, lons), jnp.float32),
            pltpu.VMEM((tracers, rows + 2, levels, lons), jnp.float32),
            pltpu.VMEM((LINE, 3 * rows + 2, levels, lons // LINE), jnp.float32),
            pltpu.VMEM((tracers, bands * rows, lons), jnp.float32),
            pltpu.VMEM(tile_index.shape, jnp.int32),
            pltpu.VMEM(region_sigma.shape, jnp.float32),
            pltpu.VMEM(region_map.shape, jnp.int32),
            pltpu.VMEM(prior_tiles.shape, jnp.float32),
            dma((4,)),
            dma((rows,)),
            dma((1,)),
            dma((pieces, 2)),
            dma((pieces, LINE)),
            dma((pieces, 2)),
            dma((1,)),
            dma((bands,)),
            dma((bands,)),
            dma((5,)),
            dma((5,)),
        ],
        compiler_params=pltpu.CompilerParams(
            collective_id=0, has_side_effects=True, vmem_limit_bytes=40 * 1024 * 1024
        ),
    )(*operands)


def solution(mesh):
    in_specs = (
        P(("inv", "tracer"), "band", None, None),
        P(("inv", "tracer"), "band", None),
        P(),
        P(),
        P("band", None),
        P("tracer", None),
        P(("inv", "band"), None, "tracer"),
        P(("inv", "band"), None, "tracer"),
        P(("inv", "band"), None, "tracer"),
    )
    out_specs = (P(("inv", "tracer"), "band", None, None), P(("inv", "tracer"), "band", None))
    body = on_device_fused if fits_fused(mesh) else on_device
    return jax.shard_map(
        body, mesh=mesh, in_specs=in_specs, out_specs=out_specs, check_vma=False
    )
```

```python
import functools
import jax
import jax.numpy as jnp
from jax import lax
from jax.experimental import pallas as pl
from jax.experimental.pallas import tpu as pltpu
from jax.sharding import PartitionSpec as P

STEPS = 2


exact_dot = lax.Precision.HIGHEST


def padded_2(block, sides, width):
    for axis, dim in sides:
        count = lax.axis_size(axis)
        forward = [(i, i + 1) for i in range(count - 1)]
        backward = [(target, source) for source, target in forward]
        low = lax.ppermute(
            lax.slice_in_dim(block, block.shape[dim] - width, None, axis=dim), axis, forward
        )
        high = lax.ppermute(lax.slice_in_dim(block, 0, width, axis=dim), axis, backward)
        block = jnp.concatenate([low, block, high], axis=dim)
    return block


def passed_along(value, axis, by):
    count = lax.axis_size(axis)
    pairs = [(i, i + by) for i in range(count) if 0 <= i + by < count]
    return lax.ppermute(value, axis, pairs)


def vertical_mixing(tracer_now, mixing):
    levels = tracer_now.shape[2]
    upper_level = jnp.concatenate(
        [tracer_now[:, :, 1:], jnp.zeros_like(tracer_now[:, :, :1])], axis=2
    )
    open_top = (lax.broadcasted_iota(jnp.int32, (levels, 1), 0) < levels - 1).astype(jnp.float32)
    flux_up = mixing * (tracer_now - upper_level) * open_top
    flux_down = jnp.concatenate([jnp.zeros_like(flux_up[:, :, :1]), flux_up[:, :, :-1]], axis=2)
    return flux_up - flux_down


def advance(tracer_now, weather, sideways, north_open, source):
    zonal, zonal_west, meridional, meridional_south, mixing = weather
    west_side, east_side = sideways(tracer_now)
    flux_east = jnp.maximum(zonal, 0.0) * tracer_now + jnp.minimum(zonal, 0.0) * east_side
    flux_west = jnp.maximum(zonal_west, 0.0) * west_side + jnp.minimum(zonal_west, 0.0) * tracer_now
    padded = padded_2(tracer_now, (("band", 1),), 1)
    north_side = padded[:, 2:]
    south_side = padded[:, :-2]
    flux_north = (
        jnp.maximum(meridional, 0.0) * tracer_now + jnp.minimum(meridional, 0.0) * north_side
    ) * north_open
    flux_south = (
        jnp.maximum(meridional_south, 0.0) * south_side
        + jnp.minimum(meridional_south, 0.0) * tracer_now
    )
    result = (
        tracer_now
        - (flux_east - flux_west)
        - (flux_north - flux_south)
        - vertical_mixing(tracer_now, mixing)
    )
    return result.at[:, :, 0, :].add(source)


def on_device(
    tracer_state,
    control,
    prior_tiles,
    tile_index,
    region_map,
    region_sigma,
    zonal_courant,
    meridional_courant,
    vertical_diffusion,
):
    band_count = lax.axis_size("band")
    band_index = lax.axis_index("band")
    tiles_count = prior_tiles.shape[0]
    lat_rows = control.shape[1]
    choose = (
        tile_index[:, :, None] == lax.broadcasted_iota(jnp.int32, (1, 1, tiles_count), 2)
    ).astype(jnp.float32)
    own_row = lax.dynamic_slice_in_dim(choose, band_index, 1, 0)[0]
    blocks = jnp.einsum("bt,tmn->bmn", own_row, prior_tiles, precision=exact_dot)
    row_block = jnp.transpose(blocks, (1, 0, 2)).reshape(lat_rows, band_count * lat_rows)
    prior_field = jnp.einsum(
        "jm,kmn->kjn",
        row_block,
        lax.all_gather(control, "band", axis=1, tiled=True),
        precision=exact_dot,
    )
    regions = region_sigma.shape[1]
    onehot = (region_map[:, :, None] == lax.broadcasted_iota(jnp.int32, (1, 1, regions), 2)).astype(
        jnp.float32
    )
    cell_sigma = jnp.einsum("kr,jnr->kjn", region_sigma, onehot, precision=exact_dot)
    emission = cell_sigma * prior_field
    latitude = band_index * lat_rows + lax.broadcasted_iota(jnp.int32, (lat_rows, 1, 1), 0)
    north_open = (latitude < band_count * lat_rows - 1).astype(jnp.float32)
    south_row = passed_along(meridional_courant[-1:], "band", 1)
    zonal, meridional, mixing, south_edge = (
        lax.all_gather(zonal_courant, "tracer", axis=2, tiled=True),
        lax.all_gather(meridional_courant, "tracer", axis=2, tiled=True),
        lax.all_gather(vertical_diffusion, "tracer", axis=2, tiled=True),
        lax.all_gather(south_row, "tracer", axis=2, tiled=True),
    )
    weather = (
        zonal,
        jnp.roll(zonal, 1, axis=2),
        meridional,
        jnp.concatenate([south_edge, meridional[:-1]], axis=0),
        mixing,
    )

    def sideways(tracer_now):
        return (jnp.roll(tracer_now, 1, axis=3), jnp.roll(tracer_now, -1, axis=3))

    tracer_field = tracer_state
    for substep in range(STEPS):
        tracer_field = advance(tracer_field, weather, sideways, north_open, emission)
    return (tracer_field, emission)


LINE = 4
STRIP = 8
HOLD = 4
LAST_PARTS = 1


def fits_fused(mesh):
    return mesh.shape["tracer"] == LINE and mesh.shape["band"] > 1


def last_parts(levels):
    return LAST_PARTS if levels % (LAST_PARTS * STRIP) == 0 else 1


def piece(c, rows, levels):
    if isinstance(c, int) and c == 0:
        return pl.ds(0, 4), pl.ds(0, levels)
    if isinstance(c, int) and c >= rows - 1:
        depth = levels // last_parts(levels)
        return pl.ds(3 * rows - 2, 2), pl.ds((c - rows + 1) * depth, depth)
    return pl.ds(3 * c + 1, 3), pl.ds(0, levels)


def mirror(z):
    return z + 1 - 2 * lax.rem(z, 2)


def transport_row(weather, emission, source, target, row, target_row, north, south, zonal, strips=None):
    tracers, _, levels, lons = source.shape
    sublane = lax.broadcasted_iota(jnp.int32, (STRIP, lons), 0)
    first_sublane, last_sublane = sublane == 0, sublane == STRIP - 1
    count = levels // STRIP
    begin, end = strips or (0, count)

    held_back = []

    def store():
        k, strip, result = held_back.pop(0)
        target[k, target_row, strip * STRIP : (strip + 1) * STRIP, :] = result

    def one(k):
        def field(at, strip):
            return source[k, at, strip * STRIP : (strip + 1) * STRIP, :]

        def item(index, strip):
            levels_here = slice(strip * STRIP, (strip + 1) * STRIP)
            return jnp.concatenate([weather[j, index, levels_here, :] for j in range(LINE)], axis=1)

        q = field(row, begin)
        q_raised = pltpu.roll(q, STRIP - 1, 0)
        below = jnp.zeros((STRIP, lons), jnp.float32)
        if begin > 0:
            q_below = field(row, begin - 1)
            q_up = jnp.where(last_sublane, q_raised, pltpu.roll(q_below, STRIP - 1, 0))
            below = pltpu.roll(item(zonal + 1, begin - 1) * (q_below - q_up), 1, 0)
        for strip in range(begin, end):
            u = item(zonal, strip)
            flux = u * jnp.where(u > 0.0, q, pltpu.roll(q, lons - 1, 1))
            result = q - flux + pltpu.roll(flux, 1, 1)
            m = item(north, strip)
            result = result - m * jnp.where(m > 0.0, q, field(row + 1, strip))
            m = item(south, strip)
            result = result + m * jnp.where(m > 0.0, field(row - 1, strip), q)
            if strip < count - 1:
                q_next = field(row, strip + 1)
                q_next_raised = pltpu.roll(q_next, STRIP - 1, 0)
                q_up = jnp.where(last_sublane, q_next_raised, q_raised)
            else:
                q_next = q_next_raised = None
                q_up = jnp.where(last_sublane, q, q_raised)
            flux = item(zonal + 1, strip) * (q - q_up)
            lowered = pltpu.roll(flux, 1, 0)
            result = result - flux + jnp.where(first_sublane, below, lowered)
            if strip == 0:
                result = result + jnp.where(first_sublane, emission[k, pl.ds(row - 1, 1), :], 0.0)
            held_back.append((k, strip, result))
            if len(held_back) > HOLD:
                store()
            q, q_raised, below = q_next, q_next_raised, lowered

    for k in range(tracers):
        one(k)
    while held_back:
        store()


def window_kernel(
    bands,
    tile_index_hbm,
    region_sigma_hbm,
    region_map_hbm,
    prior_tiles_hbm,
    state,
    control,
    zonal_courant,
    meridional_courant,
    vertical_diffusion,
    final,
    emission,
    first,
    second,
    weather,
    increments,
    tile_index,
    region_sigma,
    region_map,
    prior_tiles,
    table_sem,
    own_sem,
    state_sem,
    piece_send,
    piece_recv,
    relay_send,
    control_sem,
    control_send,
    control_recv,
    edge_send,
    edge_recv,
):
    z, b = lax.axis_index("tracer"), lax.axis_index("band")
    tracers, rows, levels, lons = state.shape
    regions = region_sigma.shape[1]
    parts, strips = last_parts(levels), levels // STRIP
    pieces = rows - 1 + parts
    halo_item, closed_item = 3 * rows, 3 * rows + 1
    near, far = mirror(z), jnp.where(z < 2, 2, 1)
    beyond, beyond_next = 3 - z, mirror(3 - z)
    inner = jnp.logical_and(z > 0, z < LINE - 1)
    has_south, has_north = b > 0, b < bands - 1

    def send(src, dst, send_sem, recv_sem, **where):
        return pltpu.make_async_remote_copy(
            src_ref=src, dst_ref=dst, send_sem=send_sem, recv_sem=recv_sem,
            device_id=where, device_id_type=pl.DeviceIdType.MESH,
        )

    barrier = pltpu.get_barrier_semaphore()
    def enter(**where):
        pl.semaphore_signal(barrier, inc=1, device_id=where, device_id_type=pl.DeviceIdType.MESH)

    enter(tracer=near)

    @pl.when(inner)
    def _():
        enter(tracer=beyond)
        enter(tracer=beyond_next)

    for step in range(1, bands):
        enter(band=lax.rem(b + step, bands))

    def own_item(c, index, array, row):
        return pltpu.make_async_copy(array.at[row], weather.at[z, index], own_sem.at[c])

    def start_own(c):
        row = (c + rows - 1) % rows
        index = 3 * c + 1
        if c == 0:
            own_item(c, 0, meridional_courant, rows - 2).start()
        if c < rows - 1:
            own_item(c, index, meridional_courant, row).start()
            index += 1
        own_item(c, index, zonal_courant, row).start()
        own_item(c, index + 1, vertical_diffusion, row).start()

    for c in range(rows):
        start_own(c)
    load_state = pltpu.make_async_copy(state, first.at[:, pl.ds(1, rows)], state_sem.at[0])
    load_state.start()
    own_rows = pl.ds(pl.multiple_of(b * rows, rows), rows)
    load_control = pltpu.make_async_copy(control, increments.at[:, own_rows], control_sem.at[0])
    load_control.start()
    tables = (
        (tile_index_hbm, tile_index), (region_sigma_hbm, region_sigma),
        (region_map_hbm, region_map), (prior_tiles_hbm, prior_tiles),
    )
    load_tables = [pltpu.make_async_copy(src, dst, table_sem.at[i]) for i, (src, dst) in enumerate(tables)]
    for load in load_tables:
        load.start()

    pl.semaphore_wait(barrier, 2 + bands - 1)

    def piece_copy(c, owner, target, sems, slot):
        part = weather.at[owner, *piece(c, rows, levels)]
        return send(part, part, sems.at[c, slot], piece_recv.at[c, owner], tracer=target)

    for c in range(pieces):
        if c < rows:
            part = weather.at[z, piece(c, rows, levels)[0]]
            pltpu.make_async_copy(part, part, own_sem.at[c]).wait()
        piece_copy(c, z, near, piece_send, 0).start()
        piece_copy(c, z, far, piece_send, 1).start()

    def edge_copy(slot):
        src, dst, step = (
            (state.at[:, rows - 1], first.at[:, 0], 1),
            (state.at[:, 0], first.at[:, rows + 1], -1),
            (second.at[:, rows], second.at[:, 0], 1),
            (second.at[:, 1], second.at[:, rows + 1], -1),
            (weather.at[:, 1], weather.at[:, halo_item], 1),
        )[slot]
        target = jnp.clip(b + step, 0, bands - 1)
        return send(src, dst, edge_send.at[slot], edge_recv.at[slot], band=target)

    def control_copy(step):
        return send(
            control, increments.at[:, own_rows], control_send.at[step], control_recv.at[b],
            band=lax.rem(b + step, bands),
        )

    for step in range(1, bands):
        control_copy(step).start()

    @pl.when(has_north)
    def _():
        edge_copy(0).start()

    @pl.when(has_south)
    def _():
        edge_copy(1).start()

    zero_row = jnp.zeros((levels, lons), jnp.float32)
    zero_item = jnp.zeros((levels, lons // LINE), jnp.float32)
    for j in range(LINE):
        weather[j, closed_item] = zero_item

    @pl.when(b == 0)
    def _():
        for j in range(LINE):
            weather[j, halo_item] = zero_item
        for k in range(tracers):
            first[k, 0] = zero_row
            second[k, 0] = zero_row

    @pl.when(b == bands - 1)
    def _():
        for k in range(tracers):
            first[k, rows + 1] = zero_row
            second[k, rows + 1] = zero_row

    load_control.wait()
    for load in load_tables:
        load.wait()
    for step in range(1, bands):
        source_band = lax.rem(b + step, bands)
        part = increments.at[:, pl.ds(pl.multiple_of(source_band * rows, rows), rows)]
        pltpu.make_async_copy(part, part, control_recv.at[source_band]).wait()
    region = region_map[...]
    choice = tile_index[pl.ds(b, 1), :]
    tiles = []
    for j in range(bands):
        tile = jnp.zeros((rows, rows), jnp.float32)
        for t in range(prior_tiles.shape[0]):
            tile = jnp.where(choice[:, j : j + 1] == t, prior_tiles[t], tile)
        tiles.append(tile)
    for k in range(tracers):
        field = jnp.zeros((rows, lons), jnp.float32)
        for j in range(bands):
            for row in range(rows):
                field = field + tiles[j][:, row : row + 1] * increments[k, j * rows + row : j * rows + row + 1, :]
        sigma = jnp.zeros((rows, lons), jnp.float32)
        for r in range(regions):
            sigma = jnp.where(region == r, region_sigma[k : k + 1, r : r + 1], sigma)
        emission[k] = sigma * field

    load_state.wait()

    @pl.when(has_south)
    def _():
        pltpu.make_async_copy(first.at[:, 0], first.at[:, 0], edge_recv.at[0]).wait()

    @pl.when(has_north)
    def _():
        pltpu.make_async_copy(first.at[:, rows + 1], first.at[:, rows + 1], edge_recv.at[1]).wait()

    def arrive(c):
        def wait_for(owner):
            part = weather.at[owner, *piece(c, rows, levels)]
            pltpu.make_async_copy(part, part, piece_recv.at[c, owner]).wait()

        for slot, owner in enumerate((beyond, beyond_next)):
            wait_for(owner)

            @pl.when(inner)
            def _():
                piece_copy(c, owner, near, relay_send, slot).start()

        wait_for(near)

    last_north = jnp.where(has_north, 1, closed_item)
    one_step = functools.partial(transport_row, weather, emission, first, second)
    two_step = functools.partial(transport_row, weather, emission, second, final)

    def second_step(row, north, south, zonal, part=None):
        two_step(row + 1, row, north, south, zonal, part)

    arrive(0)

    @pl.when(has_north)
    def _():
        edge_copy(4).start()

    one_step(rows, rows, last_north, 0, 2)

    @pl.when(has_north)
    def _():
        edge_copy(2).start()

    arrive(1)

    @pl.when(has_south)
    def _():
        pltpu.make_async_copy(weather.at[:, halo_item], weather.at[:, halo_item], edge_recv.at[4]).wait()

    one_step(1, 1, 4, halo_item, 5)

    @pl.when(has_south)
    def _():
        edge_copy(3).start()

    def middle(c, carry):
        arrive(c)
        one_step(c, c, 3 * c + 1, 3 * c - 2, 3 * c + 2)

        @pl.when(jnp.logical_and(has_south, c == 2))
        def _():
            pltpu.make_async_copy(second.at[:, 0], second.at[:, 0], edge_recv.at[2]).wait()

        second_step(c - 2, 3 * c - 2, jnp.where(c == 2, halo_item, 3 * c - 5), 3 * c - 1)
        return carry

    lax.fori_loop(2, rows - 1, middle, 0)

    @pl.when(has_north)
    def _():
        pltpu.make_async_copy(second.at[:, rows + 1], second.at[:, rows + 1], edge_recv.at[3]).wait()

    c, done = rows - 1, 0
    for part in range(parts):
        arrive(c + part)
        here = (part * strips // parts, (part + 1) * strips // parts)
        one_step(c, c, 0, 3 * c - 2, 3 * c + 1, here)
        second_step(c - 2, 3 * c - 2, 3 * c - 5, 3 * c - 1, here)
        second_step(c, last_north, 0, 2, here)
        ready = here[1] if part == parts - 1 else here[1] - 1
        second_step(c - 1, 0, 3 * c - 2, 3 * c + 1, (done, ready))
        done = ready

    for c in range(pieces):
        piece_copy(c, z, near, piece_send, 0).wait_send()
        piece_copy(c, z, far, piece_send, 1).wait_send()

        @pl.when(inner)
        def _():
            piece_copy(c, beyond, near, relay_send, 0).wait_send()
            piece_copy(c, beyond_next, near, relay_send, 1).wait_send()

    for step in range(1, bands):
        control_copy(step).wait_send()

    @pl.when(has_north)
    def _():
        for slot in (0, 2, 4):
            edge_copy(slot).wait_send()

    @pl.when(has_south)
    def _():
        for slot in (1, 3):
            edge_copy(slot).wait_send()


def move_out(final, emission, final_out, emission_out, sems):
    tracers = final.shape[0]
    copies = [pltpu.make_async_copy(emission, emission_out, sems.at[tracers])]
    copies += [pltpu.make_async_copy(final.at[k], final_out.at[k], sems.at[k]) for k in range(tracers)]
    for copy in copies:
        copy.start()
    for copy in copies:
        copy.wait()


def on_device_fused(
    tracer_state,
    control,
    prior_tiles,
    tile_index,
    region_map,
    region_sigma,
    zonal_courant,
    meridional_courant,
    vertical_diffusion,
):
    tracers, rows, levels, lons = tracer_state.shape
    bands = lax.axis_size("band")
    pieces = rows - 1 + last_parts(levels)
    dma = pltpu.SemaphoreType.DMA
    vmem = pl.BlockSpec(memory_space=pltpu.VMEM)
    hbm = pl.BlockSpec(memory_space=pltpu.HBM)
    operands = [
        pltpu.with_memory_space_constraint(operand, pltpu.HBM)
        for operand in (
            tile_index,
            region_sigma,
            region_map,
            prior_tiles,
            tracer_state,
            control,
            zonal_courant,
            meridional_courant,
            vertical_diffusion,
        )
    ]
    results = pl.pallas_call(
        functools.partial(window_kernel, bands),
        out_shape=(pltpu.VMEM(tracer_state.shape, jnp.float32), pltpu.VMEM(control.shape, jnp.float32)),
        in_specs=[hbm] * len(operands),
        out_specs=(vmem, vmem),
        scratch_shapes=[
            pltpu.VMEM((tracers, rows + 2, levels, lons), jnp.float32),
            pltpu.VMEM((tracers, rows + 2, levels, lons), jnp.float32),
            pltpu.VMEM((LINE, 3 * rows + 2, levels, lons // LINE), jnp.float32),
            pltpu.VMEM((tracers, bands * rows, lons), jnp.float32),
            pltpu.VMEM(tile_index.shape, jnp.int32),
            pltpu.VMEM(region_sigma.shape, jnp.float32),
            pltpu.VMEM(region_map.shape, jnp.int32),
            pltpu.VMEM(prior_tiles.shape, jnp.float32),
            dma((4,)),
            dma((rows,)),
            dma((1,)),
            dma((pieces, 2)),
            dma((pieces, LINE)),
            dma((pieces, 2)),
            dma((1,)),
            dma((bands,)),
            dma((bands,)),
            dma((5,)),
            dma((5,)),
        ],
        compiler_params=pltpu.CompilerParams(
            collective_id=0, has_side_effects=True, vmem_limit_bytes=40 * 1024 * 1024
        ),
    )(*operands)
    return pl.pallas_call(
        move_out,
        out_shape=(
            jax.ShapeDtypeStruct(tracer_state.shape, jnp.float32),
            jax.ShapeDtypeStruct(control.shape, jnp.float32),
        ),
        in_specs=[vmem, vmem],
        out_specs=(hbm, hbm),
        scratch_shapes=[dma((tracers + 1,))],
        compiler_params=pltpu.CompilerParams(vmem_limit_bytes=8 * 1024 * 1024),
    )(*[pltpu.with_memory_space_constraint(result, pltpu.VMEM) for result in results])


def solution(mesh):
    in_specs = (
        P(("inv", "tracer"), "band", None, None),
        P(("inv", "tracer"), "band", None),
        P(),
        P(),
        P("band", None),
        P("tracer", None),
        P(("inv", "band"), None, "tracer"),
        P(("inv", "band"), None, "tracer"),
        P(("inv", "band"), None, "tracer"),
    )
    out_specs = (P(("inv", "tracer"), "band", None, None), P(("inv", "tracer"), "band", None))
    body = on_device_fused if fits_fused(mesh) else on_device
    return jax.shard_map(
        body, mesh=mesh, in_specs=in_specs, out_specs=out_specs, check_vma=False
    )
```

```python
import functools
import jax
import jax.numpy as jnp
from jax import lax
from jax.experimental import pallas as pl
from jax.experimental.pallas import tpu as pltpu
from jax.sharding import PartitionSpec as P

STEPS = 2


exact_dot = lax.Precision.HIGHEST


def padded_2(block, sides, width):
    for axis, dim in sides:
        count = lax.axis_size(axis)
        forward = [(i, i + 1) for i in range(count - 1)]
        backward = [(target, source) for source, target in forward]
        low = lax.ppermute(
            lax.slice_in_dim(block, block.shape[dim] - width, None, axis=dim), axis, forward
        )
        high = lax.ppermute(lax.slice_in_dim(block, 0, width, axis=dim), axis, backward)
        block = jnp.concatenate([low, block, high], axis=dim)
    return block


def passed_along(value, axis, by):
    count = lax.axis_size(axis)
    pairs = [(i, i + by) for i in range(count) if 0 <= i + by < count]
    return lax.ppermute(value, axis, pairs)


def vertical_mixing(tracer_now, mixing):
    levels = tracer_now.shape[2]
    upper_level = jnp.concatenate(
        [tracer_now[:, :, 1:], jnp.zeros_like(tracer_now[:, :, :1])], axis=2
    )
    open_top = (lax.broadcasted_iota(jnp.int32, (levels, 1), 0) < levels - 1).astype(jnp.float32)
    flux_up = mixing * (tracer_now - upper_level) * open_top
    flux_down = jnp.concatenate([jnp.zeros_like(flux_up[:, :, :1]), flux_up[:, :, :-1]], axis=2)
    return flux_up - flux_down


def advance(tracer_now, weather, sideways, north_open, source):
    zonal, zonal_west, meridional, meridional_south, mixing = weather
    west_side, east_side = sideways(tracer_now)
    flux_east = jnp.maximum(zonal, 0.0) * tracer_now + jnp.minimum(zonal, 0.0) * east_side
    flux_west = jnp.maximum(zonal_west, 0.0) * west_side + jnp.minimum(zonal_west, 0.0) * tracer_now
    padded = padded_2(tracer_now, (("band", 1),), 1)
    north_side = padded[:, 2:]
    south_side = padded[:, :-2]
    flux_north = (
        jnp.maximum(meridional, 0.0) * tracer_now + jnp.minimum(meridional, 0.0) * north_side
    ) * north_open
    flux_south = (
        jnp.maximum(meridional_south, 0.0) * south_side
        + jnp.minimum(meridional_south, 0.0) * tracer_now
    )
    result = (
        tracer_now
        - (flux_east - flux_west)
        - (flux_north - flux_south)
        - vertical_mixing(tracer_now, mixing)
    )
    return result.at[:, :, 0, :].add(source)


def on_device(
    tracer_state,
    control,
    prior_tiles,
    tile_index,
    region_map,
    region_sigma,
    zonal_courant,
    meridional_courant,
    vertical_diffusion,
):
    band_count = lax.axis_size("band")
    band_index = lax.axis_index("band")
    tiles_count = prior_tiles.shape[0]
    lat_rows = control.shape[1]
    choose = (
        tile_index[:, :, None] == lax.broadcasted_iota(jnp.int32, (1, 1, tiles_count), 2)
    ).astype(jnp.float32)
    own_row = lax.dynamic_slice_in_dim(choose, band_index, 1, 0)[0]
    blocks = jnp.einsum("bt,tmn->bmn", own_row, prior_tiles, precision=exact_dot)
    row_block = jnp.transpose(blocks, (1, 0, 2)).reshape(lat_rows, band_count * lat_rows)
    prior_field = jnp.einsum(
        "jm,kmn->kjn",
        row_block,
        lax.all_gather(control, "band", axis=1, tiled=True),
        precision=exact_dot,
    )
    regions = region_sigma.shape[1]
    onehot = (region_map[:, :, None] == lax.broadcasted_iota(jnp.int32, (1, 1, regions), 2)).astype(
        jnp.float32
    )
    cell_sigma = jnp.einsum("kr,jnr->kjn", region_sigma, onehot, precision=exact_dot)
    emission = cell_sigma * prior_field
    latitude = band_index * lat_rows + lax.broadcasted_iota(jnp.int32, (lat_rows, 1, 1), 0)
    north_open = (latitude < band_count * lat_rows - 1).astype(jnp.float32)
    south_row = passed_along(meridional_courant[-1:], "band", 1)
    zonal, meridional, mixing, south_edge = (
        lax.all_gather(zonal_courant, "tracer", axis=2, tiled=True),
        lax.all_gather(meridional_courant, "tracer", axis=2, tiled=True),
        lax.all_gather(vertical_diffusion, "tracer", axis=2, tiled=True),
        lax.all_gather(south_row, "tracer", axis=2, tiled=True),
    )
    weather = (
        zonal,
        jnp.roll(zonal, 1, axis=2),
        meridional,
        jnp.concatenate([south_edge, meridional[:-1]], axis=0),
        mixing,
    )

    def sideways(tracer_now):
        return (jnp.roll(tracer_now, 1, axis=3), jnp.roll(tracer_now, -1, axis=3))

    tracer_field = tracer_state
    for substep in range(STEPS):
        tracer_field = advance(tracer_field, weather, sideways, north_open, emission)
    return (tracer_field, emission)


LINE = 4
STRIP = 8
HOLD = 4
LAST_PARTS = 1


def fits_fused(mesh):
    return mesh.shape["tracer"] == LINE and mesh.shape["band"] > 1


def last_parts(levels):
    return LAST_PARTS if levels % (LAST_PARTS * STRIP) == 0 else 1


def piece(c, rows, levels):
    if isinstance(c, int) and c == 0:
        return pl.ds(0, 4), pl.ds(0, levels)
    if isinstance(c, int) and c >= rows - 1:
        depth = levels // last_parts(levels)
        return pl.ds(3 * rows - 2, 2), pl.ds((c - rows + 1) * depth, depth)
    return pl.ds(3 * c + 1, 3), pl.ds(0, levels)


def mirror(z):
    return z + 1 - 2 * lax.rem(z, 2)


def transport_row(weather, emission, source, target, row, target_row, north, south, zonal, strips=None):
    tracers, _, levels, lons = source.shape
    sublane = lax.broadcasted_iota(jnp.int32, (STRIP, lons), 0)
    first_sublane, last_sublane = sublane == 0, sublane == STRIP - 1
    count = levels // STRIP
    begin, end = strips or (0, count)

    held_back = []

    def store():
        k, strip, result = held_back.pop(0)
        target[k, target_row, strip * STRIP : (strip + 1) * STRIP, :] = result

    def one(k):
        def field(at, strip):
            return source[k, at, strip * STRIP : (strip + 1) * STRIP, :]

        def item(index, strip):
            levels_here = slice(strip * STRIP, (strip + 1) * STRIP)
            return jnp.concatenate([weather[j, index, levels_here, :] for j in range(LINE)], axis=1)

        q = field(row, begin)
        q_raised = pltpu.roll(q, STRIP - 1, 0)
        below = jnp.zeros((STRIP, lons), jnp.float32)
        if begin > 0:
            q_below = field(row, begin - 1)
            q_up = jnp.where(last_sublane, q_raised, pltpu.roll(q_below, STRIP - 1, 0))
            below = pltpu.roll(item(zonal + 1, begin - 1) * (q_below - q_up), 1, 0)
        for strip in range(begin, end):
            u = item(zonal, strip)
            flux = u * jnp.where(u > 0.0, q, pltpu.roll(q, lons - 1, 1))
            result = q - flux + pltpu.roll(flux, 1, 1)
            m = item(north, strip)
            result = result - m * jnp.where(m > 0.0, q, field(row + 1, strip))
            m = item(south, strip)
            result = result + m * jnp.where(m > 0.0, field(row - 1, strip), q)
            if strip < count - 1:
                q_next = field(row, strip + 1)
                q_next_raised = pltpu.roll(q_next, STRIP - 1, 0)
                q_up = jnp.where(last_sublane, q_next_raised, q_raised)
            else:
                q_next = q_next_raised = None
                q_up = jnp.where(last_sublane, q, q_raised)
            flux = item(zonal + 1, strip) * (q - q_up)
            lowered = pltpu.roll(flux, 1, 0)
            result = result - flux + jnp.where(first_sublane, below, lowered)
            if strip == 0:
                result = result + jnp.where(first_sublane, emission[k, pl.ds(row - 1, 1), :], 0.0)
            held_back.append((k, strip, result))
            if len(held_back) > HOLD:
                store()
            q, q_raised, below = q_next, q_next_raised, lowered

    for k in range(tracers):
        one(k)
    while held_back:
        store()


def window_kernel(
    bands,
    tile_index_hbm,
    region_sigma_hbm,
    region_map_hbm,
    prior_tiles_hbm,
    state,
    control,
    zonal_courant,
    meridional_courant,
    vertical_diffusion,
    final,
    emission,
    first,
    second,
    weather,
    increments,
    tile_index,
    region_sigma,
    region_map,
    prior_tiles,
    table_sem,
    own_sem,
    state_sem,
    piece_send,
    piece_recv,
    relay_send,
    control_sem,
    control_send,
    control_recv,
    edge_send,
    edge_recv,
):
    z, b = lax.axis_index("tracer"), lax.axis_index("band")
    tracers, rows, levels, lons = state.shape
    regions = region_sigma.shape[1]
    parts, strips = last_parts(levels), levels // STRIP
    pieces = rows - 1 + parts
    halo_item, closed_item = 3 * rows, 3 * rows + 1
    near, far = mirror(z), jnp.where(z < 2, 2, 1)
    beyond, beyond_next = 3 - z, mirror(3 - z)
    inner = jnp.logical_and(z > 0, z < LINE - 1)
    has_south, has_north = b > 0, b < bands - 1

    def send(src, dst, send_sem, recv_sem, **where):
        return pltpu.make_async_remote_copy(
            src_ref=src, dst_ref=dst, send_sem=send_sem, recv_sem=recv_sem,
            device_id=where, device_id_type=pl.DeviceIdType.MESH,
        )

    barrier = pltpu.get_barrier_semaphore()
    def enter(**where):
        pl.semaphore_signal(barrier, inc=1, device_id=where, device_id_type=pl.DeviceIdType.MESH)

    for step in range(1, LINE):
        enter(tracer=lax.rem(z + step, LINE))
    for step in range(1, bands):
        enter(band=lax.rem(b + step, bands))

    def own_item(c, index, array, row):
        return pltpu.make_async_copy(array.at[row], weather.at[z, index], own_sem.at[c])

    def start_own(c):
        row = (c + rows - 1) % rows
        index = 3 * c + 1
        if c == 0:
            own_item(c, 0, meridional_courant, rows - 2).start()
        if c < rows - 1:
            own_item(c, index, meridional_courant, row).start()
            index += 1
        own_item(c, index, zonal_courant, row).start()
        own_item(c, index + 1, vertical_diffusion, row).start()

    for c in range(rows):
        start_own(c)
    load_state = pltpu.make_async_copy(state, first.at[:, pl.ds(1, rows)], state_sem.at[0])
    load_state.start()
    own_rows = pl.ds(pl.multiple_of(b * rows, rows), rows)
    load_control = pltpu.make_async_copy(control, increments.at[:, own_rows], control_sem.at[0])
    load_control.start()
    tables = (
        (tile_index_hbm, tile_index), (region_sigma_hbm, region_sigma),
        (region_map_hbm, region_map), (prior_tiles_hbm, prior_tiles),
    )
    load_tables = [pltpu.make_async_copy(src, dst, table_sem.at[i]) for i, (src, dst) in enumerate(tables)]
    for load in load_tables:
        load.start()

    pl.semaphore_wait(barrier, LINE - 1 + bands - 1)

    def piece_copy(c, owner, target, sems, slot):
        part = weather.at[owner, *piece(c, rows, levels)]
        return send(part, part, sems.at[c, slot], piece_recv.at[c, owner], tracer=target)

    for c in range(pieces):
        if c < rows:
            part = weather.at[z, piece(c, rows, levels)[0]]
            pltpu.make_async_copy(part, part, own_sem.at[c]).wait()
        piece_copy(c, z, near, piece_send, 0).start()
        piece_copy(c, z, far, piece_send, 1).start()

    def edge_copy(slot):
        src, dst, step = (
            (state.at[:, rows - 1], first.at[:, 0], 1),
            (state.at[:, 0], first.at[:, rows + 1], -1),
            (second.at[:, rows], second.at[:, 0], 1),
            (second.at[:, 1], second.at[:, rows + 1], -1),
            (weather.at[:, 1], weather.at[:, halo_item], 1),
        )[slot]
        target = jnp.clip(b + step, 0, bands - 1)
        return send(src, dst, edge_send.at[slot], edge_recv.at[slot], band=target)

    def control_copy(step):
        return send(
            control, increments.at[:, own_rows], control_send.at[step], control_recv.at[b],
            band=lax.rem(b + step, bands),
        )

    for step in range(1, bands):
        control_copy(step).start()

    @pl.when(has_north)
    def _():
        edge_copy(0).start()

    @pl.when(has_south)
    def _():
        edge_copy(1).start()

    zero_row = jnp.zeros((levels, lons), jnp.float32)
    zero_item = jnp.zeros((levels, lons // LINE), jnp.float32)
    for j in range(LINE):
        weather[j, closed_item] = zero_item

    @pl.when(b == 0)
    def _():
        for j in range(LINE):
            weather[j, halo_item] = zero_item
        for k in range(tracers):
            first[k, 0] = zero_row
            second[k, 0] = zero_row

    @pl.when(b == bands - 1)
    def _():
        for k in range(tracers):
            first[k, rows + 1] = zero_row
            second[k, rows + 1] = zero_row

    load_control.wait()
    for load in load_tables:
        load.wait()
    for step in range(1, bands):
        source_band = lax.rem(b + step, bands)
        part = increments.at[:, pl.ds(pl.multiple_of(source_band * rows, rows), rows)]
        pltpu.make_async_copy(part, part, control_recv.at[source_band]).wait()
    region = region_map[...]
    choice = tile_index[pl.ds(b, 1), :]
    tiles = []
    for j in range(bands):
        tile = jnp.zeros((rows, rows), jnp.float32)
        for t in range(prior_tiles.shape[0]):
            tile = jnp.where(choice[:, j : j + 1] == t, prior_tiles[t], tile)
        tiles.append(tile)
    for k in range(tracers):
        field = jnp.zeros((rows, lons), jnp.float32)
        for j in range(bands):
            for row in range(rows):
                field = field + tiles[j][:, row : row + 1] * increments[k, j * rows + row : j * rows + row + 1, :]
        sigma = jnp.zeros((rows, lons), jnp.float32)
        for r in range(regions):
            sigma = jnp.where(region == r, region_sigma[k : k + 1, r : r + 1], sigma)
        emission[k] = sigma * field

    load_state.wait()

    @pl.when(has_south)
    def _():
        pltpu.make_async_copy(first.at[:, 0], first.at[:, 0], edge_recv.at[0]).wait()

    @pl.when(has_north)
    def _():
        pltpu.make_async_copy(first.at[:, rows + 1], first.at[:, rows + 1], edge_recv.at[1]).wait()

    def arrive(c):
        def wait_for(owner):
            part = weather.at[owner, *piece(c, rows, levels)]
            pltpu.make_async_copy(part, part, piece_recv.at[c, owner]).wait()

        for slot, owner in enumerate((beyond, beyond_next)):
            wait_for(owner)

            @pl.when(inner)
            def _():
                piece_copy(c, owner, near, relay_send, slot).start()

        wait_for(near)

    last_north = jnp.where(has_north, 1, closed_item)
    one_step = functools.partial(transport_row, weather, emission, first, second)
    two_step = functools.partial(transport_row, weather, emission, second, final)

    def second_step(row, north, south, zonal, part=None):
        two_step(row + 1, row, north, south, zonal, part)

    arrive(0)

    @pl.when(has_north)
    def _():
        edge_copy(4).start()

    one_step(rows, rows, last_north, 0, 2)

    @pl.when(has_north)
    def _():
        edge_copy(2).start()

    arrive(1)

    @pl.when(has_south)
    def _():
        pltpu.make_async_copy(weather.at[:, halo_item], weather.at[:, halo_item], edge_recv.at[4]).wait()

    one_step(1, 1, 4, halo_item, 5)

    @pl.when(has_south)
    def _():
        edge_copy(3).start()

    def middle(c, carry):
        arrive(c)
        one_step(c, c, 3 * c + 1, 3 * c - 2, 3 * c + 2)

        @pl.when(jnp.logical_and(has_south, c == 2))
        def _():
            pltpu.make_async_copy(second.at[:, 0], second.at[:, 0], edge_recv.at[2]).wait()

        second_step(c - 2, 3 * c - 2, jnp.where(c == 2, halo_item, 3 * c - 5), 3 * c - 1)
        return carry

    lax.fori_loop(2, rows - 1, middle, 0)

    @pl.when(has_north)
    def _():
        pltpu.make_async_copy(second.at[:, rows + 1], second.at[:, rows + 1], edge_recv.at[3]).wait()

    c, done = rows - 1, 0
    for part in range(parts):
        arrive(c + part)
        here = (part * strips // parts, (part + 1) * strips // parts)
        one_step(c, c, 0, 3 * c - 2, 3 * c + 1, here)
        second_step(c - 2, 3 * c - 2, 3 * c - 5, 3 * c - 1, here)
        second_step(c, last_north, 0, 2, here)
        ready = here[1] if part == parts - 1 else here[1] - 1
        second_step(c - 1, 0, 3 * c - 2, 3 * c + 1, (done, ready))
        done = ready

    for c in range(pieces):
        piece_copy(c, z, near, piece_send, 0).wait_send()
        piece_copy(c, z, far, piece_send, 1).wait_send()

        @pl.when(inner)
        def _():
            piece_copy(c, beyond, near, relay_send, 0).wait_send()
            piece_copy(c, beyond_next, near, relay_send, 1).wait_send()

    for step in range(1, bands):
        control_copy(step).wait_send()

    @pl.when(has_north)
    def _():
        for slot in (0, 2, 4):
            edge_copy(slot).wait_send()

    @pl.when(has_south)
    def _():
        for slot in (1, 3):
            edge_copy(slot).wait_send()


def move_out(final, emission, final_out, emission_out, sems):
    tracers = final.shape[0]
    copies = [pltpu.make_async_copy(emission, emission_out, sems.at[tracers])]
    copies += [pltpu.make_async_copy(final.at[k], final_out.at[k], sems.at[k]) for k in range(tracers)]
    for copy in copies:
        copy.start()
    for copy in copies:
        copy.wait()


def on_device_fused(
    tracer_state,
    control,
    prior_tiles,
    tile_index,
    region_map,
    region_sigma,
    zonal_courant,
    meridional_courant,
    vertical_diffusion,
):
    tracers, rows, levels, lons = tracer_state.shape
    bands = lax.axis_size("band")
    pieces = rows - 1 + last_parts(levels)
    dma = pltpu.SemaphoreType.DMA
    vmem = pl.BlockSpec(memory_space=pltpu.VMEM)
    hbm = pl.BlockSpec(memory_space=pltpu.HBM)
    operands = [
        pltpu.with_memory_space_constraint(operand, pltpu.HBM)
        for operand in (
            tile_index,
            region_sigma,
            region_map,
            prior_tiles,
            tracer_state,
            control,
            zonal_courant,
            meridional_courant,
            vertical_diffusion,
        )
    ]
    results = pl.pallas_call(
        functools.partial(window_kernel, bands),
        out_shape=(pltpu.VMEM(tracer_state.shape, jnp.float32), pltpu.VMEM(control.shape, jnp.float32)),
        in_specs=[hbm] * len(operands),
        out_specs=(vmem, vmem),
        scratch_shapes=[
            pltpu.VMEM((tracers, rows + 2, levels, lons), jnp.float32),
            pltpu.VMEM((tracers, rows + 2, levels, lons), jnp.float32),
            pltpu.VMEM((LINE, 3 * rows + 2, levels, lons // LINE), jnp.float32),
            pltpu.VMEM((tracers, bands * rows, lons), jnp.float32),
            pltpu.VMEM(tile_index.shape, jnp.int32),
            pltpu.VMEM(region_sigma.shape, jnp.float32),
            pltpu.VMEM(region_map.shape, jnp.int32),
            pltpu.VMEM(prior_tiles.shape, jnp.float32),
            dma((4,)),
            dma((rows,)),
            dma((1,)),
            dma((pieces, 2)),
            dma((pieces, LINE)),
            dma((pieces, 2)),
            dma((1,)),
            dma((bands,)),
            dma((bands,)),
            dma((5,)),
            dma((5,)),
        ],
        compiler_params=pltpu.CompilerParams(
            collective_id=0, has_side_effects=True, vmem_limit_bytes=40 * 1024 * 1024
        ),
    )(*operands)
    return pl.pallas_call(
        move_out,
        out_shape=(
            jax.ShapeDtypeStruct(tracer_state.shape, jnp.float32),
            jax.ShapeDtypeStruct(control.shape, jnp.float32),
        ),
        in_specs=[vmem, vmem],
        out_specs=(hbm, hbm),
        scratch_shapes=[dma((tracers + 1,))],
        compiler_params=pltpu.CompilerParams(vmem_limit_bytes=8 * 1024 * 1024),
    )(*[pltpu.with_memory_space_constraint(result, pltpu.VMEM) for result in results])


def solution(mesh):
    in_specs = (
        P(("inv", "tracer"), "band", None, None),
        P(("inv", "tracer"), "band", None),
        P(),
        P(),
        P("band", None),
        P("tracer", None),
        P(("inv", "band"), None, "tracer"),
        P(("inv", "band"), None, "tracer"),
        P(("inv", "band"), None, "tracer"),
    )
    out_specs = (P(("inv", "tracer"), "band", None, None), P(("inv", "tracer"), "band", None))
    body = on_device_fused if fits_fused(mesh) else on_device
    return jax.shard_map(
        body, mesh=mesh, in_specs=in_specs, out_specs=out_specs, check_vma=False
    )
```

```python
import functools
import jax
import jax.numpy as jnp
from jax import lax
from jax.experimental import pallas as pl
from jax.experimental.pallas import tpu as pltpu
from jax.sharding import PartitionSpec as P

STEPS = 2


exact_dot = lax.Precision.HIGHEST


def padded_2(block, sides, width):
    for axis, dim in sides:
        count = lax.axis_size(axis)
        forward = [(i, i + 1) for i in range(count - 1)]
        backward = [(target, source) for source, target in forward]
        low = lax.ppermute(
            lax.slice_in_dim(block, block.shape[dim] - width, None, axis=dim), axis, forward
        )
        high = lax.ppermute(lax.slice_in_dim(block, 0, width, axis=dim), axis, backward)
        block = jnp.concatenate([low, block, high], axis=dim)
    return block


def passed_along(value, axis, by):
    count = lax.axis_size(axis)
    pairs = [(i, i + by) for i in range(count) if 0 <= i + by < count]
    return lax.ppermute(value, axis, pairs)


def vertical_mixing(tracer_now, mixing):
    levels = tracer_now.shape[2]
    upper_level = jnp.concatenate(
        [tracer_now[:, :, 1:], jnp.zeros_like(tracer_now[:, :, :1])], axis=2
    )
    open_top = (lax.broadcasted_iota(jnp.int32, (levels, 1), 0) < levels - 1).astype(jnp.float32)
    flux_up = mixing * (tracer_now - upper_level) * open_top
    flux_down = jnp.concatenate([jnp.zeros_like(flux_up[:, :, :1]), flux_up[:, :, :-1]], axis=2)
    return flux_up - flux_down


def advance(tracer_now, weather, sideways, north_open, source):
    zonal, zonal_west, meridional, meridional_south, mixing = weather
    west_side, east_side = sideways(tracer_now)
    flux_east = jnp.maximum(zonal, 0.0) * tracer_now + jnp.minimum(zonal, 0.0) * east_side
    flux_west = jnp.maximum(zonal_west, 0.0) * west_side + jnp.minimum(zonal_west, 0.0) * tracer_now
    padded = padded_2(tracer_now, (("band", 1),), 1)
    north_side = padded[:, 2:]
    south_side = padded[:, :-2]
    flux_north = (
        jnp.maximum(meridional, 0.0) * tracer_now + jnp.minimum(meridional, 0.0) * north_side
    ) * north_open
    flux_south = (
        jnp.maximum(meridional_south, 0.0) * south_side
        + jnp.minimum(meridional_south, 0.0) * tracer_now
    )
    result = (
        tracer_now
        - (flux_east - flux_west)
        - (flux_north - flux_south)
        - vertical_mixing(tracer_now, mixing)
    )
    return result.at[:, :, 0, :].add(source)


def on_device(
    tracer_state,
    control,
    prior_tiles,
    tile_index,
    region_map,
    region_sigma,
    zonal_courant,
    meridional_courant,
    vertical_diffusion,
):
    band_count = lax.axis_size("band")
    band_index = lax.axis_index("band")
    tiles_count = prior_tiles.shape[0]
    lat_rows = control.shape[1]
    choose = (
        tile_index[:, :, None] == lax.broadcasted_iota(jnp.int32, (1, 1, tiles_count), 2)
    ).astype(jnp.float32)
    own_row = lax.dynamic_slice_in_dim(choose, band_index, 1, 0)[0]
    blocks = jnp.einsum("bt,tmn->bmn", own_row, prior_tiles, precision=exact_dot)
    row_block = jnp.transpose(blocks, (1, 0, 2)).reshape(lat_rows, band_count * lat_rows)
    prior_field = jnp.einsum(
        "jm,kmn->kjn",
        row_block,
        lax.all_gather(control, "band", axis=1, tiled=True),
        precision=exact_dot,
    )
    regions = region_sigma.shape[1]
    onehot = (region_map[:, :, None] == lax.broadcasted_iota(jnp.int32, (1, 1, regions), 2)).astype(
        jnp.float32
    )
    cell_sigma = jnp.einsum("kr,jnr->kjn", region_sigma, onehot, precision=exact_dot)
    emission = cell_sigma * prior_field
    latitude = band_index * lat_rows + lax.broadcasted_iota(jnp.int32, (lat_rows, 1, 1), 0)
    north_open = (latitude < band_count * lat_rows - 1).astype(jnp.float32)
    south_row = passed_along(meridional_courant[-1:], "band", 1)
    zonal, meridional, mixing, south_edge = (
        lax.all_gather(zonal_courant, "tracer", axis=2, tiled=True),
        lax.all_gather(meridional_courant, "tracer", axis=2, tiled=True),
        lax.all_gather(vertical_diffusion, "tracer", axis=2, tiled=True),
        lax.all_gather(south_row, "tracer", axis=2, tiled=True),
    )
    weather = (
        zonal,
        jnp.roll(zonal, 1, axis=2),
        meridional,
        jnp.concatenate([south_edge, meridional[:-1]], axis=0),
        mixing,
    )

    def sideways(tracer_now):
        return (jnp.roll(tracer_now, 1, axis=3), jnp.roll(tracer_now, -1, axis=3))

    tracer_field = tracer_state
    for substep in range(STEPS):
        tracer_field = advance(tracer_field, weather, sideways, north_open, emission)
    return (tracer_field, emission)


LINE = 4
STRIP = 8
LAST_PARTS = 1


def fits_fused(mesh):
    return mesh.shape["tracer"] == LINE and mesh.shape["band"] > 1


def last_parts(levels):
    return LAST_PARTS if levels % (LAST_PARTS * STRIP) == 0 else 1


def piece(c, rows, levels):
    if isinstance(c, int) and c == 0:
        return pl.ds(0, 4), pl.ds(0, levels)
    if isinstance(c, int) and c >= rows - 1:
        depth = levels // last_parts(levels)
        return pl.ds(3 * rows - 2, 2), pl.ds((c - rows + 1) * depth, depth)
    return pl.ds(3 * c + 1, 3), pl.ds(0, levels)


def mirror(z):
    return z + 1 - 2 * lax.rem(z, 2)


def transport_row(weather, emission, source, target, row, target_row, north, south, zonal, strips=None):
    tracers, _, levels, lons = source.shape
    sublane = lax.broadcasted_iota(jnp.int32, (STRIP, lons), 0)
    first_sublane, last_sublane = sublane == 0, sublane == STRIP - 1
    count = levels // STRIP
    begin, end = strips or (0, count)

    def one(k, carry):
        def field(at, strip):
            return source[k, at, strip * STRIP : (strip + 1) * STRIP, :]

        def item(index, strip):
            levels_here = slice(strip * STRIP, (strip + 1) * STRIP)
            return jnp.concatenate([weather[j, index, levels_here, :] for j in range(LINE)], axis=1)

        q = field(row, begin)
        q_raised = pltpu.roll(q, STRIP - 1, 0)
        below = jnp.zeros((STRIP, lons), jnp.float32)
        if begin > 0:
            q_below = field(row, begin - 1)
            q_up = jnp.where(last_sublane, q_raised, pltpu.roll(q_below, STRIP - 1, 0))
            below = pltpu.roll(item(zonal + 1, begin - 1) * (q_below - q_up), 1, 0)
        for strip in range(begin, end):
            u = item(zonal, strip)
            flux = u * jnp.where(u > 0.0, q, pltpu.roll(q, lons - 1, 1))
            result = q - flux + pltpu.roll(flux, 1, 1)
            m = item(north, strip)
            result = result - m * jnp.where(m > 0.0, q, field(row + 1, strip))
            m = item(south, strip)
            result = result + m * jnp.where(m > 0.0, field(row - 1, strip), q)
            if strip < count - 1:
                q_next = field(row, strip + 1)
                q_next_raised = pltpu.roll(q_next, STRIP - 1, 0)
                q_up = jnp.where(last_sublane, q_next_raised, q_raised)
            else:
                q_next = q_next_raised = None
                q_up = jnp.where(last_sublane, q, q_raised)
            flux = item(zonal + 1, strip) * (q - q_up)
            lowered = pltpu.roll(flux, 1, 0)
            result = result - flux + jnp.where(first_sublane, below, lowered)
            if strip == 0:
                result = result + jnp.where(first_sublane, emission[k, pl.ds(row - 1, 1), :], 0.0)
            target[k, target_row, strip * STRIP : (strip + 1) * STRIP, :] = result
            q, q_raised, below = q_next, q_next_raised, lowered
        return carry

    lax.fori_loop(0, tracers, one, 0)


def window_kernel(
    bands,
    tile_index_hbm,
    region_sigma_hbm,
    region_map_hbm,
    prior_tiles_hbm,
    state,
    control,
    zonal_courant,
    meridional_courant,
    vertical_diffusion,
    final,
    emission,
    first,
    second,
    weather,
    increments,
    tile_index,
    region_sigma,
    region_map,
    prior_tiles,
    table_sem,
    own_sem,
    state_sem,
    piece_send,
    piece_recv,
    relay_send,
    control_sem,
    control_send,
    control_recv,
    edge_send,
    edge_recv,
):
    z, b = lax.axis_index("tracer"), lax.axis_index("band")
    tracers, rows, levels, lons = state.shape
    regions = region_sigma.shape[1]
    parts, strips = last_parts(levels), levels // STRIP
    pieces = rows - 1 + parts
    halo_item, closed_item = 3 * rows, 3 * rows + 1
    near, far = mirror(z), jnp.where(z < 2, 2, 1)
    beyond, beyond_next = 3 - z, mirror(3 - z)
    inner = jnp.logical_and(z > 0, z < LINE - 1)
    has_south, has_north = b > 0, b < bands - 1

    def send(src, dst, send_sem, recv_sem, **where):
        return pltpu.make_async_remote_copy(
            src_ref=src, dst_ref=dst, send_sem=send_sem, recv_sem=recv_sem,
            device_id=where, device_id_type=pl.DeviceIdType.MESH,
        )

    barrier = pltpu.get_barrier_semaphore()
    def enter(**where):
        pl.semaphore_signal(barrier, inc=1, device_id=where, device_id_type=pl.DeviceIdType.MESH)

    for step in range(1, LINE):
        enter(tracer=lax.rem(z + step, LINE))
    for step in range(1, bands):
        enter(band=lax.rem(b + step, bands))

    def own_item(c, index, array, row):
        return pltpu.make_async_copy(array.at[row], weather.at[z, index], own_sem.at[c])

    def start_own(c):
        row = (c + rows - 1) % rows
        index = 3 * c + 1
        if c == 0:
            own_item(c, 0, meridional_courant, rows - 2).start()
        if c < rows - 1:
            own_item(c, index, meridional_courant, row).start()
            index += 1
        own_item(c, index, zonal_courant, row).start()
        own_item(c, index + 1, vertical_diffusion, row).start()

    for c in range(rows):
        start_own(c)
    load_state = pltpu.make_async_copy(state, first.at[:, pl.ds(1, rows)], state_sem.at[0])
    load_state.start()
    own_rows = pl.ds(pl.multiple_of(b * rows, rows), rows)
    load_control = pltpu.make_async_copy(control, increments.at[:, own_rows], control_sem.at[0])
    load_control.start()
    tables = (
        (tile_index_hbm, tile_index), (region_sigma_hbm, region_sigma),
        (region_map_hbm, region_map), (prior_tiles_hbm, prior_tiles),
    )
    load_tables = [pltpu.make_async_copy(src, dst, table_sem.at[i]) for i, (src, dst) in enumerate(tables)]
    for load in load_tables:
        load.start()

    pl.semaphore_wait(barrier, LINE - 1 + bands - 1)

    def piece_copy(c, owner, target, sems, slot):
        part = weather.at[owner, *piece(c, rows, levels)]
        return send(part, part, sems.at[c, slot], piece_recv.at[c, owner], tracer=target)

    for c in range(pieces):
        if c < rows:
            part = weather.at[z, piece(c, rows, levels)[0]]
            pltpu.make_async_copy(part, part, own_sem.at[c]).wait()
        piece_copy(c, z, near, piece_send, 0).start()
        piece_copy(c, z, far, piece_send, 1).start()

    def edge_copy(slot):
        src, dst, step = (
            (state.at[:, rows - 1], first.at[:, 0], 1),
            (state.at[:, 0], first.at[:, rows + 1], -1),
            (second.at[:, rows], second.at[:, 0], 1),
            (second.at[:, 1], second.at[:, rows + 1], -1),
            (weather.at[:, 1], weather.at[:, halo_item], 1),
        )[slot]
        target = jnp.clip(b + step, 0, bands - 1)
        return send(src, dst, edge_send.at[slot], edge_recv.at[slot], band=target)

    def control_copy(step):
        return send(
            control, increments.at[:, own_rows], control_send.at[step], control_recv.at[b],
            band=lax.rem(b + step, bands),
        )

    for step in range(1, bands):
        control_copy(step).start()

    @pl.when(has_north)
    def _():
        edge_copy(0).start()

    @pl.when(has_south)
    def _():
        edge_copy(1).start()

    zero_row = jnp.zeros((levels, lons), jnp.float32)
    zero_item = jnp.zeros((levels, lons // LINE), jnp.float32)
    for j in range(LINE):
        weather[j, closed_item] = zero_item

    @pl.when(b == 0)
    def _():
        for j in range(LINE):
            weather[j, halo_item] = zero_item
        for k in range(tracers):
            first[k, 0] = zero_row
            second[k, 0] = zero_row

    @pl.when(b == bands - 1)
    def _():
        for k in range(tracers):
            first[k, rows + 1] = zero_row
            second[k, rows + 1] = zero_row

    load_control.wait()
    for load in load_tables:
        load.wait()
    for step in range(1, bands):
        source_band = lax.rem(b + step, bands)
        part = increments.at[:, pl.ds(pl.multiple_of(source_band * rows, rows), rows)]
        pltpu.make_async_copy(part, part, control_recv.at[source_band]).wait()
    region = region_map[...]
    choice = tile_index[pl.ds(b, 1), :]
    tiles = []
    for j in range(bands):
        tile = jnp.zeros((rows, rows), jnp.float32)
        for t in range(prior_tiles.shape[0]):
            tile = jnp.where(choice[:, j : j + 1] == t, prior_tiles[t], tile)
        tiles.append(tile)
    for k in range(tracers):
        field = jnp.zeros((rows, lons), jnp.float32)
        for j in range(bands):
            for row in range(rows):
                field = field + tiles[j][:, row : row + 1] * increments[k, j * rows + row : j * rows + row + 1, :]
        sigma = jnp.zeros((rows, lons), jnp.float32)
        for r in range(regions):
            sigma = jnp.where(region == r, region_sigma[k : k + 1, r : r + 1], sigma)
        emission[k] = sigma * field

    load_state.wait()

    @pl.when(has_south)
    def _():
        pltpu.make_async_copy(first.at[:, 0], first.at[:, 0], edge_recv.at[0]).wait()

    @pl.when(has_north)
    def _():
        pltpu.make_async_copy(first.at[:, rows + 1], first.at[:, rows + 1], edge_recv.at[1]).wait()

    def arrive(c):
        def wait_for(owner):
            part = weather.at[owner, *piece(c, rows, levels)]
            pltpu.make_async_copy(part, part, piece_recv.at[c, owner]).wait()

        for slot, owner in enumerate((beyond, beyond_next)):
            wait_for(owner)

            @pl.when(inner)
            def _():
                piece_copy(c, owner, near, relay_send, slot).start()

        wait_for(near)

    last_north = jnp.where(has_north, 1, closed_item)
    one_step = functools.partial(transport_row, weather, emission, first, second)
    two_step = functools.partial(transport_row, weather, emission, second, final)

    def items(c):
        ends = c == rows - 1
        north = jnp.where(c == 0, last_north, jnp.where(ends, 0, 3 * c + 1))
        south = jnp.where(c == 0, 0, jnp.where(c == 1, halo_item, 3 * c - 2))
        return north, south, jnp.where(ends, 3 * c + 1, 3 * c + 2)

    def wait_edge(slot, ref):
        pltpu.make_async_copy(ref, ref, edge_recv.at[slot]).wait()

    def turn(c, carry):
        @pl.when(c < rows)
        def _():
            @pl.when(c == 0)
            def _():
                arrive(0)

            @pl.when(jnp.logical_and(c > 0, c < rows - 1))
            def _():
                arrive(c)

            @pl.when(c == rows - 1)
            def _():
                arrive(rows - 1)

            @pl.when(jnp.logical_and(has_north, c == 0))
            def _():
                edge_copy(4).start()

            @pl.when(jnp.logical_and(has_south, c == 1))
            def _():
                wait_edge(4, weather.at[:, halo_item])

            row = lax.rem(c + rows - 1, rows) + 1
            one_step(row, row, *items(c))

            @pl.when(jnp.logical_and(has_north, c == 0))
            def _():
                edge_copy(2).start()

            @pl.when(jnp.logical_and(has_south, c == 1))
            def _():
                edge_copy(3).start()

        @pl.when(c >= 2)
        def _():
            @pl.when(jnp.logical_and(has_south, c == 2))
            def _():
                wait_edge(2, second.at[:, 0])

            @pl.when(jnp.logical_and(has_north, c == rows + 1))
            def _():
                wait_edge(3, second.at[:, rows + 1])

            two_step(c - 1, c - 2, *items(lax.rem(c - 1, rows)))

        return carry

    lax.fori_loop(0, rows + 2, turn, 0)

    for c in range(pieces):
        piece_copy(c, z, near, piece_send, 0).wait_send()
        piece_copy(c, z, far, piece_send, 1).wait_send()

        @pl.when(inner)
        def _():
            piece_copy(c, beyond, near, relay_send, 0).wait_send()
            piece_copy(c, beyond_next, near, relay_send, 1).wait_send()

    for step in range(1, bands):
        control_copy(step).wait_send()

    @pl.when(has_north)
    def _():
        for slot in (0, 2, 4):
            edge_copy(slot).wait_send()

    @pl.when(has_south)
    def _():
        for slot in (1, 3):
            edge_copy(slot).wait_send()


def move_out(final, emission, final_out, emission_out, sems):
    tracers = final.shape[0]
    copies = [pltpu.make_async_copy(emission, emission_out, sems.at[tracers])]
    copies += [pltpu.make_async_copy(final.at[k], final_out.at[k], sems.at[k]) for k in range(tracers)]
    for copy in copies:
        copy.start()
    for copy in copies:
        copy.wait()


def on_device_fused(
    tracer_state,
    control,
    prior_tiles,
    tile_index,
    region_map,
    region_sigma,
    zonal_courant,
    meridional_courant,
    vertical_diffusion,
):
    tracers, rows, levels, lons = tracer_state.shape
    bands = lax.axis_size("band")
    pieces = rows - 1 + last_parts(levels)
    dma = pltpu.SemaphoreType.DMA
    vmem = pl.BlockSpec(memory_space=pltpu.VMEM)
    hbm = pl.BlockSpec(memory_space=pltpu.HBM)
    operands = [
        pltpu.with_memory_space_constraint(operand, pltpu.HBM)
        for operand in (
            tile_index,
            region_sigma,
            region_map,
            prior_tiles,
            tracer_state,
            control,
            zonal_courant,
            meridional_courant,
            vertical_diffusion,
        )
    ]
    results = pl.pallas_call(
        functools.partial(window_kernel, bands),
        out_shape=(pltpu.VMEM(tracer_state.shape, jnp.float32), pltpu.VMEM(control.shape, jnp.float32)),
        in_specs=[hbm] * len(operands),
        out_specs=(vmem, vmem),
        scratch_shapes=[
            pltpu.VMEM((tracers, rows + 2, levels, lons), jnp.float32),
            pltpu.VMEM((tracers, rows + 2, levels, lons), jnp.float32),
            pltpu.VMEM((LINE, 3 * rows + 2, levels, lons // LINE), jnp.float32),
            pltpu.VMEM((tracers, bands * rows, lons), jnp.float32),
            pltpu.VMEM(tile_index.shape, jnp.int32),
            pltpu.VMEM(region_sigma.shape, jnp.float32),
            pltpu.VMEM(region_map.shape, jnp.int32),
            pltpu.VMEM(prior_tiles.shape, jnp.float32),
            dma((4,)),
            dma((rows,)),
            dma((1,)),
            dma((pieces, 2)),
            dma((pieces, LINE)),
            dma((pieces, 2)),
            dma((1,)),
            dma((bands,)),
            dma((bands,)),
            dma((5,)),
            dma((5,)),
        ],
        compiler_params=pltpu.CompilerParams(
            collective_id=0, has_side_effects=True, vmem_limit_bytes=40 * 1024 * 1024
        ),
    )(*operands)
    return pl.pallas_call(
        move_out,
        out_shape=(
            jax.ShapeDtypeStruct(tracer_state.shape, jnp.float32),
            jax.ShapeDtypeStruct(control.shape, jnp.float32),
        ),
        in_specs=[vmem, vmem],
        out_specs=(hbm, hbm),
        scratch_shapes=[dma((tracers + 1,))],
        compiler_params=pltpu.CompilerParams(vmem_limit_bytes=8 * 1024 * 1024),
    )(*[pltpu.with_memory_space_constraint(result, pltpu.VMEM) for result in results])


def solution(mesh):
    in_specs = (
        P(("inv", "tracer"), "band", None, None),
        P(("inv", "tracer"), "band", None),
        P(),
        P(),
        P("band", None),
        P("tracer", None),
        P(("inv", "band"), None, "tracer"),
        P(("inv", "band"), None, "tracer"),
        P(("inv", "band"), None, "tracer"),
    )
    out_specs = (P(("inv", "tracer"), "band", None, None), P(("inv", "tracer"), "band", None))
    body = on_device_fused if fits_fused(mesh) else on_device
    return jax.shard_map(
        body, mesh=mesh, in_specs=in_specs, out_specs=out_specs, check_vma=False
    )
```

```python
import functools
import jax
import jax.numpy as jnp
from jax import lax
from jax.experimental import pallas as pl
from jax.experimental.pallas import tpu as pltpu
from jax.sharding import PartitionSpec as P

STEPS = 2


exact_dot = lax.Precision.HIGHEST


def padded_2(block, sides, width):
    for axis, dim in sides:
        count = lax.axis_size(axis)
        forward = [(i, i + 1) for i in range(count - 1)]
        backward = [(target, source) for source, target in forward]
        low = lax.ppermute(
            lax.slice_in_dim(block, block.shape[dim] - width, None, axis=dim), axis, forward
        )
        high = lax.ppermute(lax.slice_in_dim(block, 0, width, axis=dim), axis, backward)
        block = jnp.concatenate([low, block, high], axis=dim)
    return block


def passed_along(value, axis, by):
    count = lax.axis_size(axis)
    pairs = [(i, i + by) for i in range(count) if 0 <= i + by < count]
    return lax.ppermute(value, axis, pairs)


def vertical_mixing(tracer_now, mixing):
    levels = tracer_now.shape[2]
    upper_level = jnp.concatenate(
        [tracer_now[:, :, 1:], jnp.zeros_like(tracer_now[:, :, :1])], axis=2
    )
    open_top = (lax.broadcasted_iota(jnp.int32, (levels, 1), 0) < levels - 1).astype(jnp.float32)
    flux_up = mixing * (tracer_now - upper_level) * open_top
    flux_down = jnp.concatenate([jnp.zeros_like(flux_up[:, :, :1]), flux_up[:, :, :-1]], axis=2)
    return flux_up - flux_down


def advance(tracer_now, weather, sideways, north_open, source):
    zonal, zonal_west, meridional, meridional_south, mixing = weather
    west_side, east_side = sideways(tracer_now)
    flux_east = jnp.maximum(zonal, 0.0) * tracer_now + jnp.minimum(zonal, 0.0) * east_side
    flux_west = jnp.maximum(zonal_west, 0.0) * west_side + jnp.minimum(zonal_west, 0.0) * tracer_now
    padded = padded_2(tracer_now, (("band", 1),), 1)
    north_side = padded[:, 2:]
    south_side = padded[:, :-2]
    flux_north = (
        jnp.maximum(meridional, 0.0) * tracer_now + jnp.minimum(meridional, 0.0) * north_side
    ) * north_open
    flux_south = (
        jnp.maximum(meridional_south, 0.0) * south_side
        + jnp.minimum(meridional_south, 0.0) * tracer_now
    )
    result = (
        tracer_now
        - (flux_east - flux_west)
        - (flux_north - flux_south)
        - vertical_mixing(tracer_now, mixing)
    )
    return result.at[:, :, 0, :].add(source)


def on_device(
    tracer_state,
    control,
    prior_tiles,
    tile_index,
    region_map,
    region_sigma,
    zonal_courant,
    meridional_courant,
    vertical_diffusion,
):
    band_count = lax.axis_size("band")
    band_index = lax.axis_index("band")
    tiles_count = prior_tiles.shape[0]
    lat_rows = control.shape[1]
    choose = (
        tile_index[:, :, None] == lax.broadcasted_iota(jnp.int32, (1, 1, tiles_count), 2)
    ).astype(jnp.float32)
    own_row = lax.dynamic_slice_in_dim(choose, band_index, 1, 0)[0]
    blocks = jnp.einsum("bt,tmn->bmn", own_row, prior_tiles, precision=exact_dot)
    row_block = jnp.transpose(blocks, (1, 0, 2)).reshape(lat_rows, band_count * lat_rows)
    prior_field = jnp.einsum(
        "jm,kmn->kjn",
        row_block,
        lax.all_gather(control, "band", axis=1, tiled=True),
        precision=exact_dot,
    )
    regions = region_sigma.shape[1]
    onehot = (region_map[:, :, None] == lax.broadcasted_iota(jnp.int32, (1, 1, regions), 2)).astype(
        jnp.float32
    )
    cell_sigma = jnp.einsum("kr,jnr->kjn", region_sigma, onehot, precision=exact_dot)
    emission = cell_sigma * prior_field
    latitude = band_index * lat_rows + lax.broadcasted_iota(jnp.int32, (lat_rows, 1, 1), 0)
    north_open = (latitude < band_count * lat_rows - 1).astype(jnp.float32)
    south_row = passed_along(meridional_courant[-1:], "band", 1)
    zonal, meridional, mixing, south_edge = (
        lax.all_gather(zonal_courant, "tracer", axis=2, tiled=True),
        lax.all_gather(meridional_courant, "tracer", axis=2, tiled=True),
        lax.all_gather(vertical_diffusion, "tracer", axis=2, tiled=True),
        lax.all_gather(south_row, "tracer", axis=2, tiled=True),
    )
    weather = (
        zonal,
        jnp.roll(zonal, 1, axis=2),
        meridional,
        jnp.concatenate([south_edge, meridional[:-1]], axis=0),
        mixing,
    )

    def sideways(tracer_now):
        return (jnp.roll(tracer_now, 1, axis=3), jnp.roll(tracer_now, -1, axis=3))

    tracer_field = tracer_state
    for substep in range(STEPS):
        tracer_field = advance(tracer_field, weather, sideways, north_open, emission)
    return (tracer_field, emission)


LINE = 4
STRIP = 8
LAST_PARTS = 1


def fits_fused(mesh):
    return mesh.shape["tracer"] == LINE and mesh.shape["band"] > 1


def last_parts(levels):
    return LAST_PARTS if levels % (LAST_PARTS * STRIP) == 0 else 1


def piece(c, rows, levels):
    if isinstance(c, int) and c == 0:
        return pl.ds(0, 4), pl.ds(0, levels)
    if isinstance(c, int) and c >= rows - 1:
        depth = levels // last_parts(levels)
        return pl.ds(3 * rows - 2, 2), pl.ds((c - rows + 1) * depth, depth)
    return pl.ds(3 * c + 1, 3), pl.ds(0, levels)


def mirror(z):
    return z + 1 - 2 * lax.rem(z, 2)


def transport_row(weather, emission, source, target, row, target_row, north, south, zonal, strips=None):
    tracers, _, levels, lons = source.shape
    sublane = lax.broadcasted_iota(jnp.int32, (STRIP, lons), 0)
    first_sublane, last_sublane = sublane == 0, sublane == STRIP - 1
    count = levels // STRIP
    begin, end = strips or (0, count)

    def one(k, carry):
        def field(at, strip):
            return source[k, at, strip * STRIP : (strip + 1) * STRIP, :]

        def item(index, strip):
            levels_here = slice(strip * STRIP, (strip + 1) * STRIP)
            return jnp.concatenate([weather[j, index, levels_here, :] for j in range(LINE)], axis=1)

        q = field(row, begin)
        q_raised = pltpu.roll(q, STRIP - 1, 0)
        below = jnp.zeros((STRIP, lons), jnp.float32)
        if begin > 0:
            q_below = field(row, begin - 1)
            q_up = jnp.where(last_sublane, q_raised, pltpu.roll(q_below, STRIP - 1, 0))
            below = pltpu.roll(item(zonal + 1, begin - 1) * (q_below - q_up), 1, 0)
        for strip in range(begin, end):
            u = item(zonal, strip)
            flux = u * jnp.where(u > 0.0, q, pltpu.roll(q, lons - 1, 1))
            result = q - flux + pltpu.roll(flux, 1, 1)
            m = item(north, strip)
            result = result - m * jnp.where(m > 0.0, q, field(row + 1, strip))
            m = item(south, strip)
            result = result + m * jnp.where(m > 0.0, field(row - 1, strip), q)
            if strip < count - 1:
                q_next = field(row, strip + 1)
                q_next_raised = pltpu.roll(q_next, STRIP - 1, 0)
                q_up = jnp.where(last_sublane, q_next_raised, q_raised)
            else:
                q_next = q_next_raised = None
                q_up = jnp.where(last_sublane, q, q_raised)
            flux = item(zonal + 1, strip) * (q - q_up)
            lowered = pltpu.roll(flux, 1, 0)
            result = result - flux + jnp.where(first_sublane, below, lowered)
            if strip == 0:
                result = result + jnp.where(first_sublane, emission[k, pl.ds(row - 1, 1), :], 0.0)
            target[k, target_row, strip * STRIP : (strip + 1) * STRIP, :] = result
            q, q_raised, below = q_next, q_next_raised, lowered
        return carry

    lax.fori_loop(0, tracers, one, 0)


def window_kernel(
    bands,
    tile_index_hbm,
    region_sigma_hbm,
    region_map_hbm,
    prior_tiles_hbm,
    state,
    control,
    zonal_courant,
    meridional_courant,
    vertical_diffusion,
    final,
    emission,
    first,
    second,
    weather,
    increments,
    tile_index,
    region_sigma,
    region_map,
    prior_tiles,
    table_sem,
    own_sem,
    state_sem,
    piece_send,
    piece_recv,
    relay_send,
    control_sem,
    control_send,
    control_recv,
    edge_send,
    edge_recv,
):
    z, b = lax.axis_index("tracer"), lax.axis_index("band")
    tracers, rows, levels, lons = state.shape
    regions = region_sigma.shape[1]
    parts, strips = last_parts(levels), levels // STRIP
    pieces = rows - 1 + parts
    halo_item, closed_item = 3 * rows, 3 * rows + 1
    near, far = mirror(z), jnp.where(z < 2, 2, 1)
    beyond, beyond_next = 3 - z, mirror(3 - z)
    inner = jnp.logical_and(z > 0, z < LINE - 1)
    has_south, has_north = b > 0, b < bands - 1

    def send(src, dst, send_sem, recv_sem, **where):
        return pltpu.make_async_remote_copy(
            src_ref=src, dst_ref=dst, send_sem=send_sem, recv_sem=recv_sem,
            device_id=where, device_id_type=pl.DeviceIdType.MESH,
        )

    barrier = pltpu.get_barrier_semaphore()
    def enter(**where):
        pl.semaphore_signal(barrier, inc=1, device_id=where, device_id_type=pl.DeviceIdType.MESH)

    enter(tracer=near)

    @pl.when(inner)
    def _():
        enter(tracer=beyond)
        enter(tracer=beyond_next)
    for step in range(1, bands):
        enter(band=lax.rem(b + step, bands))

    def own_item(c, index, array, row):
        return pltpu.make_async_copy(array.at[row], weather.at[z, index], own_sem.at[c])

    def start_own(c):
        row = (c + rows - 1) % rows
        index = 3 * c + 1
        if c == 0:
            own_item(c, 0, meridional_courant, rows - 2).start()
        if c < rows - 1:
            own_item(c, index, meridional_courant, row).start()
            index += 1
        own_item(c, index, zonal_courant, row).start()
        own_item(c, index + 1, vertical_diffusion, row).start()

    for c in range(rows):
        start_own(c)
    load_state = pltpu.make_async_copy(state, first.at[:, pl.ds(1, rows)], state_sem.at[0])
    load_state.start()
    own_rows = pl.ds(pl.multiple_of(b * rows, rows), rows)
    load_control = pltpu.make_async_copy(control, increments.at[:, own_rows], control_sem.at[0])
    load_control.start()
    tables = (
        (tile_index_hbm, tile_index), (region_sigma_hbm, region_sigma),
        (region_map_hbm, region_map), (prior_tiles_hbm, prior_tiles),
    )
    load_tables = [pltpu.make_async_copy(src, dst, table_sem.at[i]) for i, (src, dst) in enumerate(tables)]
    for load in load_tables:
        load.start()

    pl.semaphore_wait(barrier, 2 + bands - 1)

    def piece_copy(c, owner, target, sems, slot):
        part = weather.at[owner, *piece(c, rows, levels)]
        return send(part, part, sems.at[c, slot], piece_recv.at[c, owner], tracer=target)

    for c in range(pieces):
        if c < rows:
            part = weather.at[z, piece(c, rows, levels)[0]]
            pltpu.make_async_copy(part, part, own_sem.at[c]).wait()
        piece_copy(c, z, near, piece_send, 0).start()
        piece_copy(c, z, far, piece_send, 1).start()

    def edge_copy(slot):
        src, dst, step = (
            (state.at[:, rows - 1], first.at[:, 0], 1),
            (state.at[:, 0], first.at[:, rows + 1], -1),
            (second.at[:, rows], second.at[:, 0], 1),
            (second.at[:, 1], second.at[:, rows + 1], -1),
            (weather.at[:, 1], weather.at[:, halo_item], 1),
        )[slot]
        target = jnp.clip(b + step, 0, bands - 1)
        return send(src, dst, edge_send.at[slot], edge_recv.at[slot], band=target)

    def control_copy(step):
        return send(
            control, increments.at[:, own_rows], control_send.at[step], control_recv.at[b],
            band=lax.rem(b + step, bands),
        )

    for step in range(1, bands):
        control_copy(step).start()

    @pl.when(has_north)
    def _():
        edge_copy(0).start()

    @pl.when(has_south)
    def _():
        edge_copy(1).start()

    zero_row = jnp.zeros((levels, lons), jnp.float32)
    zero_item = jnp.zeros((levels, lons // LINE), jnp.float32)
    for j in range(LINE):
        weather[j, closed_item] = zero_item

    @pl.when(b == 0)
    def _():
        for j in range(LINE):
            weather[j, halo_item] = zero_item
        for k in range(tracers):
            first[k, 0] = zero_row
            second[k, 0] = zero_row

    @pl.when(b == bands - 1)
    def _():
        for k in range(tracers):
            first[k, rows + 1] = zero_row
            second[k, rows + 1] = zero_row

    load_control.wait()
    for load in load_tables:
        load.wait()
    for step in range(1, bands):
        source_band = lax.rem(b + step, bands)
        part = increments.at[:, pl.ds(pl.multiple_of(source_band * rows, rows), rows)]
        pltpu.make_async_copy(part, part, control_recv.at[source_band]).wait()
    region = region_map[...]
    choice = tile_index[pl.ds(b, 1), :]
    tiles = []
    for j in range(bands):
        tile = jnp.zeros((rows, rows), jnp.float32)
        for t in range(prior_tiles.shape[0]):
            tile = jnp.where(choice[:, j : j + 1] == t, prior_tiles[t], tile)
        tiles.append(tile)
    for k in range(tracers):
        field = jnp.zeros((rows, lons), jnp.float32)
        for j in range(bands):
            for row in range(rows):
                field = field + tiles[j][:, row : row + 1] * increments[k, j * rows + row : j * rows + row + 1, :]
        sigma = jnp.zeros((rows, lons), jnp.float32)
        for r in range(regions):
            sigma = jnp.where(region == r, region_sigma[k : k + 1, r : r + 1], sigma)
        emission[k] = sigma * field

    load_state.wait()

    @pl.when(has_south)
    def _():
        pltpu.make_async_copy(first.at[:, 0], first.at[:, 0], edge_recv.at[0]).wait()

    @pl.when(has_north)
    def _():
        pltpu.make_async_copy(first.at[:, rows + 1], first.at[:, rows + 1], edge_recv.at[1]).wait()

    def arrive(c):
        def wait_for(owner):
            part = weather.at[owner, *piece(c, rows, levels)]
            pltpu.make_async_copy(part, part, piece_recv.at[c, owner]).wait()

        for slot, owner in enumerate((beyond, beyond_next)):
            wait_for(owner)

            @pl.when(inner)
            def _():
                piece_copy(c, owner, near, relay_send, slot).start()

        wait_for(near)

    last_north = jnp.where(has_north, 1, closed_item)
    one_step = functools.partial(transport_row, weather, emission, first, second)
    two_step = functools.partial(transport_row, weather, emission, second, final)

    def items(c):
        ends = c == rows - 1
        north = jnp.where(c == 0, last_north, jnp.where(ends, 0, 3 * c + 1))
        south = jnp.where(c == 0, 0, jnp.where(c == 1, halo_item, 3 * c - 2))
        return north, south, jnp.where(ends, 3 * c + 1, 3 * c + 2)

    def wait_edge(slot, ref):
        pltpu.make_async_copy(ref, ref, edge_recv.at[slot]).wait()

    def turn(c, carry):
        @pl.when(c < rows)
        def _():
            @pl.when(c == 0)
            def _():
                arrive(0)

            @pl.when(jnp.logical_and(c > 0, c < rows - 1))
            def _():
                arrive(c)

            @pl.when(c == rows - 1)
            def _():
                arrive(rows - 1)

            @pl.when(jnp.logical_and(has_north, c == 0))
            def _():
                edge_copy(4).start()

            @pl.when(jnp.logical_and(has_south, c == 1))
            def _():
                wait_edge(4, weather.at[:, halo_item])

            row = lax.rem(c + rows - 1, rows) + 1
            one_step(row, row, *items(c))

            @pl.when(jnp.logical_and(has_north, c == 0))
            def _():
                edge_copy(2).start()

            @pl.when(jnp.logical_and(has_south, c == 1))
            def _():
                edge_copy(3).start()

        @pl.when(c >= 2)
        def _():
            @pl.when(jnp.logical_and(has_south, c == 2))
            def _():
                wait_edge(2, second.at[:, 0])

            @pl.when(jnp.logical_and(has_north, c == rows + 1))
            def _():
                wait_edge(3, second.at[:, rows + 1])

            two_step(c - 1, c - 2, *items(lax.rem(c - 1, rows)))

        return carry

    lax.fori_loop(0, rows + 2, turn, 0)

    for c in range(pieces):
        piece_copy(c, z, near, piece_send, 0).wait_send()
        piece_copy(c, z, far, piece_send, 1).wait_send()

        @pl.when(inner)
        def _():
            piece_copy(c, beyond, near, relay_send, 0).wait_send()
            piece_copy(c, beyond_next, near, relay_send, 1).wait_send()

    for step in range(1, bands):
        control_copy(step).wait_send()

    @pl.when(has_north)
    def _():
        for slot in (0, 2, 4):
            edge_copy(slot).wait_send()

    @pl.when(has_south)
    def _():
        for slot in (1, 3):
            edge_copy(slot).wait_send()


def move_out(final, emission, final_out, emission_out, sems):
    tracers = final.shape[0]
    copies = [pltpu.make_async_copy(emission, emission_out, sems.at[tracers])]
    copies += [pltpu.make_async_copy(final.at[k], final_out.at[k], sems.at[k]) for k in range(tracers)]
    for copy in copies:
        copy.start()
    for copy in copies:
        copy.wait()


def on_device_fused(
    tracer_state,
    control,
    prior_tiles,
    tile_index,
    region_map,
    region_sigma,
    zonal_courant,
    meridional_courant,
    vertical_diffusion,
):
    tracers, rows, levels, lons = tracer_state.shape
    bands = lax.axis_size("band")
    pieces = rows - 1 + last_parts(levels)
    dma = pltpu.SemaphoreType.DMA
    vmem = pl.BlockSpec(memory_space=pltpu.VMEM)
    hbm = pl.BlockSpec(memory_space=pltpu.HBM)
    operands = [
        pltpu.with_memory_space_constraint(operand, pltpu.HBM)
        for operand in (
            tile_index,
            region_sigma,
            region_map,
            prior_tiles,
            tracer_state,
            control,
            zonal_courant,
            meridional_courant,
            vertical_diffusion,
        )
    ]
    results = pl.pallas_call(
        functools.partial(window_kernel, bands),
        out_shape=(pltpu.VMEM(tracer_state.shape, jnp.float32), pltpu.VMEM(control.shape, jnp.float32)),
        in_specs=[hbm] * len(operands),
        out_specs=(vmem, vmem),
        scratch_shapes=[
            pltpu.VMEM((tracers, rows + 2, levels, lons), jnp.float32),
            pltpu.VMEM((tracers, rows + 2, levels, lons), jnp.float32),
            pltpu.VMEM((LINE, 3 * rows + 2, levels, lons // LINE), jnp.float32),
            pltpu.VMEM((tracers, bands * rows, lons), jnp.float32),
            pltpu.VMEM(tile_index.shape, jnp.int32),
            pltpu.VMEM(region_sigma.shape, jnp.float32),
            pltpu.VMEM(region_map.shape, jnp.int32),
            pltpu.VMEM(prior_tiles.shape, jnp.float32),
            dma((4,)),
            dma((rows,)),
            dma((1,)),
            dma((pieces, 2)),
            dma((pieces, LINE)),
            dma((pieces, 2)),
            dma((1,)),
            dma((bands,)),
            dma((bands,)),
            dma((5,)),
            dma((5,)),
        ],
        compiler_params=pltpu.CompilerParams(
            collective_id=0, has_side_effects=True, vmem_limit_bytes=40 * 1024 * 1024
        ),
    )(*operands)
    return pl.pallas_call(
        move_out,
        out_shape=(
            jax.ShapeDtypeStruct(tracer_state.shape, jnp.float32),
            jax.ShapeDtypeStruct(control.shape, jnp.float32),
        ),
        in_specs=[vmem, vmem],
        out_specs=(hbm, hbm),
        scratch_shapes=[dma((tracers + 1,))],
        compiler_params=pltpu.CompilerParams(vmem_limit_bytes=8 * 1024 * 1024),
    )(*[pltpu.with_memory_space_constraint(result, pltpu.VMEM) for result in results])


def solution(mesh):
    in_specs = (
        P(("inv", "tracer"), "band", None, None),
        P(("inv", "tracer"), "band", None),
        P(),
        P(),
        P("band", None),
        P("tracer", None),
        P(("inv", "band"), None, "tracer"),
        P(("inv", "band"), None, "tracer"),
        P(("inv", "band"), None, "tracer"),
    )
    out_specs = (P(("inv", "tracer"), "band", None, None), P(("inv", "tracer"), "band", None))
    body = on_device_fused if fits_fused(mesh) else on_device
    return jax.shard_map(
        body, mesh=mesh, in_specs=in_specs, out_specs=out_specs, check_vma=False
    )
```
